512 devices in a mesh: tm: 32 (over z, x), series: 16 (over y, core).
Axes of the slice: x: 4, y: 8, z: 8, core: 2. Of those that a mesh axis runs over, the one named last changes fastest.
Arguments:
- readings: bfloat16 [512, 16384], P('tm', 'series'), may hold values from -8 to 8
- present: int32 [512, 16384], P('tm', 'series'), may hold values 0 or 1
- loadings: bfloat16 [16384, 128], P('series'), may hold values from -1 to 1
- noise_precision: float32 [16384], P('series'), may hold values from 0.5 to 2
- update_gain: float32 [128], replicated, may hold values from 7.8125e-06 to 0.0078125
- factor_rate: float32 [128], replicated, may hold values from 0.0001 to 0.01
- smooth_rate: float32 [128], replicated, may hold values from 0.0001 to 0.05
- regions: int32 [16384], P('series'), may hold values from 0 to 15
Outputs:
- smoothed: float32 [512, 128], P('tm')
- histogram: float32 [16, 20], replicated
The draws below stay inside these ranges and needn't reach their ends.
All inputs are finite; a program needn't handle non-finite values. No bound on the sum of `present` on one device may be relied on, other than what follows from the above.
Results may differ from the reference program's by a relative error of at most 0.0004.
Values sent between devices are 32-bit elements; how exact they have to be, the bound alone decides.
No kernel may reach another device: no remote copies, remote signals or barrier semaphores. Data moves between devices by JAX's collectives and lax.ppermute only.
A program may use at most 64 MiB of HBM per device.

```python
import math
import jax
import jax.numpy as jnp
from jax import lax

K = 128
BINS = 20
GROUPS = 16
T_SIZE = 512
NS = 16384


def model_draw(key):
    base = jax.random.fold_in(key, 7001)
    rate_key = jax.random.fold_in(base, 1)
    start_key = jax.random.fold_in(base, 2)
    shock_key = jax.random.fold_in(base, 3)
    load_key = jax.random.fold_in(base, 4)
    noise_key = jax.random.fold_in(base, 5)
    one_minus = jnp.exp(jax.random.uniform(rate_key, (K,), jnp.float32, math.log(0.001), math.log(0.1)))
    coef = 1.0 - one_minus
    innov = jnp.sqrt(one_minus * (2.0 - one_minus))
    start = jax.random.normal(start_key, (K,), jnp.float32)
    shocks = jax.random.normal(shock_key, (T_SIZE, K), jnp.float32)

    def advance(level, shock):
        level = coef * level + innov * shock
        return (level, level)
    _, path = lax.scan(advance, start, shocks)
    loadings = jnp.clip(jax.random.normal(load_key, (NS, K), jnp.float32) * (2.0 * K) ** (-0.5), -1.0, 1.0)
    noise = jax.random.normal(noise_key, (T_SIZE, NS), jnp.float32) * 0.7
    common = jnp.dot(path, loadings.T, precision=lax.Precision.HIGHEST)
    readings = jnp.clip(common + noise, -8.0, 8.0)
    return (readings, loadings)


def draw_readings(key, part):
    readings, _ = model_draw(key)
    return readings.astype(jnp.bfloat16)


def draw_loadings(key, part):
    _, loadings = model_draw(key)
    return loadings.astype(jnp.bfloat16)


def with_ends(entries, own_key, smallest, largest):
    shape = entries.shape
    spot = [jax.random.randint(jax.random.fold_in(own_key, axis), (), 0, shape[axis]) for axis in range(len(shape))]
    entries = entries.at[tuple(spot)].set(smallest)
    longest = shape.index(max(shape))
    spot[longest] = (spot[longest] + 1) % shape[longest]
    return entries.at[tuple(spot)].set(largest)


def levels(rng, dims, cuts, smallest, high):
    def one(axis_at, blocks):
        steps = jax.random.uniform(jax.random.fold_in(jax.random.fold_in(rng, 6), axis_at), (blocks,), jnp.float32, smallest / len(cuts), high / len(cuts))
        return jnp.repeat(jnp.exp(steps), dims[axis_at] // blocks).reshape((-1,) + (1,) * (len(dims) - axis_at - 1))

    level = one(*cuts[0])
    for cut in cuts[1:]:
        level = level * one(*cut)
    return level


def setup_inputs(seed: int = 0) -> dict:
    splits = jax.random.split(jax.random.key(seed), 9)
    return {
        "readings": draw_readings(jax.random.fold_in(splits[8], 71), 0),
        "present": with_ends((jax.random.randint(splits[1], (T_SIZE, NS), 0, 5) < 4).astype(jnp.int32), jax.random.fold_in(splits[1], 1), 0, 1),
        "loadings": draw_loadings(jax.random.fold_in(splits[8], 71), 0),
        "noise_precision": jnp.clip(jnp.exp(math.log(2.0) - 1.3862944 * jax.random.uniform(splits[3], (NS,), jnp.float32) ** levels(splits[3], (NS,), ((0, 16),), -0.2, 0.2)), 0.5, 2.0),
        "update_gain": jnp.clip(jnp.exp(jax.random.uniform(splits[4], (K,), jnp.float32, math.log(7.812500371073838e-06), math.log(0.0078125))), 7.812500371073838e-06, 0.0078125),
        "factor_rate": jnp.clip(jnp.exp(jax.random.uniform(splits[5], (K,), jnp.float32, math.log(0.0001), math.log(0.01))), 0.0001, 0.01),
        "smooth_rate": jnp.clip(jnp.exp(jax.random.uniform(splits[6], (K,), jnp.float32, math.log(0.0001), math.log(0.05))), 0.0001, 0.05),
        "regions": with_ends(jax.random.randint(splits[7], (NS,), 0, GROUPS), jax.random.fold_in(splits[7], 1), 0, GROUPS - 1).astype(jnp.int32),
    }


highest = lax.Precision.HIGHEST

def normal_cdf(values):
    return 0.5 * (1.0 + lax.erf(values * 0.7071067811865476))

def reference(readings, present, loadings, noise_precision, update_gain, factor_rate, smooth_rate, regions):
    weight = present.astype(jnp.float32) * noise_precision[None, :]

    def per_hour(hour):
        scaled = (loadings * weight[hour][:, None]).astype(jnp.bfloat16)
        inform = lax.dot_general(scaled, loadings, (((0,), (0,)), ((), ())), preferred_element_type=jnp.float32)
        scores = jnp.dot(readings[hour], scaled, preferred_element_type=jnp.float32)
        return (inform, scores)
    inform, scores = lax.map(per_hour, jnp.arange(T_SIZE))
    decays = jnp.exp(-factor_rate)
    retain = jnp.exp(-smooth_rate)
    identity = jnp.eye(K, dtype=jnp.float32)

    def forward(current, stepped):
        inform_t, scores_t = stepped
        transit = (identity - update_gain[:, None] * inform_t) * decays[None, :]
        current = jnp.dot(transit, current, precision=highest) + update_gain * scores_t
        return (current, current)
    _, filtered = lax.scan(forward, jnp.zeros((K,), jnp.float32), (inform, scores))
    boundary = decays * filtered[-1]

    def backward(following, filter_row):
        smooth_row = (1.0 - retain * decays) * filter_row + retain * following
        return (smooth_row, smooth_row)
    _, smoothed = lax.scan(backward, boundary, filtered, reverse=True)
    fitted = lax.dot_general(smoothed.astype(jnp.bfloat16), loadings, (((1,), (1,)), ((), ())), preferred_element_type=jnp.float32)
    standard = (readings.astype(jnp.float32) - fitted) * jnp.sqrt(noise_precision)[None, :]
    probab = normal_cdf(standard)
    observed = present.astype(jnp.float32)
    member = (regions[:, None] == jnp.arange(GROUPS)[None, :]).astype(jnp.float32)
    binned = []
    for bin_index in range(BINS):
        kernel = jnp.maximum(0.0, 1.0 - BINS * jnp.abs(probab - (bin_index + 0.5) / BINS))
        binned.append(lax.optimization_barrier(jnp.sum(observed * kernel, axis=0)))
    bin_table = jnp.stack(binned)
    tallies = jnp.dot(bin_table, member, precision=highest)
    histogram = tallies.T * (BINS * GROUPS / (T_SIZE * NS))
    return (smoothed, histogram)
```

```python
import jax
import jax.numpy as jnp
from jax import lax
from jax.experimental import pallas as pl
from jax.experimental.pallas import tpu as pltpu
from jax.sharding import Mesh
from jax.sharding import PartitionSpec as P

BINS = 20
GROUPS = 16
SERIES = ("y", "c")
TM = ("z", "x")
F32 = jnp.float32
BF16 = jnp.bfloat16
VM = pl.BlockSpec(memory_space=pltpu.VMEM)
SM = pl.BlockSpec(memory_space=pltpu.SMEM)
PARAMS = pltpu.CompilerParams(vmem_limit_bytes=40 * 1024 * 1024)


def iotas(rows, lanes):
    shape = (rows, lanes)
    return lax.broadcasted_iota(jnp.int32, shape, 0), lax.broadcasted_iota(jnp.int32, shape, 1)


def halves(a):
    high = a.astype(BF16)
    return high, (a - high.astype(F32)).astype(BF16)


def bdot(a, b):
    return jnp.dot(a, b, preferred_element_type=F32)


def dot3(a, b):
    ah, al = halves(a)
    bh, bl = halves(b)
    return bdot(ah, bh) + (bdot(ah, bl) + bdot(al, bh))


def across(a, b):
    return lax.dot_general(a, b, (((1,), (1,)), ((), ())), preferred_element_type=F32)


def joined(earlier, later):
    k = later.shape[1]
    product = dot3(earlier, later[:k])
    return jnp.concatenate([product[:k], product[k:] + later[k:]], axis=0)


def information_kernel(readings, present, loadings, noise, out):
    hours = readings.shape[0]
    load = loadings[...]
    k = load.shape[1]
    half = k // 2
    scaled = (jnp.transpose(load.astype(F32)) * noise[...]).astype(BF16)
    seen = present[...].astype(F32).astype(BF16)
    scores = across(readings[...] * seen, scaled)
    row, lane = iotas(half, k)
    row_k, lane_k = iotas(k, k)
    for h in range(hours):
        inform = bdot(scaled * seen[h : h + 1, :], load)
        folded = pltpu.roll(inform[half:], half, 1)
        out[h, :half] = jnp.where(lane >= row, inform[:half], folded)
        diagonal = jnp.sum(jnp.where(row_k == lane_k, inform, 0.0), axis=0, keepdims=True)
        out[h, half:] = jnp.concatenate(
            [diagonal, scores[h : h + 1], jnp.zeros((6, k), F32)], axis=0
        )


def block_kernel(packed, gain, factor_rate, leaves, pairs, quads, eighths, total):
    hours = packed.shape[0]
    k = packed.shape[2]
    half = k // 2
    gain_row = gain[...]
    decay_col = jnp.transpose(jnp.broadcast_to(jnp.exp(-factor_rate[...]), (k, k)))
    row, lane = iotas(half, k)
    row_k, lane_k = iotas(k, k)
    on_diag = row_k == lane_k
    identity = on_diag.astype(F32)
    maps = []
    for h in range(hours):
        page = packed[h]
        top = page[:half]
        upper = jnp.where(lane >= row, top, 0.0)
        lower = pltpu.roll(jnp.where(lane < row, top, 0.0), half, 1)
        part = jnp.concatenate([upper, lower], axis=0)
        inform = jnp.where(on_diag, page[half : half + 1], part + jnp.transpose(part))
        matrix = (identity - inform * gain_row) * decay_col
        shift = gain_row * page[half + 1 : half + 2]
        one = jnp.concatenate([matrix, shift, jnp.zeros((7, k), F32)], axis=0)
        leaves[h] = one
    for i in range(hours // 2):
        pairs[i] = joined(leaves[2 * i], leaves[2 * i + 1])
    for i in range(hours // 4):
        quads[i] = joined(pairs[2 * i], pairs[2 * i + 1])
    for i in range(hours // 8):
        eighths[i] = joined(quads[2 * i], quads[2 * i + 1])
    total[...] = joined(eighths[0], eighths[1])


def four_kernel(blocks, total):
    total[...] = joined(joined(blocks[0], blocks[1]), joined(blocks[2], blocks[3]))


def applied(current, one):
    k = one.shape[1]
    return dot3(current, one[:k]) + one[k : k + 1]


def filter_kernel(
    place, planes, blocks, leaves, pairs, quads, eighths, factor_rate, smooth_rate, partial, sent, last
):
    k = factor_rate.shape[1]
    z, x, at_end = place[0], place[1], place[2]
    current = jnp.zeros((8, k), F32)
    for i in range(planes.shape[0] - 1):
        current = jnp.where(i < z, applied(current, planes[i]), current)
    for i in range(blocks.shape[0] - 1):
        current = jnp.where(i < x, applied(current, blocks[i]), current)
    after = {-1: current}
    after[7] = applied(current, eighths[0])
    after[3] = applied(current, quads[0])
    after[11] = applied(after[7], quads[2])
    after[15] = applied(after[7], eighths[1])
    for i in range(4):
        after[4 * i + 1] = applied(after[4 * i - 1], pairs[2 * i])
    for i in range(8):
        after[2 * i] = applied(after[2 * i - 1], leaves[2 * i])
    hours = leaves.shape[0]
    decays = jnp.exp(-factor_rate[...])
    rate = smooth_rate[...]
    retain = jnp.exp(-rate)
    own = 1.0 - retain * decays
    following = jnp.zeros((1, k), F32)
    for h in reversed(range(hours)):
        following = own * after[h][:1] + retain * following
        partial[h : h + 1] = following
    boundary = jnp.where(at_end == 1, decays * after[hours - 1][:1], 0.0)
    last[...] = boundary
    sent[...] = following + jnp.exp(-hours * rate) * boundary


def histogram_kernel(
    place, partial, last, later, smooth_rate, readings, present, loadings, noise, regions, scale, smoothed, out
):
    hours, k = partial.shape
    count = later.shape[0]
    own = place[3]
    rate = smooth_rate[...]
    row, _ = iotas(count, k)
    steps = row - own - 1
    weight = jnp.exp(-(jnp.maximum(steps, 0) * hours).astype(F32) * rate)
    trailing = jnp.sum(jnp.where(steps >= 0, weight * later[...], 0.0), axis=0, keepdims=True)
    trailing = trailing + last[...]
    hour, _ = iotas(hours, k)
    powers = jnp.exp(-(hours - hour).astype(F32) * rate)
    smooth = partial[...] + powers * trailing
    smoothed[...] = smooth
    fitted = across(smooth.astype(BF16), loadings[...])
    standard = (readings[...].astype(F32) - fitted) * jnp.sqrt(noise[...])
    probab = 0.5 * (1.0 + lax.erf(standard * 0.7071067811865476))
    seen = present[...].astype(F32)
    rows = []
    for b in range(BINS):
        kernel = jnp.maximum(0.0, 1.0 - BINS * jnp.abs(probab - (b + 0.5) / BINS))
        rows.append(jnp.sum(seen * kernel, axis=0, keepdims=True))
    rows.append(jnp.zeros((4, probab.shape[1]), F32))
    table = jnp.concatenate(rows, axis=0)
    slot, _ = iotas(128, probab.shape[1])
    member = (lax.rem(slot, GROUPS) == regions[...]).astype(F32).astype(BF16)
    high, low = halves(table)
    lowest = (table - high.astype(F32) - low.astype(F32)).astype(BF16)
    wide = across(high, member) + (across(low, member) + across(lowest, member))
    brow, blane = iotas(24, 128)
    kept = jnp.where(lax.div(blane, GROUPS) == lax.rem(brow, 8), wide, 0.0) * scale[0]
    out[...] = jnp.concatenate(
        [jnp.sum(kept[8 * r : 8 * r + 8], axis=0, keepdims=True) for r in range(3)], axis=0
    )


def sent_to_all(shard, axis):
    count = lax.axis_size(axis)
    return lax.all_to_all(
        jnp.broadcast_to(shard[None], (count, *shard.shape)), axis, 0, 0, tiled=True
    )


def shape_of(*sizes):
    return jax.ShapeDtypeStruct(sizes, F32)


def body(
    readings, present, loadings, noise_precision, update_gain, factor_rate, smooth_rate, regions
):
    hours, series = readings.shape
    k = loadings.shape[1]
    noise = noise_precision.reshape(1, series)
    gain, factor, smooth = (a.reshape(1, k) for a in (update_gain, factor_rate, smooth_rate))
    z, x = lax.axis_index("z"), lax.axis_index("x")
    nz, nx = lax.axis_size("z"), lax.axis_size("x")
    own = z * nx + x
    place = jnp.stack([z, x, (own == nz * nx - 1).astype(jnp.int32), own]).astype(jnp.int32)

    packed = pl.pallas_call(
        information_kernel,
        out_shape=shape_of(hours, k // 2 + 8, k),
        in_specs=[VM] * 4,
        out_specs=VM,
        compiler_params=PARAMS,
        name="information",
    )(readings, present, loadings, noise)

    height = k // 2 + 8
    cores, ny = lax.axis_size("c"), lax.axis_size("y")
    packed = packed.reshape(cores, hours // cores, height, k)
    packed = lax.all_to_all(packed, "c", 0, 0, tiled=True).sum(axis=0)
    packed = lax.all_to_all(packed, "y", 0, 0, tiled=True).sum(axis=0)
    packed = sent_to_all(packed, "y")
    packed = lax.all_gather(packed, "c").reshape(hours, height, k)

    tall = k + 8
    leaves, pairs, quads, eighths, total = pl.pallas_call(
        block_kernel,
        out_shape=[
            shape_of(hours, tall, k),
            shape_of(hours // 2, tall, k),
            shape_of(hours // 4, tall, k),
            shape_of(hours // 8, tall, k),
            shape_of(tall, k),
        ],
        in_specs=[VM] * 3,
        out_specs=[VM] * 5,
        compiler_params=PARAMS,
        name="block",
    )(packed, gain, factor)

    blocks = lax.all_gather(total, "x")
    plane = pl.pallas_call(
        four_kernel,
        out_shape=shape_of(tall, k),
        in_specs=[VM],
        out_specs=VM,
        compiler_params=PARAMS,
        name="four",
    )(blocks)
    planes = sent_to_all(plane, "z")

    partial, sent, last = pl.pallas_call(
        filter_kernel,
        out_shape=[shape_of(hours, k), shape_of(1, k), shape_of(1, k)],
        in_specs=[SM] + [VM] * 8,
        out_specs=[VM] * 3,
        compiler_params=PARAMS,
        name="filter",
    )(place, planes, blocks, leaves, pairs, quads, eighths, factor, smooth)

    later = sent_to_all(sent, TM).reshape(nz * nx, k)
    hours_all = hours * nz * nx
    series_all = series * ny * cores
    scale = jnp.full((1,), BINS * GROUPS / (hours_all * series_all), F32)
    smoothed, local = pl.pallas_call(
        histogram_kernel,
        out_shape=[shape_of(hours, k), shape_of(3, 128)],
        in_specs=[SM] + [VM] * 9 + [SM],
        out_specs=[VM] * 2,
        compiler_params=PARAMS,
        name="histogram",
    )(place, partial, last, later, smooth, readings, present, loadings, noise, regions.reshape(1, series), scale)

    local = lax.all_gather(local, "c").sum(axis=0)
    local = sent_to_all(local, ("x", "y")).sum(axis=0)
    local = sent_to_all(local, "z").sum(axis=0)
    histogram = local.reshape(24, GROUPS)[:BINS].T
    return (smoothed, histogram)


def solution(mesh):
    split = Mesh(mesh.devices.reshape(8, 4, 8, 2), ("z", "x", "y", "c"))
    in_specs = (P(TM, SERIES), P(TM, SERIES), P(SERIES, None), P(SERIES), P(), P(), P(), P(SERIES))
    out_specs = (P(TM, None), P())
    return jax.shard_map(body, mesh=split, in_specs=in_specs, out_specs=out_specs, check_vma=False)
```

```python
import jax
import jax.numpy as jnp
from jax import lax
from jax.experimental import pallas as pl
from jax.experimental.pallas import tpu as pltpu
from jax.sharding import Mesh
from jax.sharding import PartitionSpec as P

BINS = 20
GROUPS = 16
SERIES = ("y", "c")
TM = ("z", "x")
F32 = jnp.float32
BF16 = jnp.bfloat16
VM = pl.BlockSpec(memory_space=pltpu.VMEM)
SM = pl.BlockSpec(memory_space=pltpu.SMEM)
HB = pl.BlockSpec(memory_space=pltpu.HBM)
PARAMS = pltpu.CompilerParams(vmem_limit_bytes=40 * 1024 * 1024)


def iotas(rows, lanes):
    shape = (rows, lanes)
    return lax.broadcasted_iota(jnp.int32, shape, 0), lax.broadcasted_iota(jnp.int32, shape, 1)


def halves(a):
    high = a.astype(BF16)
    return high, (a - high.astype(F32)).astype(BF16)


def bdot(a, b):
    return jnp.dot(a, b, preferred_element_type=F32)


def dot3(a, b):
    ah, al = halves(a)
    bh, bl = halves(b)
    return bdot(ah, bh) + (bdot(ah, bl) + bdot(al, bh))


def across(a, b):
    return lax.dot_general(a, b, (((1,), (1,)), ((), ())), preferred_element_type=F32)


def joined(earlier, later, fade):
    k = fade.shape[1]
    wide = jnp.concatenate([later[0][:k], later[1][:k]], axis=1)
    product = dot3(earlier[0], wide)
    maps = jnp.concatenate([product[:k, :k], product[k:, :k] + later[0][k:]], axis=0)
    gives = jnp.concatenate([product[:k, k:], product[k:, k:] + later[1][k:]], axis=0)
    return maps, earlier[1] + fade * gives


def information_kernel(
    place, readings_hbm, present_hbm, loadings_hbm, noise_hbm, kept, sent,
    readings, present, loadings, noise, seen, scores, sems,
):
    pairs = (
        (loadings_hbm, loadings),
        (noise_hbm, noise),
        (present_hbm, present),
        (readings_hbm, readings),
    )
    copies = [pltpu.make_async_copy(a, b, sems.at[i]) for i, (a, b) in enumerate(pairs)]
    for copy in copies:
        copy.start()
    for copy in copies:
        copy.wait()
    count = kept.shape[0]
    core = place[2]
    load = loadings[...]
    k = load.shape[1]
    half = k // 2
    scaled = (jnp.transpose(load.astype(F32)) * noise[...]).astype(BF16)
    seen[...] = present[...].astype(F32)
    scores[...] = across(readings[...] * seen[...].astype(BF16), scaled)
    row, lane = iotas(half, k)
    row_k, lane_k = iotas(k, k)
    for slot, out in enumerate((kept, sent)):
        first = (core if slot == 0 else 1 - core) * count
        for i in range(count):
            observed = seen[pl.ds(first + i, 1), :].astype(BF16)
            inform = bdot(scaled * observed, load)
            folded = pltpu.roll(inform[half:], half, 1)
            out[i, :half] = jnp.where(lane >= row, inform[:half], folded)
            diagonal = jnp.sum(jnp.where(row_k == lane_k, inform, 0.0), axis=0, keepdims=True)
            out[i, half:] = jnp.concatenate(
                [diagonal, scores[pl.ds(first + i, 1), :], jnp.zeros((6, k), F32)], axis=0
            )


def block_kernel(
    place, packed, gain, factor_rate, smooth_rate, leaves, pairs, quads, eighths, half_total,
    given1, given2, given4, given8,
):
    hours = packed.shape[0]
    k = packed.shape[2]
    half = k // 2
    gain_row = gain[...]
    decay_row = jnp.exp(-factor_rate[...])
    decay_col = jnp.transpose(jnp.broadcast_to(decay_row, (k, k)))
    rate = smooth_rate[...]
    weight = 1.0 - jnp.exp(-rate) * decay_row
    row, lane = iotas(half, k)
    row_k, lane_k = iotas(k, k)
    on_diag = row_k == lane_k
    identity = on_diag.astype(F32)
    for h in range(hours):
        page = packed[h]
        top = page[:half]
        upper = jnp.where(lane >= row, top, 0.0)
        lower = pltpu.roll(jnp.where(lane < row, top, 0.0), half, 1)
        part = jnp.concatenate([upper, lower], axis=0)
        inform = jnp.where(on_diag, page[half : half + 1], part + jnp.transpose(part))
        matrix = (identity - inform * gain_row) * decay_col
        shift = gain_row * page[half + 1 : half + 2]
        one = jnp.concatenate([matrix, shift, jnp.zeros((7, k), F32)], axis=0)
        leaves[h] = one
        given1[h] = one * weight
    below, given = leaves, given1
    for span, above, gives in ((1, pairs, given2), (2, quads, given4), (4, eighths, given8)):
        fade = jnp.exp(-span * rate)
        for i in range(hours // (2 * span)):
            above[i], gives[i] = joined(
                (below[2 * i], given[2 * i]), (below[2 * i + 1], given[2 * i + 1]), fade
            )
        below, given = above, gives
    total = joined((below[0], given[0]), (below[1], given[1]), jnp.exp(-8.0 * rate))
    half_total[...] = jnp.where(place[2] == 0, total[0], total[1])


def four_kernel(place, blocks, smooth_rate, half_total):
    rate = smooth_rate[...]
    short, long = jnp.exp(-16.0 * rate), jnp.exp(-32.0 * rate)
    one = joined((blocks[0, 0], blocks[1, 0]), (blocks[0, 1], blocks[1, 1]), short)
    two = joined((blocks[0, 2], blocks[1, 2]), (blocks[0, 3], blocks[1, 3]), short)
    total = joined(one, two, long)
    half_total[...] = jnp.where(place[2] == 0, total[0], total[1])


def applied(current, one):
    k = one.shape[1]
    return dot3(current, one[:k]) + one[k : k + 1]


def walked(nodes, start, own):
    k = nodes.shape[3]
    current = found = start
    gives = []
    for i in range(nodes.shape[1]):
        found = jnp.where(i == own, current, found)
        wide = jnp.concatenate([nodes[0, i, :k], nodes[1, i, :k]], axis=1)
        product = dot3(current, wide)
        gives.append(product[:1, k:] + nodes[1, i, k : k + 1])
        current = product[:, :k] + nodes[0, i, k : k + 1]
    return found, current, gives


def followed(gives, after, own, fade):
    found = following = after
    for i in reversed(range(len(gives))):
        found = jnp.where(i == own, following, found)
        following = gives[i] + fade * following
    return found


def final_kernel(
    place, planes, blocks, leaves, pairs, quads, eighths, factor_rate, smooth_rate,
    readings, present, loadings, noise, regions, scale, smoothed, out,
):
    hours, _, k = leaves.shape
    z, x = place[0], place[1]
    decays = jnp.exp(-factor_rate[...])
    rate = smooth_rate[...]
    retain = jnp.exp(-rate)
    start, final, plane_gives = walked(planes, jnp.zeros((8, k), F32), z)
    span = hours * blocks.shape[1]
    behind_plane = followed(plane_gives, decays * final[:1], z, jnp.exp(-span * rate))
    start, _, block_gives = walked(blocks, start, x)
    following = followed(block_gives, behind_plane, x, jnp.exp(-hours * rate))
    after = {-1: start}
    after[7] = applied(start, eighths[0])
    after[3] = applied(start, quads[0])
    after[11] = applied(after[7], quads[2])
    after[15] = applied(after[7], eighths[1])
    for i in range(4):
        after[4 * i + 1] = applied(after[4 * i - 1], pairs[2 * i])
    for i in range(8):
        after[2 * i] = applied(after[2 * i - 1], leaves[2 * i])
    weight = 1.0 - retain * decays
    for h in reversed(range(hours)):
        following = weight * after[h][:1] + retain * following
        smoothed[h : h + 1] = following
    fitted = across(smoothed[...].astype(BF16), loadings[...])
    standard = (readings[...].astype(F32) - fitted) * jnp.sqrt(noise[...])
    probab = 0.5 * (1.0 + lax.erf(standard * 0.7071067811865476))
    seen = present[...].astype(F32)
    rows = []
    for b in range(BINS):
        kernel = jnp.maximum(0.0, 1.0 - BINS * jnp.abs(probab - (b + 0.5) / BINS))
        rows.append(jnp.sum(seen * kernel, axis=0, keepdims=True))
    rows.append(jnp.zeros((4, probab.shape[1]), F32))
    table = jnp.concatenate(rows, axis=0)
    slot, _ = iotas(128, probab.shape[1])
    member = (lax.rem(slot, GROUPS) == regions[...]).astype(F32).astype(BF16)
    high, low = halves(table)
    lowest = (table - high.astype(F32) - low.astype(F32)).astype(BF16)
    wide = across(high, member) + (across(low, member) + across(lowest, member))
    brow, blane = iotas(24, 128)
    kept = jnp.where(lax.div(blane, GROUPS) == lax.rem(brow, 8), wide, 0.0) * scale[0]
    out[...] = jnp.concatenate(
        [jnp.sum(kept[8 * r : 8 * r + 8], axis=0, keepdims=True) for r in range(3)], axis=0
    )


def sent_to_all(shard, axis):
    count = lax.axis_size(axis)
    return lax.all_to_all(
        jnp.broadcast_to(shard[None], (count, *shard.shape)), axis, 0, 0, tiled=True
    )


def shape_of(*sizes):
    return jax.ShapeDtypeStruct(sizes, F32)


def body(
    readings, present, loadings, noise_precision, update_gain, factor_rate, smooth_rate, regions
):
    hours, series = readings.shape
    k = loadings.shape[1]
    height, tall = k // 2 + 8, k + 8
    noise = noise_precision.reshape(1, series)
    gain, factor, smooth = (a.reshape(1, k) for a in (update_gain, factor_rate, smooth_rate))
    z, x, core = (lax.axis_index(a) for a in ("z", "x", "c"))
    nz, nx, ny, cores = (lax.axis_size(a) for a in ("z", "x", "y", "c"))
    place = jnp.stack([z, x, core]).astype(jnp.int32)
    share = hours // cores

    kept, sent = pl.pallas_call(
        information_kernel,
        out_shape=[shape_of(share, height, k)] * 2,
        in_specs=[SM] + [HB] * 4,
        out_specs=[VM] * 2,
        scratch_shapes=[
            pltpu.VMEM((hours, series), BF16),
            pltpu.VMEM((hours, series), jnp.int32),
            pltpu.VMEM((series, k), BF16),
            pltpu.VMEM((1, series), F32),
            pltpu.VMEM((hours, series), F32),
            pltpu.VMEM((hours, k), F32),
            pltpu.SemaphoreType.DMA((4,)),
        ],
        compiler_params=PARAMS,
        name="information",
    )(place, readings, present, loadings, noise)
    arrived = lax.dynamic_index_in_dim(lax.all_gather(sent, "c"), 1 - core, 0, keepdims=False)
    packed = lax.all_to_all(kept + arrived, "y", 0, 0, tiled=True).sum(axis=0)
    packed = sent_to_all(packed, "y")
    packed = lax.all_gather(packed, "c").reshape(hours, height, k)

    nodes = [shape_of(hours // n, tall, k) for n in (1, 2, 4, 8)]
    leaves, pairs, quads, eighths, half_total = pl.pallas_call(
        block_kernel,
        out_shape=nodes + [shape_of(tall, k)],
        in_specs=[SM] + [VM] * 4,
        out_specs=[VM] * 5,
        scratch_shapes=[pltpu.VMEM((hours // n, tall, k), F32) for n in (1, 2, 4, 8)],
        compiler_params=PARAMS,
        name="block",
    )(place, packed, gain, factor, smooth)
    blocks = lax.all_gather(sent_to_all(half_total, "x"), "c")

    half_total = pl.pallas_call(
        four_kernel,
        out_shape=shape_of(tall, k),
        in_specs=[SM] + [VM] * 2,
        out_specs=VM,
        compiler_params=PARAMS,
        name="four",
    )(place, blocks, smooth)
    planes = lax.all_gather(sent_to_all(half_total, "z"), "c")

    hours_all = hours * nz * nx
    series_all = series * ny * cores
    scale = jnp.full((1,), BINS * GROUPS / (hours_all * series_all), F32)
    smoothed, local = pl.pallas_call(
        final_kernel,
        out_shape=[shape_of(hours, k), shape_of(3, 128)],
        in_specs=[SM] + [VM] * 13 + [SM],
        out_specs=[VM] * 2,
        compiler_params=PARAMS,
        name="final",
    )(
        place, planes, blocks, leaves, pairs, quads, eighths, factor, smooth,
        readings, present, loadings, noise, regions.reshape(1, series), scale,
    )

    local = sent_to_all(local, SERIES).sum(axis=0)
    local = sent_to_all(local, TM).sum(axis=0)
    histogram = local.reshape(24, GROUPS)[:BINS].T
    return (smoothed, histogram)


def solution(mesh):
    split = Mesh(mesh.devices.reshape(8, 4, 8, 2), ("z", "x", "y", "c"))
    in_specs = (P(TM, SERIES), P(TM, SERIES), P(SERIES, None), P(SERIES), P(), P(), P(), P(SERIES))
    out_specs = (P(TM, None), P())
    return jax.shard_map(body, mesh=split, in_specs=in_specs, out_specs=out_specs, check_vma=False)
```

```python
import jax
import jax.numpy as jnp
from jax import lax
from jax.experimental import pallas as pl
from jax.experimental.pallas import tpu as pltpu
from jax.sharding import Mesh
from jax.sharding import PartitionSpec as P

BINS = 20
GROUPS = 16
SERIES = ("y", "c")
TM = ("z", "x")
F32 = jnp.float32
BF16 = jnp.bfloat16
VM = pl.BlockSpec(memory_space=pltpu.VMEM)
SM = pl.BlockSpec(memory_space=pltpu.SMEM)
HB = pl.BlockSpec(memory_space=pltpu.HBM)
PARAMS = pltpu.CompilerParams(vmem_limit_bytes=40 * 1024 * 1024)


def iotas(rows, lanes):
    shape = (rows, lanes)
    return lax.broadcasted_iota(jnp.int32, shape, 0), lax.broadcasted_iota(jnp.int32, shape, 1)


def halves(a):
    high = a.astype(BF16)
    return high, (a - high.astype(F32)).astype(BF16)


def bdot(a, b):
    return jnp.dot(a, b, preferred_element_type=F32)


def dot3(a, b):
    ah, al = halves(a)
    bh, bl = halves(b)
    return bdot(ah, bh) + (bdot(ah, bl) + bdot(al, bh))


def across(a, b):
    return lax.dot_general(a, b, (((1,), (1,)), ((), ())), preferred_element_type=F32)


def joined(earlier, later, fade):
    k = fade.shape[1]
    wide = jnp.concatenate([later[0][:k], later[1][:k]], axis=1)
    product = dot3(earlier[0], wide)
    maps = jnp.concatenate([product[:k, :k], product[k:, :k] + later[0][k:]], axis=0)
    gives = jnp.concatenate([product[:k, k:], product[k:, k:] + later[1][k:]], axis=0)
    return maps, earlier[1] + fade * gives


def information_kernel(
    place, readings_hbm, present_hbm, loadings_hbm, noise_hbm, kept, sent,
    readings, present, loadings, noise, seen, scores, sems,
):
    pairs = (
        (loadings_hbm, loadings),
        (noise_hbm, noise),
        (present_hbm, present),
        (readings_hbm, readings),
    )
    copies = [pltpu.make_async_copy(a, b, sems.at[i]) for i, (a, b) in enumerate(pairs)]
    for copy in copies:
        copy.start()
    for copy in copies:
        copy.wait()
    count = kept.shape[0]
    core = place[2]
    load = loadings[...]
    k = load.shape[1]
    half = k // 2
    scaled = (jnp.transpose(load.astype(F32)) * noise[...]).astype(BF16)
    seen[...] = present[...].astype(F32)
    scores[...] = across(readings[...] * seen[...].astype(BF16), scaled)
    row, lane = iotas(half, k)
    row_k, lane_k = iotas(k, k)
    for slot, out in enumerate((kept, sent)):
        first = (core if slot == 0 else 1 - core) * count
        for i in range(count):
            observed = seen[pl.ds(first + i, 1), :].astype(BF16)
            inform = bdot(scaled * observed, load)
            folded = pltpu.roll(inform[half:], half, 1)
            out[i, :half] = jnp.where(lane >= row, inform[:half], folded)
            diagonal = jnp.sum(jnp.where(row_k == lane_k, inform, 0.0), axis=0, keepdims=True)
            out[i, half:] = jnp.concatenate(
                [diagonal, scores[pl.ds(first + i, 1), :], jnp.zeros((6, k), F32)], axis=0
            )


def block_kernel(
    place, packed, gain, factor_rate, smooth_rate, leaves, pairs, quads, eighths, half_total,
    given1, given2, given4, given8,
):
    hours = packed.shape[0]
    k = packed.shape[2]
    half = k // 2
    gain_row = gain[...]
    decay_row = jnp.exp(-factor_rate[...])
    decay_col = jnp.transpose(jnp.broadcast_to(decay_row, (k, k)))
    rate = smooth_rate[...]
    weight = 1.0 - jnp.exp(-rate) * decay_row
    row, lane = iotas(half, k)
    row_k, lane_k = iotas(k, k)
    on_diag = row_k == lane_k
    identity = on_diag.astype(F32)
    for h in range(hours):
        page = packed[h]
        top = page[:half]
        upper = jnp.where(lane >= row, top, 0.0)
        lower = pltpu.roll(jnp.where(lane < row, top, 0.0), half, 1)
        part = jnp.concatenate([upper, lower], axis=0)
        inform = jnp.where(on_diag, page[half : half + 1], part + jnp.transpose(part))
        matrix = (identity - inform * gain_row) * decay_col
        shift = gain_row * page[half + 1 : half + 2]
        one = jnp.concatenate([matrix, shift, jnp.zeros((7, k), F32)], axis=0)
        leaves[h] = one
        given1[h] = one * weight
    below, given = leaves, given1
    for span, above, gives in ((1, pairs, given2), (2, quads, given4), (4, eighths, given8)):
        fade = jnp.exp(-span * rate)
        for i in range(hours // (2 * span)):
            above[i], gives[i] = joined(
                (below[2 * i], given[2 * i]), (below[2 * i + 1], given[2 * i + 1]), fade
            )
        below, given = above, gives
    total = joined((below[0], given[0]), (below[1], given[1]), jnp.exp(-8.0 * rate))
    half_total[...] = jnp.where(place[2] == 0, total[0], total[1])


def four_kernel(place, blocks, smooth_rate, half_total):
    rate = smooth_rate[...]
    short, long = jnp.exp(-16.0 * rate), jnp.exp(-32.0 * rate)
    one = joined((blocks[0, 0], blocks[1, 0]), (blocks[0, 1], blocks[1, 1]), short)
    two = joined((blocks[0, 2], blocks[1, 2]), (blocks[0, 3], blocks[1, 3]), short)
    total = joined(one, two, long)
    half_total[...] = jnp.where(place[2] == 0, total[0], total[1])


def applied(current, one):
    k = one.shape[1]
    return dot3(current, one[:k]) + one[k : k + 1]


def walked(nodes, start, own):
    k = start.shape[1]
    current = found = start
    gives = []
    for i, (group, at) in enumerate((n, j) for n in nodes for j in range(n.shape[1])):
        found = jnp.where(i == own, current, found)
        wide = jnp.concatenate([group[0, at, :k], group[1, at, :k]], axis=1)
        product = dot3(current, wide)
        gives.append(product[:1, k:] + group[1, at, k : k + 1])
        current = product[:, :k] + group[0, at, k : k + 1]
    return found, current, gives


def followed(gives, after, own, fade):
    found = following = after
    for i in reversed(range(len(gives))):
        found = jnp.where(i == own, following, found)
        following = gives[i] + fade * following
    return found


def final_kernel(
    place, planes_low, planes_high, blocks, leaves, pairs, quads, eighths, factor_rate, smooth_rate,
    readings, present, loadings, noise, regions, scale, smoothed, out,
):
    hours, _, k = leaves.shape
    z, x = place[0], place[1]
    decays = jnp.exp(-factor_rate[...])
    rate = smooth_rate[...]
    retain = jnp.exp(-rate)
    start, final, plane_gives = walked((planes_low, planes_high), jnp.zeros((8, k), F32), z)
    span = hours * blocks.shape[1]
    behind_plane = followed(plane_gives, decays * final[:1], z, jnp.exp(-span * rate))
    start, _, block_gives = walked((blocks,), start, x)
    following = followed(block_gives, behind_plane, x, jnp.exp(-hours * rate))
    after = {-1: start}
    after[7] = applied(start, eighths[0])
    after[3] = applied(start, quads[0])
    after[11] = applied(after[7], quads[2])
    after[15] = applied(after[7], eighths[1])
    for i in range(4):
        after[4 * i + 1] = applied(after[4 * i - 1], pairs[2 * i])
    for i in range(8):
        after[2 * i] = applied(after[2 * i - 1], leaves[2 * i])
    weight = 1.0 - retain * decays
    for h in reversed(range(hours)):
        following = weight * after[h][:1] + retain * following
        smoothed[h : h + 1] = following
    fitted = across(smoothed[...].astype(BF16), loadings[...])
    standard = (readings[...].astype(F32) - fitted) * jnp.sqrt(noise[...])
    probab = 0.5 * (1.0 + lax.erf(standard * 0.7071067811865476))
    seen = present[...].astype(F32)
    rows = []
    for b in range(BINS):
        kernel = jnp.maximum(0.0, 1.0 - BINS * jnp.abs(probab - (b + 0.5) / BINS))
        rows.append(jnp.sum(seen * kernel, axis=0, keepdims=True))
    rows.append(jnp.zeros((4, probab.shape[1]), F32))
    table = jnp.concatenate(rows, axis=0)
    slot, _ = iotas(128, probab.shape[1])
    member = (lax.rem(slot, GROUPS) == regions[...]).astype(F32).astype(BF16)
    high, low = halves(table)
    lowest = (table - high.astype(F32) - low.astype(F32)).astype(BF16)
    wide = across(high, member) + (across(low, member) + across(lowest, member))
    brow, blane = iotas(24, 128)
    kept = jnp.where(lax.div(blane, GROUPS) == lax.rem(brow, 8), wide, 0.0) * scale[0]
    out[...] = jnp.concatenate(
        [jnp.sum(kept[8 * r : 8 * r + 8], axis=0, keepdims=True) for r in range(3)], axis=0
    )


def sent_to_all(shard, axis):
    count = lax.axis_size(axis)
    return lax.all_to_all(
        jnp.broadcast_to(shard[None], (count, *shard.shape)), axis, 0, 0, tiled=True
    )


def shape_of(*sizes):
    return jax.ShapeDtypeStruct(sizes, F32)


def body(
    readings, present, loadings, noise_precision, update_gain, factor_rate, smooth_rate, regions
):
    hours, series = readings.shape
    k = loadings.shape[1]
    height, tall = k // 2 + 8, k + 8
    noise = noise_precision.reshape(1, series)
    gain, factor, smooth = (a.reshape(1, k) for a in (update_gain, factor_rate, smooth_rate))
    z, x, core = (lax.axis_index(a) for a in ("z", "x", "c"))
    nz, nx, ny, cores = (lax.axis_size(a) for a in ("z", "x", "y", "c"))
    place = jnp.stack([z, x, core]).astype(jnp.int32)
    share = hours // cores

    kept, sent = pl.pallas_call(
        information_kernel,
        out_shape=[shape_of(share, height, k)] * 2,
        in_specs=[SM] + [HB] * 4,
        out_specs=[VM] * 2,
        scratch_shapes=[
            pltpu.VMEM((hours, series), BF16),
            pltpu.VMEM((hours, series), jnp.int32),
            pltpu.VMEM((series, k), BF16),
            pltpu.VMEM((1, series), F32),
            pltpu.VMEM((hours, series), F32),
            pltpu.VMEM((hours, k), F32),
            pltpu.SemaphoreType.DMA((4,)),
        ],
        compiler_params=pltpu.CompilerParams(vmem_limit_bytes=60 * 1024 * 1024),
        name="information",
    )(place, readings, present, loadings, noise)
    arrived = lax.dynamic_index_in_dim(lax.all_gather(sent, "c"), 1 - core, 0, keepdims=False)
    packed = lax.all_to_all(kept + arrived, "y", 0, 0, tiled=True).sum(axis=0)
    packed = sent_to_all(packed, "y")
    packed = lax.all_gather(packed, "c").reshape(hours, height, k)

    nodes = [shape_of(hours // n, tall, k) for n in (1, 2, 4, 8)]
    leaves, pairs, quads, eighths, half_total = pl.pallas_call(
        block_kernel,
        out_shape=nodes + [shape_of(tall, k)],
        in_specs=[SM] + [VM] * 4,
        out_specs=[VM] * 5,
        scratch_shapes=[pltpu.VMEM((hours // n, tall, k), F32) for n in (1, 2, 4, 8)],
        compiler_params=PARAMS,
        name="block",
    )(place, packed, gain, factor, smooth)
    blocks = lax.all_gather(sent_to_all(half_total, "x"), "c")

    half_total = pl.pallas_call(
        four_kernel,
        out_shape=shape_of(tall, k),
        in_specs=[SM] + [VM] * 2,
        out_specs=VM,
        compiler_params=PARAMS,
        name="four",
    )(place, blocks, smooth)
    half_planes = sent_to_all(half_total, "z")
    planes = [lax.all_gather(half_planes[at : at + 4], "c") for at in range(0, nz, 4)]

    hours_all = hours * nz * nx
    series_all = series * ny * cores
    scale = jnp.full((1,), BINS * GROUPS / (hours_all * series_all), F32)
    smoothed, local = pl.pallas_call(
        final_kernel,
        out_shape=[shape_of(hours, k), shape_of(3, 128)],
        in_specs=[SM] + [VM] * 14 + [SM],
        out_specs=[VM] * 2,
        compiler_params=PARAMS,
        name="final",
    )(
        place, *planes, blocks, leaves, pairs, quads, eighths, factor, smooth,
        readings, present, loadings, noise, regions.reshape(1, series), scale,
    )

    local = sent_to_all(local, SERIES).sum(axis=0)
    local = sent_to_all(local, TM).sum(axis=0)
    histogram = local.reshape(24, GROUPS)[:BINS].T
    return (smoothed, histogram)


def solution(mesh):
    split = Mesh(mesh.devices.reshape(8, 4, 8, 2), ("z", "x", "y", "c"))
    in_specs = (P(TM, SERIES), P(TM, SERIES), P(SERIES, None), P(SERIES), P(), P(), P(), P(SERIES))
    out_specs = (P(TM, None), P())
    return jax.shard_map(body, mesh=split, in_specs=in_specs, out_specs=out_specs, check_vma=False)
```

```python
import jax
import jax.numpy as jnp
from jax import lax
from jax.experimental import pallas as pl
from jax.experimental.pallas import tpu as pltpu
from jax.sharding import Mesh
from jax.sharding import PartitionSpec as P

BINS = 20
GROUPS = 16
SERIES = ("y", "c")
TM = ("z", "x")
F32 = jnp.float32
BF16 = jnp.bfloat16
VM = pl.BlockSpec(memory_space=pltpu.VMEM)
SM = pl.BlockSpec(memory_space=pltpu.SMEM)
HB = pl.BlockSpec(memory_space=pltpu.HBM)
PARAMS = pltpu.CompilerParams(vmem_limit_bytes=40 * 1024 * 1024)


def iotas(rows, lanes):
    shape = (rows, lanes)
    return lax.broadcasted_iota(jnp.int32, shape, 0), lax.broadcasted_iota(jnp.int32, shape, 1)


def halves(a):
    high = a.astype(BF16)
    return high, (a - high.astype(F32)).astype(BF16)


def bdot(a, b):
    return jnp.dot(a, b, preferred_element_type=F32)


def dot3(a, b):
    rows = a.shape[0]
    ah, al = halves(a)
    bh, bl = halves(b)
    both = bdot(jnp.concatenate([ah, al], axis=0), bh)
    return both[:rows] + (both[rows:] + bdot(ah, bl))


def across(a, b):
    return lax.dot_general(a, b, (((1,), (1,)), ((), ())), preferred_element_type=F32)


def joined(earlier, later, fade):
    k = fade.shape[1]
    wide = jnp.concatenate([later[0][:k], later[1][:k]], axis=1)
    product = dot3(earlier[0], wide)
    maps = jnp.concatenate([product[:k, :k], product[k:, :k] + later[0][k:]], axis=0)
    gives = jnp.concatenate([product[:k, k:], product[k:, k:] + later[1][k:]], axis=0)
    return maps, earlier[1] + fade * gives


def information_kernel(
    readings_hbm, present_hbm, loadings_hbm, noise_hbm, kept, sent,
    readings, present, loadings, noise, seen, scores, sems,
):
    pairs = (
        (loadings_hbm, loadings),
        (noise_hbm, noise),
        (present_hbm, present),
        (readings_hbm, readings),
    )
    copies = [pltpu.make_async_copy(a, b, sems.at[i]) for i, (a, b) in enumerate(pairs)]
    for copy in copies:
        copy.start()
    core = lax.axis_index("c")
    count, _, k = kept.shape
    half = k // 2
    copies[0].wait()
    copies[1].wait()
    load = loadings[...]
    turned = jnp.transpose(load.astype(F32))
    scaled_wide = turned * noise[...]
    scaled = scaled_wide.astype(BF16)
    turned = turned.astype(BF16)
    columns = jnp.concatenate([load, jnp.transpose(scaled.astype(F32)).astype(BF16)], axis=0)
    lines = jnp.concatenate([scaled, turned], axis=1)
    copies[2].wait()
    seen[...] = present[...].astype(F32)
    copies[3].wait()
    scores[...] = across(readings[...] * seen[...].astype(BF16), scaled)
    row, lane = iotas(half, k)
    row_k, lane_k = iotas(k, k)
    for slot, out in enumerate((kept, sent)):
        first = (core if slot == 0 else 1 - core) * count
        for i in range(count):
            observed = seen[pl.ds(first + i, 1), :].astype(BF16)
            inform = 0.5 * bdot(lines * jnp.concatenate([observed, observed], axis=1), columns)
            folded = pltpu.roll(inform[half:], half, 1)
            out[i, :half] = jnp.where(lane >= row, inform[:half], folded)
            diagonal = jnp.sum(jnp.where(row_k == lane_k, inform, 0.0), axis=0, keepdims=True)
            out[i, half:] = jnp.concatenate(
                [diagonal, scores[pl.ds(first + i, 1), :], jnp.zeros((6, k), F32)], axis=0
            )


def block_kernel(
    packed, gain, factor_rate, smooth_rate, leaves, pairs, quads, eighths, half_total,
    given1, given2, given4, given8,
):
    hours = packed.shape[0]
    k = packed.shape[2]
    half = k // 2
    gain_row = gain[...]
    decay_row = jnp.exp(-factor_rate[...])
    decay_col = jnp.transpose(jnp.broadcast_to(decay_row, (k, k)))
    rate = smooth_rate[...]
    weight = 1.0 - jnp.exp(-rate) * decay_row
    row, lane = iotas(half, k)
    row_k, lane_k = iotas(k, k)
    on_diag = row_k == lane_k
    identity = on_diag.astype(F32)
    for h in range(hours):
        page = packed[h]
        top = page[:half]
        upper = jnp.where(lane >= row, top, 0.0)
        lower = pltpu.roll(jnp.where(lane < row, top, 0.0), half, 1)
        part = jnp.concatenate([upper, lower], axis=0)
        inform = jnp.where(on_diag, page[half : half + 1], part + jnp.transpose(part))
        matrix = (identity - inform * gain_row) * decay_col
        shift = gain_row * page[half + 1 : half + 2]
        one = jnp.concatenate([matrix, shift, jnp.zeros((7, k), F32)], axis=0)
        leaves[h] = one
        given1[h] = one * weight
    below, given = leaves, given1
    for span, above, gives in ((1, pairs, given2), (2, quads, given4), (4, eighths, given8)):
        fade = jnp.exp(-span * rate)
        for i in range(hours // (2 * span)):
            above[i], gives[i] = joined(
                (below[2 * i], given[2 * i]), (below[2 * i + 1], given[2 * i + 1]), fade
            )
        below, given = above, gives
    total = joined((below[0], given[0]), (below[1], given[1]), jnp.exp(-8.0 * rate))
    half_total[...] = jnp.where(lax.axis_index("c") == 0, total[0], total[1])


def four_kernel(blocks, smooth_rate, half_total):
    rate = smooth_rate[...]
    short, long = jnp.exp(-16.0 * rate), jnp.exp(-32.0 * rate)
    one = joined((blocks[0, 0], blocks[1, 0]), (blocks[0, 1], blocks[1, 1]), short)
    two = joined((blocks[0, 2], blocks[1, 2]), (blocks[0, 3], blocks[1, 3]), short)
    total = joined(one, two, long)
    half_total[...] = jnp.where(lax.axis_index("c") == 0, total[0], total[1])


def applied(current, one):
    k = one.shape[1]
    return dot3(current, one[:k]) + one[k : k + 1]


def walked(nodes, current, own):
    k = current.shape[1]
    found = current
    gives = []
    for i, (maps, given) in enumerate(nodes):
        found = jnp.where(i == own, current, found)
        if maps.shape[0] < k:
            gives.append(None)
            current = current + maps[:1]
            continue
        product = dot3(current, jnp.concatenate([maps[:k], given[:k]], axis=1))
        gives.append(product[:1, k:] + given[k : k + 1])
        current = product[:, :k] + maps[k : k + 1]
    return found, current, gives


def followed(gives, after, own, fade):
    found = following = after
    for i in reversed(range(len(gives))):
        found = jnp.where(i == own, following, found)
        if gives[i] is not None:
            following = gives[i] + fade * following
    return found


def final_kernel(
    planes, blocks, leaves, pairs, quads, eighths, factor_rate, smooth_rate,
    readings, present, loadings, noise, regions, scale, smoothed, out,
):
    hours, _, k = leaves.shape
    z, x = lax.axis_index("z"), lax.axis_index("x")
    decays = jnp.exp(-factor_rate[...])
    rate = smooth_rate[...]
    retain = jnp.exp(-rate)
    tall = blocks.shape[2]
    plane_nodes = [(planes[0, : tall - k], planes[1, : tall - k])]
    for at in range(tall - k, planes.shape[1], tall):
        plane_nodes.append((planes[0, at : at + tall], planes[1, at : at + tall]))
    start, final, plane_gives = walked(plane_nodes, jnp.zeros((8, k), F32), z)
    span = hours * blocks.shape[1]
    behind_plane = followed(plane_gives, decays * final[:1], z, jnp.exp(-span * rate))
    block_nodes = [(blocks[0, i], blocks[1, i]) for i in range(blocks.shape[1])]
    start, _, block_gives = walked(block_nodes, start, x)
    following = followed(block_gives, behind_plane, x, jnp.exp(-hours * rate))
    after = {-1: start}
    after[7] = applied(start, eighths[0])
    after[3] = applied(start, quads[0])
    after[11] = applied(after[7], quads[2])
    after[15] = applied(after[7], eighths[1])
    for i in range(4):
        after[4 * i + 1] = applied(after[4 * i - 1], pairs[2 * i])
    for i in range(8):
        after[2 * i] = applied(after[2 * i - 1], leaves[2 * i])
    weight = 1.0 - retain * decays
    for h in reversed(range(hours)):
        following = weight * after[h][:1] + retain * following
        smoothed[h : h + 1] = following
    fitted = across(smoothed[...].astype(BF16), loadings[...])
    standard = (readings[...].astype(F32) - fitted) * jnp.sqrt(noise[...])
    probab = 0.5 * (1.0 + lax.erf(standard * 0.7071067811865476))
    seen = present[...].astype(F32)
    rows = []
    for b in range(BINS):
        kernel = jnp.maximum(0.0, 1.0 - BINS * jnp.abs(probab - (b + 0.5) / BINS))
        rows.append(jnp.sum(seen * kernel, axis=0, keepdims=True))
    rows.append(jnp.zeros((4, probab.shape[1]), F32))
    table = jnp.concatenate(rows, axis=0)
    slot, _ = iotas(128, probab.shape[1])
    member = (lax.rem(slot, GROUPS) == regions[...]).astype(F32).astype(BF16)
    high, low = halves(table)
    lowest = (table - high.astype(F32) - low.astype(F32)).astype(BF16)
    wide = across(high, member) + (across(low, member) + across(lowest, member))
    brow, blane = iotas(24, 128)
    kept = jnp.where(lax.div(blane, GROUPS) == lax.rem(brow, 8), wide, 0.0) * scale[0]
    out[...] = jnp.concatenate(
        [jnp.sum(kept[8 * r : 8 * r + 8], axis=0, keepdims=True) for r in range(3)], axis=0
    )


def tail_kernel(parts, out):
    total = jnp.sum(parts[...], axis=0)
    slots = 128 // GROUPS
    group, lane = iotas(GROUPS, 128)
    slot, column = iotas(128, 128)
    found = jnp.zeros((GROUPS, 128), F32)
    for r in range(3):
        spread = jnp.where(lax.rem(lane, GROUPS) == group, total[r : r + 1], 0.0)
        chosen = (lax.div(slot, GROUPS) + slots * r == column).astype(F32).astype(BF16)
        high, low = halves(spread)
        lowest = (spread - high.astype(F32) - low.astype(F32)).astype(BF16)
        found = found + (bdot(high, chosen) + (bdot(low, chosen) + bdot(lowest, chosen)))
    out[...] = found[:, :BINS]


def sent_to_all(shard, axis):
    count = lax.axis_size(axis)
    return lax.all_to_all(
        jnp.broadcast_to(shard[None], (count, *shard.shape)), axis, 0, 0, tiled=True
    )


def shape_of(*sizes):
    return jax.ShapeDtypeStruct(sizes, F32)


def body(
    readings, present, loadings, noise_precision, update_gain, factor_rate, smooth_rate, regions
):
    hours, series = readings.shape
    k = loadings.shape[1]
    height, tall = k // 2 + 8, k + 8
    noise = noise_precision.reshape(1, series)
    gain, factor, smooth = (a.reshape(1, k) for a in (update_gain, factor_rate, smooth_rate))
    core = lax.axis_index("c")
    nz, nx, ny, cores = (lax.axis_size(a) for a in ("z", "x", "y", "c"))
    share = hours // cores

    kept, sent = pl.pallas_call(
        information_kernel,
        out_shape=[shape_of(share, height, k)] * 2,
        in_specs=[HB] * 4,
        out_specs=[VM] * 2,
        scratch_shapes=[
            pltpu.VMEM((hours, series), BF16),
            pltpu.VMEM((hours, series), jnp.int32),
            pltpu.VMEM((series, k), BF16),
            pltpu.VMEM((1, series), F32),
            pltpu.VMEM((hours, series), F32),
            pltpu.VMEM((hours, k), F32),
            pltpu.SemaphoreType.DMA((4,)),
        ],
        compiler_params=PARAMS,
        name="information",
    )(*(pltpu.with_memory_space_constraint(a, pltpu.HBM) for a in (readings, present, loadings, noise)))
    arrived = lax.dynamic_index_in_dim(lax.all_gather(sent, "c"), 1 - core, 0, keepdims=False)
    packed = lax.all_to_all(kept + arrived, "y", 0, 0, tiled=True).sum(axis=0)
    packed = sent_to_all(packed, "y")
    packed = lax.all_gather(packed, "c").reshape(hours, height, k)

    nodes = [shape_of(hours // n, tall, k) for n in (1, 2, 4, 8)]
    leaves, pairs, quads, eighths, half_total = pl.pallas_call(
        block_kernel,
        out_shape=nodes + [shape_of(tall, k)],
        in_specs=[VM] * 4,
        out_specs=[VM] * 5,
        scratch_shapes=[pltpu.VMEM((hours // n, tall, k), F32) for n in (1, 2, 4, 8)],
        compiler_params=PARAMS,
        name="block",
    )(packed, gain, factor, smooth)
    blocks = lax.all_gather(sent_to_all(half_total, "x"), "c")

    half_total = pl.pallas_call(
        four_kernel,
        out_shape=shape_of(tall, k),
        in_specs=[VM] * 2,
        out_specs=VM,
        compiler_params=PARAMS,
        name="four",
    )(blocks, smooth)
    half_planes = sent_to_all(half_total, "z").reshape(nz * tall, k)
    planes = lax.all_gather(half_planes[k:], "c")

    hours_all = hours * nz * nx
    series_all = series * ny * cores
    scale = jnp.full((1,), BINS * GROUPS / (hours_all * series_all), F32)
    smoothed, local = pl.pallas_call(
        final_kernel,
        out_shape=[shape_of(hours, k), shape_of(3, 128)],
        in_specs=[VM] * 13 + [SM],
        out_specs=[VM] * 2,
        compiler_params=PARAMS,
        name="final",
    )(
        planes, blocks, leaves, pairs, quads, eighths, factor, smooth,
        readings, present, loadings, noise, regions.reshape(1, series), scale,
    )

    local = sent_to_all(local, SERIES).sum(axis=0)
    histogram = pl.pallas_call(
        tail_kernel,
        out_shape=shape_of(GROUPS, BINS),
        in_specs=[VM],
        out_specs=VM,
        compiler_params=PARAMS,
        name="tail",
    )(sent_to_all(local, TM))
    return (smoothed, histogram)


def solution(mesh):
    split = Mesh(mesh.devices.reshape(8, 4, 8, 2), ("z", "x", "y", "c"))
    in_specs = (P(TM, SERIES), P(TM, SERIES), P(SERIES, None), P(SERIES), P(), P(), P(), P(SERIES))
    out_specs = (P(TM, None), P())
    return jax.shard_map(body, mesh=split, in_specs=in_specs, out_specs=out_specs, check_vma=False)
```

```python
import jax
import jax.numpy as jnp
from jax import lax
from jax.experimental import pallas as pl
from jax.experimental.pallas import tpu as pltpu
from jax.sharding import Mesh
from jax.sharding import PartitionSpec as P

BINS = 20
GROUPS = 16
SERIES = ("y", "c")
NEAR = ("zl", "x")
TM = ("zh", *NEAR)
F32 = jnp.float32
BF16 = jnp.bfloat16
VM = pl.BlockSpec(memory_space=pltpu.VMEM)
SM = pl.BlockSpec(memory_space=pltpu.SMEM)
HB = pl.BlockSpec(memory_space=pltpu.HBM)
PARAMS = pltpu.CompilerParams(vmem_limit_bytes=40 * 1024 * 1024)


def iotas(rows, lanes):
    shape = (rows, lanes)
    return lax.broadcasted_iota(jnp.int32, shape, 0), lax.broadcasted_iota(jnp.int32, shape, 1)


def halves(a):
    high = a.astype(BF16)
    return high, (a - high.astype(F32)).astype(BF16)


def bdot(a, b):
    return jnp.dot(a, b, preferred_element_type=F32)


def dot3(a, b):
    rows = a.shape[0]
    ah, al = halves(a)
    bh, bl = halves(b)
    both = bdot(jnp.concatenate([ah, al], axis=0), bh)
    return both[:rows] + (both[rows:] + bdot(ah, bl))


def across(a, b):
    return lax.dot_general(a, b, (((1,), (1,)), ((), ())), preferred_element_type=F32)


def joined(earlier, later, fade):
    k = fade.shape[1]
    wide = jnp.concatenate([later[0][:k], later[1][:k]], axis=1)
    product = dot3(earlier[0], wide)
    maps = jnp.concatenate([product[:k, :k], product[k:, :k] + later[0][k:]], axis=0)
    gives = jnp.concatenate([product[:k, k:], product[k:, k:] + later[1][k:]], axis=0)
    return maps, earlier[1] + fade * gives


def information_kernel(
    readings_hbm, present_hbm, loadings_hbm, noise_hbm, kept, sent,
    readings, present, loadings, noise, seen, scores, sems,
):
    pairs = (
        (loadings_hbm, loadings),
        (noise_hbm, noise),
        (present_hbm, present),
        (readings_hbm, readings),
    )
    copies = [pltpu.make_async_copy(a, b, sems.at[i]) for i, (a, b) in enumerate(pairs)]
    for copy in copies:
        copy.start()
    core = lax.axis_index("c")
    count, _, k = kept.shape
    half = k // 2
    copies[0].wait()
    copies[1].wait()
    load = loadings[...]
    scaled = (jnp.transpose(load.astype(F32)) * noise[...]).astype(BF16)
    copies[2].wait()
    seen[...] = present[...].astype(F32)
    copies[3].wait()
    scores[...] = across(readings[...] * seen[...].astype(BF16), scaled)
    row, lane = iotas(half, k)
    row_k, lane_k = iotas(k, k)
    for slot, out in enumerate((kept, sent)):
        first = (core if slot == 0 else 1 - core) * count
        for i in range(count):
            observed = seen[pl.ds(first + i, 1), :].astype(BF16)
            inform = bdot(scaled * observed, load)
            folded = pltpu.roll(inform[half:], half, 1)
            out[i, :half] = jnp.where(lane >= row, inform[:half], folded)
            diagonal = jnp.sum(jnp.where(row_k == lane_k, inform, 0.0), axis=0, keepdims=True)
            out[i, half:] = jnp.concatenate(
                [diagonal, scores[pl.ds(first + i, 1), :], jnp.zeros((6, k), F32)], axis=0
            )


def block_kernel(
    packed, gain, factor_rate, smooth_rate, leaves, pairs, quads, eighths, half_total,
    given1, given2, given4, given8,
):
    hours = packed.shape[0]
    k = packed.shape[2]
    half = k // 2
    gain_row = gain[...]
    decay_row = jnp.exp(-factor_rate[...])
    decay_col = jnp.transpose(jnp.broadcast_to(decay_row, (k, k)))
    rate = smooth_rate[...]
    weight = 1.0 - jnp.exp(-rate) * decay_row
    row, lane = iotas(half, k)
    row_k, lane_k = iotas(k, k)
    on_diag = row_k == lane_k
    identity = on_diag.astype(F32)
    for h in range(hours):
        page = packed[h]
        top = page[:half]
        upper = jnp.where(lane >= row, top, 0.0)
        lower = pltpu.roll(jnp.where(lane < row, top, 0.0), half, 1)
        part = jnp.concatenate([upper, lower], axis=0)
        inform = jnp.where(on_diag, page[half : half + 1], part + jnp.transpose(part))
        matrix = (identity - inform * gain_row) * decay_col
        shift = gain_row * page[half + 1 : half + 2]
        one = jnp.concatenate([matrix, shift, jnp.zeros((7, k), F32)], axis=0)
        leaves[h] = one
        given1[h] = one * weight
    below, given = leaves, given1
    for span, above, gives in ((1, pairs, given2), (2, quads, given4), (4, eighths, given8)):
        fade = jnp.exp(-span * rate)
        for i in range(hours // (2 * span)):
            above[i], gives[i] = joined(
                (below[2 * i], given[2 * i]), (below[2 * i + 1], given[2 * i + 1]), fade
            )
        below, given = above, gives
    total = joined((below[0], given[0]), (below[1], given[1]), jnp.exp(-8.0 * rate))
    half_total[...] = jnp.where(lax.axis_index("c") == 0, total[0], total[1])


def near_kernel(low, high, smooth_rate, half_total):
    rate = smooth_rate[...]
    nodes = [(part[0, i], part[1, i]) for part in (low, high) for i in range(part.shape[1])]
    hours = 16.0
    while len(nodes) > 1:
        fade = jnp.exp(-hours * rate)
        nodes = [joined(nodes[i], nodes[i + 1], fade) for i in range(0, len(nodes), 2)]
        hours = 2.0 * hours
    half_total[...] = jnp.where(lax.axis_index("c") == 0, nodes[0][0], nodes[0][1])


def applied(current, one):
    k = one.shape[1]
    return dot3(current, one[:k]) + one[k : k + 1]


def walked(nodes, current, own):
    k = current.shape[1]
    found = current
    gives = []
    for i, (maps, given) in enumerate(nodes):
        found = jnp.where(i == own, current, found)
        product = dot3(current, jnp.concatenate([maps[:k], given[:k]], axis=1))
        gives.append(product[:1, k:] + given[k : k + 1])
        current = product[:, :k] + maps[k : k + 1]
    return found, current, gives


def followed(gives, after, own, fade):
    found = following = after
    for i in reversed(range(len(gives))):
        found = jnp.where(i == own, following, found)
        following = gives[i] + fade * following
    return found


def final_kernel(
    planes, low, high, leaves, pairs, quads, eighths, factor_rate, smooth_rate,
    readings, present, loadings, noise, regions, scale, smoothed, out,
):
    hours, _, k = leaves.shape
    far, near = lax.axis_index("zh"), lax.axis_index(NEAR)
    decays = jnp.exp(-factor_rate[...])
    rate = smooth_rate[...]
    retain = jnp.exp(-rate)
    plane_nodes = [(planes[0, i], planes[1, i]) for i in range(planes.shape[1])]
    block_nodes = [(part[0, i], part[1, i]) for part in (low, high) for i in range(part.shape[1])]
    start, final, plane_gives = walked(plane_nodes, jnp.zeros((8, k), F32), far)
    span = hours * len(block_nodes)
    behind_plane = followed(plane_gives, decays * final[:1], far, jnp.exp(-span * rate))
    start, _, block_gives = walked(block_nodes, start, near)
    following = followed(block_gives, behind_plane, near, jnp.exp(-hours * rate))
    after = {-1: start}
    after[7] = applied(start, eighths[0])
    after[3] = applied(start, quads[0])
    after[11] = applied(after[7], quads[2])
    after[15] = applied(after[7], eighths[1])
    for i in range(4):
        after[4 * i + 1] = applied(after[4 * i - 1], pairs[2 * i])
    for i in range(8):
        after[2 * i] = applied(after[2 * i - 1], leaves[2 * i])
    weight = 1.0 - retain * decays
    for h in reversed(range(hours)):
        following = weight * after[h][:1] + retain * following
        smoothed[h : h + 1] = following
    fitted = across(smoothed[...].astype(BF16), loadings[...])
    standard = (readings[...].astype(F32) - fitted) * jnp.sqrt(noise[...])
    probab = 0.5 * (1.0 + lax.erf(standard * 0.7071067811865476))
    seen = present[...].astype(F32)
    rows = []
    for b in range(BINS):
        kernel = jnp.maximum(0.0, 1.0 - BINS * jnp.abs(probab - (b + 0.5) / BINS))
        rows.append(jnp.sum(seen * kernel, axis=0, keepdims=True))
    rows.append(jnp.zeros((4, probab.shape[1]), F32))
    table = jnp.concatenate(rows, axis=0)
    slot, _ = iotas(128, probab.shape[1])
    member = (lax.rem(slot, GROUPS) == regions[...]).astype(F32).astype(BF16)
    wide = across(jnp.concatenate(halves(table), axis=0), member)
    wide = wide[:24] + wide[24:]
    brow, blane = iotas(24, 128)
    kept = jnp.where(lax.div(blane, GROUPS) == lax.rem(brow, 8), wide, 0.0) * scale[0]
    out[...] = jnp.concatenate(
        [jnp.sum(kept[8 * r : 8 * r + 8], axis=0, keepdims=True) for r in range(3)], axis=0
    )


def tail_kernel(parts, out):
    total = jnp.sum(parts[...], axis=0)
    group, lane = iotas(GROUPS, 128)
    slot, column = iotas(128, 128)
    spread = jnp.concatenate(
        [jnp.where(lax.rem(lane, GROUPS) == group, total[r : r + 1], 0.0) for r in range(3)], axis=1
    )
    first = lax.div(slot, GROUPS)
    chosen = jnp.concatenate([(first + 8 * r == column).astype(F32) for r in range(3)], axis=0)
    found = bdot(jnp.concatenate(halves(spread), axis=0), chosen.astype(BF16))
    out[...] = (found[:GROUPS] + found[GROUPS:])[:, :BINS]


def sent_to_all(shard, axis):
    count = lax.axis_size(axis)
    return lax.all_to_all(
        jnp.broadcast_to(shard[None], (count, *shard.shape)), axis, 0, 0, tiled=True
    )


def shape_of(*sizes):
    return jax.ShapeDtypeStruct(sizes, F32)


def body(
    readings, present, loadings, noise_precision, update_gain, factor_rate, smooth_rate, regions
):
    hours, series = readings.shape
    k = loadings.shape[1]
    height, tall = k // 2 + 8, k + 8
    noise = noise_precision.reshape(1, series)
    gain, factor, smooth = (a.reshape(1, k) for a in (update_gain, factor_rate, smooth_rate))
    core = lax.axis_index("c")
    blocks, ny, cores = (lax.axis_size(a) for a in (TM, "y", "c"))
    share = hours // cores

    kept, sent = pl.pallas_call(
        information_kernel,
        out_shape=[shape_of(share, height, k)] * 2,
        in_specs=[HB] * 4,
        out_specs=[VM] * 2,
        scratch_shapes=[
            pltpu.VMEM((hours, series), BF16),
            pltpu.VMEM((hours, series), jnp.int32),
            pltpu.VMEM((series, k), BF16),
            pltpu.VMEM((1, series), F32),
            pltpu.VMEM((hours, series), F32),
            pltpu.VMEM((hours, k), F32),
            pltpu.SemaphoreType.DMA((4,)),
        ],
        compiler_params=PARAMS,
        name="information",
    )(*(pltpu.with_memory_space_constraint(a, pltpu.HBM) for a in (readings, present, loadings, noise)))
    arrived = lax.dynamic_index_in_dim(lax.all_gather(sent, "c"), 1 - core, 0, keepdims=False)
    packed = lax.all_to_all(kept + arrived, "y", 0, 0, tiled=True).sum(axis=0)
    packed = sent_to_all(packed, "y")
    packed = lax.all_gather(packed, "c").reshape(hours, height, k)

    nodes = [shape_of(hours // n, tall, k) for n in (1, 2, 4, 8)]
    leaves, pairs, quads, eighths, half_total = pl.pallas_call(
        block_kernel,
        out_shape=nodes + [shape_of(tall, k)],
        in_specs=[VM] * 4,
        out_specs=[VM] * 5,
        scratch_shapes=[pltpu.VMEM((hours // n, tall, k), F32) for n in (1, 2, 4, 8)],
        compiler_params=PARAMS,
        name="block",
    )(packed, gain, factor, smooth)
    parts = sent_to_all(half_total, NEAR)
    middle = parts.shape[0] // 2
    parts = [lax.all_gather(part, "c") for part in (parts[:middle], parts[middle:])]

    half_total = pl.pallas_call(
        near_kernel,
        out_shape=shape_of(tall, k),
        in_specs=[VM] * 3,
        out_specs=VM,
        compiler_params=PARAMS,
        name="near",
    )(*parts, smooth)
    planes = lax.all_gather(sent_to_all(half_total, "zh"), "c")

    hours_all = hours * blocks
    series_all = series * ny * cores
    scale = jnp.full((1,), BINS * GROUPS / (hours_all * series_all), F32)
    smoothed, local = pl.pallas_call(
        final_kernel,
        out_shape=[shape_of(hours, k), shape_of(3, 128)],
        in_specs=[VM] * 14 + [SM],
        out_specs=[VM] * 2,
        compiler_params=PARAMS,
        name="final",
    )(
        planes, *parts, leaves, pairs, quads, eighths, factor, smooth,
        readings, present, loadings, noise, regions.reshape(1, series), scale,
    )

    local = sent_to_all(local, SERIES).sum(axis=0)
    histogram = pl.pallas_call(
        tail_kernel,
        out_shape=shape_of(GROUPS, BINS),
        in_specs=[VM],
        out_specs=VM,
        compiler_params=PARAMS,
        name="tail",
    )(sent_to_all(local, TM))
    return (smoothed, histogram)


def solution(mesh):
    split = Mesh(mesh.devices.reshape(4, 2, 4, 8, 2), (*TM, *SERIES))
    in_specs = (P(TM, SERIES), P(TM, SERIES), P(SERIES, None), P(SERIES), P(), P(), P(), P(SERIES))
    out_specs = (P(TM, None), P())
    return jax.shard_map(body, mesh=split, in_specs=in_specs, out_specs=out_specs, check_vma=False)
```

```python
import jax
import jax.numpy as jnp
from jax import lax
from jax.experimental import pallas as pl
from jax.experimental.pallas import tpu as pltpu
from jax.sharding import Mesh
from jax.sharding import PartitionSpec as P

BINS = 20
GROUPS = 16
SERIES = ("y", "c")
NEAR = ("zl", "x")
TM = ("zh", *NEAR)
F32 = jnp.float32
BF16 = jnp.bfloat16
VM = pl.BlockSpec(memory_space=pltpu.VMEM)
SM = pl.BlockSpec(memory_space=pltpu.SMEM)
HB = pl.BlockSpec(memory_space=pltpu.HBM)
PARAMS = pltpu.CompilerParams(vmem_limit_bytes=40 * 1024 * 1024)


def iotas(rows, lanes):
    shape = (rows, lanes)
    return lax.broadcasted_iota(jnp.int32, shape, 0), lax.broadcasted_iota(jnp.int32, shape, 1)


def halves(a):
    high = a.astype(BF16)
    return high, (a - high.astype(F32)).astype(BF16)


def bdot(a, b):
    return jnp.dot(a, b, preferred_element_type=F32)


def dot3(a, b):
    rows = a.shape[0]
    ah, al = halves(a)
    bh, bl = halves(b)
    both = bdot(jnp.concatenate([ah, al], axis=0), bh)
    return both[:rows] + (both[rows:] + bdot(ah, bl))


def across(a, b):
    return lax.dot_general(a, b, (((1,), (1,)), ((), ())), preferred_element_type=F32)


def joined(earlier, later, fade):
    k = fade.shape[1]
    wide = jnp.concatenate([later[0][:k], later[1][:k]], axis=1)
    product = dot3(earlier[0], wide)
    maps = jnp.concatenate([product[:k, :k], product[k:, :k] + later[0][k:]], axis=0)
    gives = jnp.concatenate([product[:k, k:], product[k:, k:] + later[1][k:]], axis=0)
    return maps, earlier[1] + fade * gives


def information_kernel(
    readings_hbm, present_hbm, loadings_hbm, noise_hbm, kept, sent,
    readings, present, loadings, noise, seen, scores, sems,
):
    pairs = (
        (loadings_hbm, loadings),
        (noise_hbm, noise),
        (present_hbm, present),
        (readings_hbm, readings),
    )
    copies = [pltpu.make_async_copy(a, b, sems.at[i]) for i, (a, b) in enumerate(pairs)]
    for copy in copies:
        copy.start()
    core = lax.axis_index("c")
    count, _, k = kept.shape
    half = k // 2
    copies[0].wait()
    copies[1].wait()
    load = loadings[...]
    scaled = (jnp.transpose(load.astype(F32)) * noise[...]).astype(BF16)
    copies[2].wait()
    seen[...] = present[...].astype(F32)
    copies[3].wait()
    scores[...] = across(readings[...] * seen[...].astype(BF16), scaled)
    row, lane = iotas(half, k)
    row_k, lane_k = iotas(k, k)
    for slot, out in enumerate((kept, sent)):
        first = (core if slot == 0 else 1 - core) * count
        for i in range(count):
            observed = seen[pl.ds(first + i, 1), :].astype(BF16)
            inform = bdot(scaled * observed, load)
            folded = pltpu.roll(inform[half:], half, 1)
            out[i, :half] = jnp.where(lane >= row, inform[:half], folded)
            diagonal = jnp.sum(jnp.where(row_k == lane_k, inform, 0.0), axis=0, keepdims=True)
            out[i, half:] = jnp.concatenate(
                [diagonal, scores[pl.ds(first + i, 1), :], jnp.zeros((6, k), F32)], axis=0
            )


def block_kernel(
    packed, gain, factor_rate, smooth_rate, leaves, pairs, quads, eighths, sent,
    given1, given2, given4, given8,
):
    hours = packed.shape[0]
    k = packed.shape[2]
    half = k // 2
    gain_row = gain[...]
    decay_row = jnp.exp(-factor_rate[...])
    decay_col = jnp.transpose(jnp.broadcast_to(decay_row, (k, k)))
    rate = smooth_rate[...]
    weight = 1.0 - jnp.exp(-rate) * decay_row
    row, lane = iotas(half, k)
    row_k, lane_k = iotas(k, k)
    on_diag = row_k == lane_k
    identity = on_diag.astype(F32)
    for h in range(hours):
        page = packed[h]
        top = page[:half]
        upper = jnp.where(lane >= row, top, 0.0)
        lower = pltpu.roll(jnp.where(lane < row, top, 0.0), half, 1)
        part = jnp.concatenate([upper, lower], axis=0)
        inform = jnp.where(on_diag, page[half : half + 1], part + jnp.transpose(part))
        matrix = (identity - inform * gain_row) * decay_col
        shift = gain_row * page[half + 1 : half + 2]
        one = jnp.concatenate([matrix, shift, jnp.zeros((7, k), F32)], axis=0)
        leaves[h] = one
        given1[h] = one * weight
    below, given = leaves, given1
    for span, above, gives in ((1, pairs, given2), (2, quads, given4), (4, eighths, given8)):
        fade = jnp.exp(-span * rate)
        for i in range(hours // (2 * span)):
            above[i], gives[i] = joined(
                (below[2 * i], given[2 * i]), (below[2 * i + 1], given[2 * i + 1]), fade
            )
        below, given = above, gives
    total = joined((below[0], given[0]), (below[1], given[1]), jnp.exp(-8.0 * rate))
    rows = jnp.concatenate([total[0][k : k + 1], total[1][k : k + 1], jnp.zeros((6, k), F32)], axis=0)
    first = lax.axis_index("c") == 0
    sent[:k] = jnp.where(first, total[0][:k], total[1][:k])
    sent[k : k + 8] = rows
    sent[k + 8 :] = jnp.where(first, total[1][k - 8 : k], total[0][k - 8 : k])


def block_node(parts, sides, i):
    k = parts.shape[2]
    first = lax.axis_index("c") == 0
    own, other, rows = parts[i, k - 8 : k], parts[i, k + 8 :], parts[i, k : k + 8]
    none = jnp.zeros((7, k), F32)
    maps = [sides[0, i], jnp.where(first, own, other), rows[:1], none]
    given = [sides[1, i], jnp.where(first, other, own), rows[1:2], none]
    return jnp.concatenate(maps, axis=0), jnp.concatenate(given, axis=0)


def near_kernel(parts, sides, smooth_rate, twos, fours, half_total):
    rate = smooth_rate[...]
    nodes = [block_node(parts, sides, i) for i in range(parts.shape[0])]
    hours = 16.0
    for kept in (twos, fours, None):
        fade = jnp.exp(-hours * rate)
        nodes = [joined(nodes[i], nodes[i + 1], fade) for i in range(0, len(nodes), 2)]
        if kept is not None:
            for i, node in enumerate(nodes):
                kept[0, i], kept[1, i] = node
        hours = 2.0 * hours
    half_total[...] = jnp.where(lax.axis_index("c") == 0, nodes[0][0], nodes[0][1])


def applied(current, one):
    k = one.shape[1]
    return dot3(current, one[:k]) + one[k : k + 1]


def stepped(current, node):
    maps, given = node
    k = current.shape[1]
    product = dot3(current, jnp.concatenate([maps[:k], given[:k]], axis=1))
    return product[:, :k] + maps[k : k + 1], product[:1, k:] + given[k : k + 1]


def walked(nodes, current, own):
    found = current
    gives = []
    for i, node in enumerate(nodes):
        found = jnp.where(i == own, current, found)
        current, give = stepped(current, node)
        gives.append(give)
    return found, current, gives


def followed(gives, after, own, fade):
    found = following = after
    for i in reversed(range(len(gives))):
        found = jnp.where(i == own, following, found)
        following = gives[i] + fade * following
    return found


def narrowed(current, following, left, right, goes_right, fade):
    middle = applied(current, left)
    _, give = stepped(middle, right)
    before = jnp.where(goes_right, middle, current)
    return before, jnp.where(goes_right, following, give + fade * following)


def final_kernel(
    planes, fours, twos, parts, sides, leaves, pairs, quads, eighths, factor_rate, smooth_rate,
    readings, present, loadings, noise, regions, scale, smoothed, out,
):
    hours, _, k = leaves.shape
    far, near = lax.axis_index("zh"), lax.axis_index(NEAR)
    decays = jnp.exp(-factor_rate[...])
    rate = smooth_rate[...]
    retain = jnp.exp(-rate)
    plane_nodes = [(planes[0, i], planes[1, i]) for i in range(planes.shape[1])]
    start, final, plane_gives = walked(plane_nodes, jnp.zeros((8, k), F32), far)
    count = parts.shape[0]
    following = followed(
        plane_gives, decays * final[:1], far, jnp.exp(-float(count * hours) * rate)
    )
    for part, size in ((fours, 4), (twos, 2), (None, 1)):
        slot = lax.div(near, size)
        first = slot - lax.rem(slot, 2)
        if part is None:
            left, right = (block_node(parts, sides, first + i) for i in (0, 1))
        else:
            left, right = ((part[0, first + i], part[1, first + i]) for i in (0, 1))
        start, following = narrowed(
            start, following, left[0], right, first < slot, jnp.exp(-float(size * hours) * rate)
        )
    after = {-1: start}
    after[7] = applied(start, eighths[0])
    after[3] = applied(start, quads[0])
    after[11] = applied(after[7], quads[2])
    after[15] = applied(after[7], eighths[1])
    for i in range(4):
        after[4 * i + 1] = applied(after[4 * i - 1], pairs[2 * i])
    for i in range(8):
        after[2 * i] = applied(after[2 * i - 1], leaves[2 * i])
    weight = 1.0 - retain * decays
    for h in reversed(range(hours)):
        following = weight * after[h][:1] + retain * following
        smoothed[h : h + 1] = following
    fitted = across(smoothed[...].astype(BF16), loadings[...])
    standard = (readings[...].astype(F32) - fitted) * jnp.sqrt(noise[...])
    probab = 0.5 * (1.0 + lax.erf(standard * 0.7071067811865476))
    seen = present[...].astype(F32)
    rows = []
    for b in range(BINS):
        kernel = jnp.maximum(0.0, 1.0 - BINS * jnp.abs(probab - (b + 0.5) / BINS))
        rows.append(jnp.sum(seen * kernel, axis=0, keepdims=True))
    rows.append(jnp.zeros((4, probab.shape[1]), F32))
    table = jnp.concatenate(rows, axis=0)
    slot, _ = iotas(128, probab.shape[1])
    member = (lax.rem(slot, GROUPS) == regions[...]).astype(F32).astype(BF16)
    wide = across(jnp.concatenate(halves(table), axis=0), member)
    wide = wide[:24] + wide[24:]
    brow, blane = iotas(24, 128)
    kept = jnp.where(lax.div(blane, GROUPS) == lax.rem(brow, 8), wide, 0.0) * scale[0]
    out[...] = jnp.concatenate(
        [jnp.sum(kept[8 * r : 8 * r + 8], axis=0, keepdims=True) for r in range(3)], axis=0
    )


def tail_kernel(parts, out):
    total = jnp.sum(parts[...], axis=0)
    group, lane = iotas(GROUPS, 128)
    slot, column = iotas(128, 128)
    spread = jnp.concatenate(
        [jnp.where(lax.rem(lane, GROUPS) == group, total[r : r + 1], 0.0) for r in range(3)], axis=1
    )
    first = lax.div(slot, GROUPS)
    chosen = jnp.concatenate([(first + 8 * r == column).astype(F32) for r in range(3)], axis=0)
    found = bdot(jnp.concatenate(halves(spread), axis=0), chosen.astype(BF16))
    out[...] = (found[:GROUPS] + found[GROUPS:])[:, :BINS]


def sent_to_all(shard, axis):
    count = lax.axis_size(axis)
    return lax.all_to_all(
        jnp.broadcast_to(shard[None], (count, *shard.shape)), axis, 0, 0, tiled=True
    )


def shape_of(*sizes):
    return jax.ShapeDtypeStruct(sizes, F32)


def body(
    readings, present, loadings, noise_precision, update_gain, factor_rate, smooth_rate, regions
):
    hours, series = readings.shape
    k = loadings.shape[1]
    height, tall = k // 2 + 8, k + 8
    noise = noise_precision.reshape(1, series)
    gain, factor, smooth = (a.reshape(1, k) for a in (update_gain, factor_rate, smooth_rate))
    core = lax.axis_index("c")
    blocks, ny, cores = (lax.axis_size(a) for a in (TM, "y", "c"))
    share = hours // cores

    kept, sent = pl.pallas_call(
        information_kernel,
        out_shape=[shape_of(share, height, k)] * 2,
        in_specs=[HB] * 4,
        out_specs=[VM] * 2,
        scratch_shapes=[
            pltpu.VMEM((hours, series), BF16),
            pltpu.VMEM((hours, series), jnp.int32),
            pltpu.VMEM((series, k), BF16),
            pltpu.VMEM((1, series), F32),
            pltpu.VMEM((hours, series), F32),
            pltpu.VMEM((hours, k), F32),
            pltpu.SemaphoreType.DMA((4,)),
        ],
        compiler_params=PARAMS,
        name="information",
    )(*(pltpu.with_memory_space_constraint(a, pltpu.HBM) for a in (readings, present, loadings, noise)))
    arrived = lax.dynamic_index_in_dim(lax.all_gather(sent, "c"), 1 - core, 0, keepdims=False)
    packed = lax.all_to_all(kept + arrived, "y", 0, 0, tiled=True).sum(axis=0)
    packed = sent_to_all(packed, "y")
    packed = lax.all_gather(packed, "c").reshape(hours, height, k)

    nodes = [shape_of(hours // n, tall, k) for n in (1, 2, 4, 8)]
    leaves, pairs, quads, eighths, sent = pl.pallas_call(
        block_kernel,
        out_shape=nodes + [shape_of(tall + 8, k)],
        in_specs=[VM] * 4,
        out_specs=[VM] * 5,
        scratch_shapes=[pltpu.VMEM((hours // n, tall, k), F32) for n in (1, 2, 4, 8)],
        compiler_params=PARAMS,
        name="block",
    )(packed, gain, factor, smooth)
    parts = sent_to_all(sent, NEAR)
    count = parts.shape[0]
    sides = lax.all_gather(parts[:, : k - 8], "c")

    twos, fours, half_total = pl.pallas_call(
        near_kernel,
        out_shape=[
            shape_of(2, count // 2, tall, k),
            shape_of(2, count // 4, tall, k),
            shape_of(tall, k),
        ],
        in_specs=[VM] * 3,
        out_specs=[VM] * 3,
        compiler_params=PARAMS,
        name="near",
    )(parts, sides, smooth)
    planes = lax.all_gather(sent_to_all(half_total, "zh"), "c")

    hours_all = hours * blocks
    series_all = series * ny * cores
    scale = jnp.full((1,), BINS * GROUPS / (hours_all * series_all), F32)
    smoothed, local = pl.pallas_call(
        final_kernel,
        out_shape=[shape_of(hours, k), shape_of(3, 128)],
        in_specs=[VM] * 16 + [SM],
        out_specs=[VM] * 2,
        compiler_params=PARAMS,
        name="final",
    )(
        planes, fours, twos, parts, sides, leaves, pairs, quads, eighths, factor, smooth,
        readings, present, loadings, noise, regions.reshape(1, series), scale,
    )

    local = sent_to_all(local, SERIES).sum(axis=0)
    histogram = pl.pallas_call(
        tail_kernel,
        out_shape=shape_of(GROUPS, BINS),
        in_specs=[VM],
        out_specs=VM,
        compiler_params=PARAMS,
        name="tail",
    )(sent_to_all(local, TM))
    return (smoothed, histogram)


def solution(mesh):
    split = Mesh(mesh.devices.reshape(4, 2, 4, 8, 2), (*TM, *SERIES))
    in_specs = (P(TM, SERIES), P(TM, SERIES), P(SERIES, None), P(SERIES), P(), P(), P(), P(SERIES))
    out_specs = (P(TM, None), P())
    return jax.shard_map(body, mesh=split, in_specs=in_specs, out_specs=out_specs, check_vma=False)
```

```python
import jax
import jax.numpy as jnp
from jax import lax
from jax.experimental import pallas as pl
from jax.experimental.pallas import tpu as pltpu
from jax.sharding import Mesh
from jax.sharding import PartitionSpec as P

BINS = 20
GROUPS = 16
SERIES = ("y", "c")
NEAR = ("zl", "x")
TM = ("zh", *NEAR)
F32 = jnp.float32
BF16 = jnp.bfloat16
VM = pl.BlockSpec(memory_space=pltpu.VMEM)
SM = pl.BlockSpec(memory_space=pltpu.SMEM)
HB = pl.BlockSpec(memory_space=pltpu.HBM)
PARAMS = pltpu.CompilerParams(vmem_limit_bytes=40 * 1024 * 1024)


def iotas(rows, lanes):
    shape = (rows, lanes)
    return lax.broadcasted_iota(jnp.int32, shape, 0), lax.broadcasted_iota(jnp.int32, shape, 1)


def halves(a):
    high = a.astype(BF16)
    return high, (a - high.astype(F32)).astype(BF16)


def bdot(a, b):
    return jnp.dot(a, b, preferred_element_type=F32)


def dot3(a, b):
    rows = a.shape[0]
    ah, al = halves(a)
    bh, bl = halves(b)
    both = bdot(jnp.concatenate([ah, al], axis=0), bh)
    return both[:rows] + (both[rows:] + bdot(ah, bl))


def across(a, b):
    return lax.dot_general(a, b, (((1,), (1,)), ((), ())), preferred_element_type=F32)


def joined(earlier, later, fade):
    k = fade.shape[1]
    wide = jnp.concatenate([later[0][:k], later[1][:k]], axis=1)
    product = dot3(earlier[0], wide)
    maps = jnp.concatenate([product[:k, :k], product[k:, :k] + later[0][k:]], axis=0)
    gives = jnp.concatenate([product[:k, k:], product[k:, k:] + later[1][k:]], axis=0)
    return maps, earlier[1] + fade * gives


def information_kernel(
    readings_hbm, present_hbm, loadings_hbm, noise_hbm, kept, sent,
    readings, present, loadings, noise, seen, scores, sems,
):
    pairs = (
        (loadings_hbm, loadings),
        (noise_hbm, noise),
        (present_hbm, present),
        (readings_hbm, readings),
    )
    copies = [pltpu.make_async_copy(a, b, sems.at[i]) for i, (a, b) in enumerate(pairs)]
    for copy in copies:
        copy.start()
    core = lax.axis_index("c")
    count, _, k = kept.shape
    half = k // 2
    copies[0].wait()
    copies[1].wait()
    load = loadings[...]
    scaled = (jnp.transpose(load.astype(F32)) * noise[...]).astype(BF16)
    copies[2].wait()
    seen[...] = present[...].astype(F32)
    copies[3].wait()
    scores[...] = across(readings[...] * seen[...].astype(BF16), scaled)
    row, lane = iotas(half, k)
    row_k, lane_k = iotas(k, k)
    for slot, out in enumerate((kept, sent)):
        first = (core if slot == 0 else 1 - core) * count
        for i in range(count):
            observed = seen[pl.ds(first + i, 1), :].astype(BF16)
            inform = bdot(scaled * observed, load)
            folded = pltpu.roll(inform[half:], half, 1)
            out[i, :half] = jnp.where(lane >= row, inform[:half], folded)
            diagonal = jnp.sum(jnp.where(row_k == lane_k, inform, 0.0), axis=0, keepdims=True)
            out[i, half : half + 2] = jnp.concatenate(
                [diagonal, scores[pl.ds(first + i, 1), :]], axis=0
            )


def block_kernel(
    packed, gain, factor_rate, smooth_rate, leaves, pairs, quads, eighths, sent,
    given1, given2, given4, given8,
):
    hours = packed.shape[0]
    k = packed.shape[2]
    half = k // 2
    gain_row = gain[...]
    decay_row = jnp.exp(-factor_rate[...])
    decay_col = jnp.transpose(jnp.broadcast_to(decay_row, (k, k)))
    rate = smooth_rate[...]
    weight = 1.0 - jnp.exp(-rate) * decay_row
    row, lane = iotas(half, k)
    row_k, lane_k = iotas(k, k)
    on_diag = row_k == lane_k
    identity = on_diag.astype(F32)
    for h in range(hours):
        page = packed[h]
        top = page[:half]
        upper = jnp.where(lane >= row, top, 0.0)
        lower = pltpu.roll(jnp.where(lane < row, top, 0.0), half, 1)
        part = jnp.concatenate([upper, lower], axis=0)
        inform = jnp.where(on_diag, page[half : half + 1], part + jnp.transpose(part))
        matrix = (identity - inform * gain_row) * decay_col
        shift = gain_row * page[half + 1 : half + 2]
        one = jnp.concatenate([matrix, shift, jnp.zeros((7, k), F32)], axis=0)
        leaves[h] = one
        given1[h] = one * weight
    below, given = leaves, given1
    for span, above, gives in ((1, pairs, given2), (2, quads, given4), (4, eighths, given8)):
        fade = jnp.exp(-span * rate)
        for i in range(hours // (2 * span)):
            above[i], gives[i] = joined(
                (below[2 * i], given[2 * i]), (below[2 * i + 1], given[2 * i + 1]), fade
            )
        below, given = above, gives
    total = joined((below[0], given[0]), (below[1], given[1]), jnp.exp(-8.0 * rate))
    first = lax.axis_index("c") == 0
    sent[:k] = jnp.where(first, total[0][:k], total[1][:k])
    sent[k : k + 8] = jnp.where(first, total[1][k - 8 : k], total[0][k - 8 : k])
    sent[k + 8 :] = jnp.concatenate([total[0][k : k + 1], total[1][k : k + 1]], axis=0)


def block_node(parts, sides, i):
    k = parts.shape[2]
    first = lax.axis_index("c") == 0
    own, other, rows = parts[i, k - 8 : k], parts[i, k : k + 8], parts[i, k + 8 :]
    none = jnp.zeros((7, k), F32)
    maps = [sides[0, i], jnp.where(first, own, other), rows[:1], none]
    given = [sides[1, i], jnp.where(first, other, own), rows[1:2], none]
    return jnp.concatenate(maps, axis=0), jnp.concatenate(given, axis=0)


def near_kernel(parts, sides, smooth_rate, twos, fours, half_total):
    rate = smooth_rate[...]
    nodes = [block_node(parts, sides, i) for i in range(parts.shape[0])]
    hours = 16.0
    for kept in (twos, fours, None):
        fade = jnp.exp(-hours * rate)
        nodes = [joined(nodes[i], nodes[i + 1], fade) for i in range(0, len(nodes), 2)]
        if kept is not None:
            for i, node in enumerate(nodes):
                kept[0, i], kept[1, i] = node
        hours = 2.0 * hours
    half_total[...] = jnp.where(lax.axis_index("c") == 0, *nodes[0])[: half_total.shape[0]]


def applied(current, one):
    k = one.shape[1]
    return dot3(current, one[:k]) + one[k : k + 1]


def stepped(current, node):
    maps, given = node
    k = current.shape[1]
    product = dot3(current, jnp.concatenate([maps[:k], given[:k]], axis=1))
    return product[:, :k] + maps[k : k + 1], product[:1, k:] + given[k : k + 1]


def walked(nodes, current, own):
    found = current
    gives = []
    for i, node in enumerate(nodes):
        found = jnp.where(i == own, current, found)
        current, give = stepped(current, node)
        gives.append(give)
    return found, current, gives


def followed(gives, after, own, fade):
    found = following = after
    for i in reversed(range(len(gives))):
        found = jnp.where(i == own, following, found)
        following = gives[i] + fade * following
    return found


def narrowed(current, following, left, right, goes_right, fade):
    middle = applied(current, left)
    _, give = stepped(middle, right)
    before = jnp.where(goes_right, middle, current)
    return before, jnp.where(goes_right, following, give + fade * following)


def final_kernel(
    planes, fours, twos, parts, sides, leaves, pairs, quads, eighths, factor_rate, smooth_rate,
    readings, present, loadings, noise, regions, scale, smoothed, out,
):
    hours, _, k = leaves.shape
    far, near = lax.axis_index("zh"), lax.axis_index(NEAR)
    decays = jnp.exp(-factor_rate[...])
    rate = smooth_rate[...]
    retain = jnp.exp(-rate)
    plane_nodes = [(planes[0, i], planes[1, i]) for i in range(planes.shape[1])]
    start, final, plane_gives = walked(plane_nodes, jnp.zeros((8, k), F32), far)
    count = parts.shape[0]
    following = followed(
        plane_gives, decays * final[:1], far, jnp.exp(-float(count * hours) * rate)
    )
    for part, size in ((fours, 4), (twos, 2), (None, 1)):
        slot = lax.div(near, size)
        first = slot - lax.rem(slot, 2)
        if part is None:
            left, right = (block_node(parts, sides, first + i) for i in (0, 1))
        else:
            left, right = ((part[0, first + i], part[1, first + i]) for i in (0, 1))
        start, following = narrowed(
            start, following, left[0], right, first < slot, jnp.exp(-float(size * hours) * rate)
        )
    after = {-1: start}
    after[7] = applied(start, eighths[0])
    after[3] = applied(start, quads[0])
    after[11] = applied(after[7], quads[2])
    after[15] = applied(after[7], eighths[1])
    for i in range(4):
        after[4 * i + 1] = applied(after[4 * i - 1], pairs[2 * i])
    for i in range(8):
        after[2 * i] = applied(after[2 * i - 1], leaves[2 * i])
    weight = 1.0 - retain * decays
    for h in reversed(range(hours)):
        following = weight * after[h][:1] + retain * following
        smoothed[h : h + 1] = following
    fitted = across(smoothed[...].astype(BF16), loadings[...])
    standard = (readings[...].astype(F32) - fitted) * jnp.sqrt(noise[...])
    probab = 0.5 * (1.0 + lax.erf(standard * 0.7071067811865476))
    seen = present[...].astype(F32)
    rows = []
    for b in range(BINS):
        kernel = jnp.maximum(0.0, 1.0 - BINS * jnp.abs(probab - (b + 0.5) / BINS))
        rows.append(jnp.sum(seen * kernel, axis=0, keepdims=True))
    rows.append(jnp.zeros((4, probab.shape[1]), F32))
    table = jnp.concatenate(rows, axis=0)
    slot, _ = iotas(128, probab.shape[1])
    member = (lax.rem(slot, GROUPS) == regions[...]).astype(F32).astype(BF16)
    wide = across(jnp.concatenate(halves(table), axis=0), member)
    wide = wide[:24] + wide[24:]
    brow, blane = iotas(24, 128)
    kept = jnp.where(lax.div(blane, GROUPS) == lax.rem(brow, 8), wide, 0.0) * scale[0]
    out[...] = jnp.concatenate(
        [jnp.sum(kept[8 * r : 8 * r + 8], axis=0, keepdims=True) for r in range(3)], axis=0
    )


def tail_kernel(parts, out):
    total = jnp.sum(parts[...], axis=0)
    group, lane = iotas(GROUPS, 128)
    slot, column = iotas(128, 128)
    spread = jnp.concatenate(
        [jnp.where(lax.rem(lane, GROUPS) == group, total[r : r + 1], 0.0) for r in range(3)], axis=1
    )
    first = lax.div(slot, GROUPS)
    chosen = jnp.concatenate([(first + 8 * r == column).astype(F32) for r in range(3)], axis=0)
    found = bdot(jnp.concatenate(halves(spread), axis=0), chosen.astype(BF16))
    out[...] = (found[:GROUPS] + found[GROUPS:])[:, :BINS]


def sent_to_all(shard, axis):
    count = lax.axis_size(axis)
    return lax.all_to_all(
        jnp.broadcast_to(shard[None], (count, *shard.shape)), axis, 0, 0, tiled=True
    )


def shape_of(*sizes):
    return jax.ShapeDtypeStruct(sizes, F32)


def body(
    readings, present, loadings, noise_precision, update_gain, factor_rate, smooth_rate, regions
):
    hours, series = readings.shape
    k = loadings.shape[1]
    height, tall = k // 2 + 2, k + 8
    padded = -(-height // 8) * 8
    noise = noise_precision.reshape(1, series)
    gain, factor, smooth = (a.reshape(1, k) for a in (update_gain, factor_rate, smooth_rate))
    core = lax.axis_index("c")
    blocks, ny, cores = (lax.axis_size(a) for a in (TM, "y", "c"))
    share = hours // cores

    kept, sent = pl.pallas_call(
        information_kernel,
        out_shape=[shape_of(share, height, k), shape_of(share, padded, k)],
        in_specs=[HB] * 4,
        out_specs=[VM] * 2,
        scratch_shapes=[
            pltpu.VMEM((hours, series), BF16),
            pltpu.VMEM((hours, series), jnp.int32),
            pltpu.VMEM((series, k), BF16),
            pltpu.VMEM((1, series), F32),
            pltpu.VMEM((hours, series), F32),
            pltpu.VMEM((hours, k), F32),
            pltpu.SemaphoreType.DMA((4,)),
        ],
        compiler_params=PARAMS,
        name="information",
    )(*(pltpu.with_memory_space_constraint(a, pltpu.HBM) for a in (readings, present, loadings, noise)))
    arrived = lax.dynamic_index_in_dim(lax.all_gather(sent, "c"), 1 - core, 0, keepdims=False)
    packed = lax.all_to_all(kept + arrived[:, :height], "y", 0, 0, tiled=True).sum(axis=0)
    packed = jnp.pad(sent_to_all(packed, "y"), ((0, 0), (0, padded - height), (0, 0)))
    packed = lax.all_gather(packed, "c").reshape(hours, padded, k)

    nodes = [shape_of(hours // n, tall, k) for n in (1, 2, 4, 8)]
    leaves, pairs, quads, eighths, sent = pl.pallas_call(
        block_kernel,
        out_shape=nodes + [shape_of(k + 10, k)],
        in_specs=[VM] * 4,
        out_specs=[VM] * 5,
        scratch_shapes=[pltpu.VMEM((hours // n, tall, k), F32) for n in (1, 2, 4, 8)],
        compiler_params=PARAMS,
        name="block",
    )(packed, gain, factor, smooth)
    parts = sent_to_all(sent, NEAR)
    count = parts.shape[0]
    sides = lax.all_gather(parts[:, : k - 8], "c")

    twos, fours, half_total = pl.pallas_call(
        near_kernel,
        out_shape=[
            shape_of(2, count // 2, tall, k),
            shape_of(2, count // 4, tall, k),
            shape_of(k + 1, k),
        ],
        in_specs=[VM] * 3,
        out_specs=[VM] * 3,
        compiler_params=PARAMS,
        name="near",
    )(parts, sides, smooth)
    planes = lax.all_gather(sent_to_all(half_total, "zh"), "c")

    hours_all = hours * blocks
    series_all = series * ny * cores
    scale = jnp.full((1,), BINS * GROUPS / (hours_all * series_all), F32)
    smoothed, local = pl.pallas_call(
        final_kernel,
        out_shape=[shape_of(hours, k), shape_of(3, 128)],
        in_specs=[VM] * 16 + [SM],
        out_specs=[VM] * 2,
        compiler_params=PARAMS,
        name="final",
    )(
        planes, fours, twos, parts, sides, leaves, pairs, quads, eighths, factor, smooth,
        readings, present, loadings, noise, regions.reshape(1, series), scale,
    )

    local = sent_to_all(local, SERIES).sum(axis=0)
    histogram = pl.pallas_call(
        tail_kernel,
        out_shape=shape_of(GROUPS, BINS),
        in_specs=[VM],
        out_specs=VM,
        compiler_params=PARAMS,
        name="tail",
    )(sent_to_all(local, TM))
    return (smoothed, histogram)


def solution(mesh):
    split = Mesh(mesh.devices.reshape(4, 2, 4, 8, 2), (*TM, *SERIES))
    in_specs = (P(TM, SERIES), P(TM, SERIES), P(SERIES, None), P(SERIES), P(), P(), P(), P(SERIES))
    out_specs = (P(TM, None), P())
    return jax.shard_map(body, mesh=split, in_specs=in_specs, out_specs=out_specs, check_vma=False)
```

```python
import jax
import jax.numpy as jnp
from jax import lax
from jax.experimental import pallas as pl
from jax.experimental.pallas import tpu as pltpu
from jax.sharding import Mesh
from jax.sharding import PartitionSpec as P

BINS = 20
GROUPS = 16
SERIES = ("y", "c")
NEAR = ("zl", "x")
TM = ("za", "zb", *NEAR)
F32 = jnp.float32
BF16 = jnp.bfloat16
VM = pl.BlockSpec(memory_space=pltpu.VMEM)
SM = pl.BlockSpec(memory_space=pltpu.SMEM)
HB = pl.BlockSpec(memory_space=pltpu.HBM)
PARAMS = pltpu.CompilerParams(vmem_limit_bytes=40 * 1024 * 1024)


def iotas(rows, lanes):
    shape = (rows, lanes)
    return lax.broadcasted_iota(jnp.int32, shape, 0), lax.broadcasted_iota(jnp.int32, shape, 1)


def halves(a):
    high = a.astype(BF16)
    return high, (a - high.astype(F32)).astype(BF16)


def bdot(a, b):
    return jnp.dot(a, b, preferred_element_type=F32)


def dot3(a, b):
    rows = a.shape[0]
    ah, al = halves(a)
    bh, bl = halves(b)
    both = bdot(jnp.concatenate([ah, al], axis=0), bh)
    return both[:rows] + (both[rows:] + bdot(ah, bl))


def across(a, b):
    return lax.dot_general(a, b, (((1,), (1,)), ((), ())), preferred_element_type=F32)


def joined(earlier, later, fade):
    k = fade.shape[1]
    wide = jnp.concatenate([later[0][:k], later[1][:k]], axis=1)
    product = dot3(earlier[0], wide)
    maps = jnp.concatenate([product[:k, :k], product[k:, :k] + later[0][k:]], axis=0)
    gives = jnp.concatenate([product[:k, k:], product[k:, k:] + later[1][k:]], axis=0)
    return maps, earlier[1] + fade * gives


def information_kernel(
    readings_hbm, present_hbm, loadings_hbm, noise_hbm, kept, sent,
    readings, present, loadings, noise, seen, scores, sems,
):
    pairs = (
        (loadings_hbm, loadings),
        (noise_hbm, noise),
        (present_hbm, present),
        (readings_hbm, readings),
    )
    copies = [pltpu.make_async_copy(a, b, sems.at[i]) for i, (a, b) in enumerate(pairs)]
    for copy in copies:
        copy.start()
    core = lax.axis_index("c")
    count, _, k = kept.shape
    half = k // 2
    copies[0].wait()
    copies[1].wait()
    load = loadings[...]
    scaled = (jnp.transpose(load.astype(F32)) * noise[...]).astype(BF16)
    copies[2].wait()
    seen[...] = present[...].astype(F32)
    copies[3].wait()
    scores[...] = across(readings[...] * seen[...].astype(BF16), scaled)
    row, lane = iotas(half, k)
    row_k, lane_k = iotas(k, k)
    for slot, out in enumerate((kept, sent)):
        first = (core if slot == 0 else 1 - core) * count
        for i in range(count):
            observed = seen[pl.ds(first + i, 1), :].astype(BF16)
            inform = bdot(scaled * observed, load)
            folded = pltpu.roll(inform[half:], half, 1)
            out[i, :half] = jnp.where(lane >= row, inform[:half], folded)
            diagonal = jnp.sum(jnp.where(row_k == lane_k, inform, 0.0), axis=0, keepdims=True)
            out[i, half : half + 2] = jnp.concatenate(
                [diagonal, scores[pl.ds(first + i, 1), :]], axis=0
            )


def block_kernel(
    packed, gain, factor_rate, smooth_rate, leaves, pairs, quads, eighths, sent,
    given1, given2, given4, given8,
):
    hours = packed.shape[0]
    k = packed.shape[2]
    half = k // 2
    gain_row = gain[...]
    decay_row = jnp.exp(-factor_rate[...])
    decay_col = jnp.transpose(jnp.broadcast_to(decay_row, (k, k)))
    rate = smooth_rate[...]
    weight = 1.0 - jnp.exp(-rate) * decay_row
    row, lane = iotas(half, k)
    row_k, lane_k = iotas(k, k)
    on_diag = row_k == lane_k
    identity = on_diag.astype(F32)
    for h in range(hours):
        page = packed[h]
        top = page[:half]
        upper = jnp.where(lane >= row, top, 0.0)
        lower = pltpu.roll(jnp.where(lane < row, top, 0.0), half, 1)
        part = jnp.concatenate([upper, lower], axis=0)
        inform = jnp.where(on_diag, page[half : half + 1], part + jnp.transpose(part))
        matrix = (identity - inform * gain_row) * decay_col
        shift = gain_row * page[half + 1 : half + 2]
        one = jnp.concatenate([matrix, shift, jnp.zeros((7, k), F32)], axis=0)
        leaves[h] = one
        given1[h] = one * weight
    below, given = leaves, given1
    for span, above, gives in ((1, pairs, given2), (2, quads, given4), (4, eighths, given8)):
        fade = jnp.exp(-span * rate)
        for i in range(hours // (2 * span)):
            above[i], gives[i] = joined(
                (below[2 * i], given[2 * i]), (below[2 * i + 1], given[2 * i + 1]), fade
            )
        below, given = above, gives
    total = joined((below[0], given[0]), (below[1], given[1]), jnp.exp(-8.0 * rate))
    first = lax.axis_index("c") == 0
    sent[:k] = jnp.where(first, total[0][:k], total[1][:k])
    sent[k : k + 8] = jnp.where(first, total[1][k - 8 : k], total[0][k - 8 : k])
    sent[k + 8 :] = jnp.concatenate([total[0][k : k + 1], total[1][k : k + 1]], axis=0)


def block_node(parts, sides, i):
    k = parts.shape[2]
    first = lax.axis_index("c") == 0
    own, other, rows = parts[i, k - 8 : k], parts[i, k : k + 8], parts[i, k + 8 :]
    none = jnp.zeros((7, k), F32)
    maps = [sides[0, i], jnp.where(first, own, other), rows[:1], none]
    given = [sides[1, i], jnp.where(first, other, own), rows[1:2], none]
    return jnp.concatenate(maps, axis=0), jnp.concatenate(given, axis=0)


def near_kernel(parts, sides, smooth_rate, twos, fours, half_total):
    rate = smooth_rate[...]
    nodes = [block_node(parts, sides, i) for i in range(parts.shape[0])]
    hours = 16.0
    for kept in (twos, fours, None):
        fade = jnp.exp(-hours * rate)
        nodes = [joined(nodes[i], nodes[i + 1], fade) for i in range(0, len(nodes), 2)]
        if kept is not None:
            for i, node in enumerate(nodes):
                kept[0, i], kept[1, i] = node
        hours = 2.0 * hours
    half_total[...] = jnp.where(lax.axis_index("c") == 0, *nodes[0])[: half_total.shape[0]]


def far_pair(pair):
    return [(pair[2 * i], pair[2 * i + 1]) for i in (0, 1)]


def half_kernel(pair, factor_rate, smooth_rate, sent):
    k = smooth_rate.shape[1]
    share = sent.shape[0] - 8
    rate = smooth_rate[...]
    none = jnp.zeros((7, k), F32)
    nodes = [[jnp.concatenate([part, none], axis=0) for part in node] for node in far_pair(pair)]
    maps, gives = joined(*nodes, jnp.exp(-128.0 * rate))
    gives = gives + jnp.exp(-256.0 * rate - factor_rate[...]) * maps
    sent[:share] = jnp.where(lax.axis_index("c") == 0, gives[:share], gives[share:k])
    sent[share:] = jnp.concatenate([maps[k : k + 1], gives[k : k + 1], none[:6]], axis=0)


def applied(current, one):
    k = one.shape[1]
    return dot3(current, one[:k]) + one[k : k + 1]


def stepped(current, node):
    maps, given = node
    k = current.shape[1]
    product = dot3(current, jnp.concatenate([maps[:k], given[:k]], axis=1))
    return product[:, :k] + maps[k : k + 1], product[:1, k:] + given[k : k + 1]


def walked(nodes, current, own):
    found = current
    gives = []
    for i, node in enumerate(nodes):
        found = jnp.where(i == own, current, found)
        current, give = stepped(current, node)
        gives.append(give)
    return found, current, gives


def followed(gives, after, own, fade):
    found = following = after
    for i in reversed(range(len(gives))):
        found = jnp.where(i == own, following, found)
        following = gives[i] + fade * following
    return found


def narrowed(current, following, left, right, goes_right, fade):
    middle = applied(current, left)
    _, give = stepped(middle, right)
    before = jnp.where(goes_right, middle, current)
    return before, jnp.where(goes_right, following, give + fade * following)


def final_kernel(
    pair, halves_sent, fours, twos, parts, sides, leaves, pairs, quads, eighths, factor_rate, smooth_rate,
    readings, present, loadings, noise, regions, scale, smoothed, out,
):
    hours, _, k = leaves.shape
    upper, far, near = (lax.axis_index(a) for a in ("za", "zb", NEAR))
    decays = jnp.exp(-factor_rate[...])
    rate = smooth_rate[...]
    retain = jnp.exp(-rate)
    share = halves_sent.shape[1] - 8
    middle = jnp.broadcast_to(halves_sent[0, share : share + 1], (8, k))
    later = jnp.concatenate([halves_sent[2, :share], halves_sent[3, :share]], axis=0)
    behind = (dot3(middle, later) + halves_sent[2, share + 1 : share + 2])[:1]
    start = jnp.where(upper == 0, 0.0, middle)
    start, final, far_gives = walked(far_pair(pair), start, far)
    count = parts.shape[0]
    following = followed(
        far_gives,
        jnp.where(upper == 0, behind, decays * final[:1]),
        far,
        jnp.exp(-float(count * hours) * rate),
    )
    for part, size in ((fours, 4), (twos, 2), (None, 1)):
        slot = lax.div(near, size)
        first = slot - lax.rem(slot, 2)
        if part is None:
            left, right = (block_node(parts, sides, first + i) for i in (0, 1))
        else:
            left, right = ((part[0, first + i], part[1, first + i]) for i in (0, 1))
        start, following = narrowed(
            start, following, left[0], right, first < slot, jnp.exp(-float(size * hours) * rate)
        )
    after = {-1: start}
    after[7] = applied(start, eighths[0])
    after[3] = applied(start, quads[0])
    after[11] = applied(after[7], quads[2])
    after[15] = applied(after[7], eighths[1])
    for i in range(4):
        after[4 * i + 1] = applied(after[4 * i - 1], pairs[2 * i])
    for i in range(8):
        after[2 * i] = applied(after[2 * i - 1], leaves[2 * i])
    weight = 1.0 - retain * decays
    for h in reversed(range(hours)):
        following = weight * after[h][:1] + retain * following
        smoothed[h : h + 1] = following
    fitted = across(smoothed[...].astype(BF16), loadings[...])
    standard = (readings[...].astype(F32) - fitted) * jnp.sqrt(noise[...])
    probab = 0.5 * (1.0 + lax.erf(standard * 0.7071067811865476))
    seen = present[...].astype(F32)
    rows = []
    for b in range(BINS):
        kernel = jnp.maximum(0.0, 1.0 - BINS * jnp.abs(probab - (b + 0.5) / BINS))
        rows.append(jnp.sum(seen * kernel, axis=0, keepdims=True))
    rows.append(jnp.zeros((4, probab.shape[1]), F32))
    table = jnp.concatenate(rows, axis=0)
    slot, _ = iotas(128, probab.shape[1])
    member = (lax.rem(slot, GROUPS) == regions[...]).astype(F32).astype(BF16)
    wide = across(jnp.concatenate(halves(table), axis=0), member)
    wide = wide[:24] + wide[24:]
    brow, blane = iotas(24, 128)
    kept = jnp.where(lax.div(blane, GROUPS) == lax.rem(brow, 8), wide, 0.0) * scale[0]
    out[...] = jnp.concatenate(
        [jnp.sum(kept[8 * r : 8 * r + 8], axis=0, keepdims=True) for r in range(3)], axis=0
    )


def tail_kernel(parts, out):
    total = jnp.sum(parts[...], axis=0)
    group, lane = iotas(GROUPS, 128)
    slot, column = iotas(128, 128)
    spread = jnp.concatenate(
        [jnp.where(lax.rem(lane, GROUPS) == group, total[r : r + 1], 0.0) for r in range(3)], axis=1
    )
    first = lax.div(slot, GROUPS)
    chosen = jnp.concatenate([(first + 8 * r == column).astype(F32) for r in range(3)], axis=0)
    found = bdot(jnp.concatenate(halves(spread), axis=0), chosen.astype(BF16))
    out[...] = (found[:GROUPS] + found[GROUPS:])[:, :BINS]


def sent_to_all(shard, axis):
    count = lax.axis_size(axis)
    return lax.all_to_all(
        jnp.broadcast_to(shard[None], (count, *shard.shape)), axis, 0, 0, tiled=True
    )


def shape_of(*sizes):
    return jax.ShapeDtypeStruct(sizes, F32)


def body(
    readings, present, loadings, noise_precision, update_gain, factor_rate, smooth_rate, regions
):
    hours, series = readings.shape
    k = loadings.shape[1]
    height, tall = k // 2 + 2, k + 8
    padded = -(-height // 8) * 8
    noise = noise_precision.reshape(1, series)
    gain, factor, smooth = (a.reshape(1, k) for a in (update_gain, factor_rate, smooth_rate))
    core = lax.axis_index("c")
    blocks, ny, cores = (lax.axis_size(a) for a in (TM, "y", "c"))
    share = hours // cores

    kept, sent = pl.pallas_call(
        information_kernel,
        out_shape=[shape_of(share, height, k), shape_of(share, padded, k)],
        in_specs=[HB] * 4,
        out_specs=[VM] * 2,
        scratch_shapes=[
            pltpu.VMEM((hours, series), BF16),
            pltpu.VMEM((hours, series), jnp.int32),
            pltpu.VMEM((series, k), BF16),
            pltpu.VMEM((1, series), F32),
            pltpu.VMEM((hours, series), F32),
            pltpu.VMEM((hours, k), F32),
            pltpu.SemaphoreType.DMA((4,)),
        ],
        compiler_params=PARAMS,
        name="information",
    )(*(pltpu.with_memory_space_constraint(a, pltpu.HBM) for a in (readings, present, loadings, noise)))
    arrived = lax.dynamic_index_in_dim(lax.all_gather(sent, "c"), 1 - core, 0, keepdims=False)
    packed = lax.all_to_all(kept + arrived[:, :height], "y", 0, 0, tiled=True).sum(axis=0)
    packed = jnp.pad(sent_to_all(packed, "y"), ((0, 0), (0, padded - height), (0, 0)))
    packed = lax.all_gather(packed, "c").reshape(hours, padded, k)

    nodes = [shape_of(hours // n, tall, k) for n in (1, 2, 4, 8)]
    leaves, pairs, quads, eighths, sent = pl.pallas_call(
        block_kernel,
        out_shape=nodes + [shape_of(k + 10, k)],
        in_specs=[VM] * 4,
        out_specs=[VM] * 5,
        scratch_shapes=[pltpu.VMEM((hours // n, tall, k), F32) for n in (1, 2, 4, 8)],
        compiler_params=PARAMS,
        name="block",
    )(packed, gain, factor, smooth)
    parts = sent_to_all(sent, NEAR)
    count = parts.shape[0]
    sides = lax.all_gather(parts[:, : k - 8], "c")

    twos, fours, half_total = pl.pallas_call(
        near_kernel,
        out_shape=[
            shape_of(2, count // 2, tall, k),
            shape_of(2, count // 4, tall, k),
            shape_of(k + 1, k),
        ],
        in_specs=[VM] * 3,
        out_specs=[VM] * 3,
        compiler_params=PARAMS,
        name="near",
    )(parts, sides, smooth)
    pair = lax.all_gather(half_total, ("zb", "c"))
    half_sent = pl.pallas_call(
        half_kernel,
        out_shape=shape_of(k // 2 + 8, k),
        in_specs=[VM] * 3,
        out_specs=VM,
        compiler_params=PARAMS,
        name="half",
    )(pair, factor, smooth)
    halves_sent = lax.all_gather(half_sent, ("za", "c"))

    hours_all = hours * blocks
    series_all = series * ny * cores
    scale = jnp.full((1,), BINS * GROUPS / (hours_all * series_all), F32)
    smoothed, local = pl.pallas_call(
        final_kernel,
        out_shape=[shape_of(hours, k), shape_of(3, 128)],
        in_specs=[VM] * 17 + [SM],
        out_specs=[VM] * 2,
        compiler_params=PARAMS,
        name="final",
    )(
        pair, halves_sent, fours, twos, parts, sides, leaves, pairs, quads, eighths, factor, smooth,
        readings, present, loadings, noise, regions.reshape(1, series), scale,
    )

    local = sent_to_all(local, SERIES).sum(axis=0)
    histogram = pl.pallas_call(
        tail_kernel,
        out_shape=shape_of(GROUPS, BINS),
        in_specs=[VM],
        out_specs=VM,
        compiler_params=PARAMS,
        name="tail",
    )(sent_to_all(local, TM))
    return (smoothed, histogram)


def solution(mesh):
    split = Mesh(mesh.devices.reshape(2, 2, 2, 4, 8, 2), (*TM, *SERIES))
    in_specs = (P(TM, SERIES), P(TM, SERIES), P(SERIES, None), P(SERIES), P(), P(), P(), P(SERIES))
    out_specs = (P(TM, None), P())
    return jax.shard_map(body, mesh=split, in_specs=in_specs, out_specs=out_specs, check_vma=False)
```

```python
import jax
import jax.numpy as jnp
from jax import lax
from jax.experimental import pallas as pl
from jax.experimental.pallas import tpu as pltpu
from jax.sharding import Mesh
from jax.sharding import PartitionSpec as P

BINS = 20
GROUPS = 16
SERIES = ("y", "c")
NEAR = ("zl", "x")
TM = ("zh", *NEAR)
F32 = jnp.float32
BF16 = jnp.bfloat16
VM = pl.BlockSpec(memory_space=pltpu.VMEM)
SM = pl.BlockSpec(memory_space=pltpu.SMEM)
HB = pl.BlockSpec(memory_space=pltpu.HBM)
PARAMS = pltpu.CompilerParams(vmem_limit_bytes=40 * 1024 * 1024)


def iotas(rows, lanes):
    shape = (rows, lanes)
    return lax.broadcasted_iota(jnp.int32, shape, 0), lax.broadcasted_iota(jnp.int32, shape, 1)


def halves(a):
    high = a.astype(BF16)
    return high, (a - high.astype(F32)).astype(BF16)


def bdot(a, b):
    return jnp.dot(a, b, preferred_element_type=F32)


def dot3(a, b):
    rows = a.shape[0]
    ah, al = halves(a)
    bh, bl = halves(b)
    both = bdot(jnp.concatenate([ah, al], axis=0), bh)
    return both[:rows] + (both[rows:] + bdot(ah, bl))


def across(a, b):
    return lax.dot_general(a, b, (((1,), (1,)), ((), ())), preferred_element_type=F32)


def joined(earlier, later, fade):
    k = fade.shape[1]
    wide = jnp.concatenate([later[0][:k], later[1][:k]], axis=1)
    product = dot3(earlier[0], wide)
    maps = jnp.concatenate([product[:k, :k], product[k:, :k] + later[0][k:]], axis=0)
    gives = jnp.concatenate([product[:k, k:], product[k:, k:] + later[1][k:]], axis=0)
    return maps, earlier[1] + fade * gives


def information_kernel(
    readings_hbm, present_hbm, loadings_hbm, noise_hbm, kept, sent,
    readings, present, loadings, noise, seen, scores, sems,
):
    pairs = (
        (loadings_hbm, loadings),
        (noise_hbm, noise),
        (present_hbm, present),
        (readings_hbm, readings),
    )
    copies = [pltpu.make_async_copy(a, b, sems.at[i]) for i, (a, b) in enumerate(pairs)]
    for copy in copies:
        copy.start()
    core = lax.axis_index("c")
    count, _, k = kept.shape
    half = k // 2
    copies[0].wait()
    copies[1].wait()
    load = loadings[...]
    scaled = (jnp.transpose(load.astype(F32)) * noise[...]).astype(BF16)
    copies[2].wait()
    seen[...] = present[...].astype(F32)
    copies[3].wait()
    scores[...] = across(readings[...] * seen[...].astype(BF16), scaled)
    row, lane = iotas(half, k)
    row_k, lane_k = iotas(k, k)
    for slot, out in enumerate((kept, sent)):
        first = (core if slot == 0 else 1 - core) * count
        for i in range(count):
            observed = seen[pl.ds(first + i, 1), :].astype(BF16)
            inform = bdot(scaled * observed, load)
            folded = pltpu.roll(inform[half:], half, 1)
            out[i, :half] = jnp.where(lane >= row, inform[:half], folded)
            diagonal = jnp.sum(jnp.where(row_k == lane_k, inform, 0.0), axis=0, keepdims=True)
            out[i, half : half + 2] = jnp.concatenate(
                [diagonal, scores[pl.ds(first + i, 1), :]], axis=0
            )


def block_kernel(
    packed, gain, factor_rate, smooth_rate, leaves, pairs, quads, eighths, sent
):
    hours = packed.shape[0]
    k = packed.shape[2]
    half = k // 2
    gain_row = gain[...]
    decay_row = jnp.exp(-factor_rate[...])
    decay_col = jnp.transpose(jnp.broadcast_to(decay_row, (k, k)))
    rate = smooth_rate[...]
    weight = 1.0 - jnp.exp(-rate) * decay_row
    row, lane = iotas(half, k)
    row_k, lane_k = iotas(k, k)
    on_diag = row_k == lane_k
    identity = on_diag.astype(F32)
    levels = {1: leaves, 2: pairs, 4: quads, 8: eighths}

    def leaf(h):
        page = packed[h]
        top = page[:half]
        upper = jnp.where(lane >= row, top, 0.0)
        lower = pltpu.roll(jnp.where(lane < row, top, 0.0), half, 1)
        part = jnp.concatenate([upper, lower], axis=0)
        inform = jnp.where(on_diag, page[half : half + 1], part + jnp.transpose(part))
        matrix = (identity - inform * gain_row) * decay_col
        shift = gain_row * page[half + 1 : half + 2]
        maps = jnp.concatenate([matrix, shift, jnp.zeros((7, k), F32)], axis=0)
        return maps, maps * weight

    def grown(at, span):
        if span == 1:
            node = leaf(at)
        else:
            middle = span // 2
            node = joined(
                grown(at, middle), grown(at + middle, middle), jnp.exp(-float(middle) * rate)
            )
        if span in levels:
            levels[span][at // span] = node[0]
        return node

    total = grown(0, hours)
    first = lax.axis_index("c") == 0
    sent[:k] = jnp.where(first, total[0][:k], total[1][:k])
    sent[k : k + 8] = jnp.where(first, total[1][k - 8 : k], total[0][k - 8 : k])
    sent[k + 8 :] = jnp.concatenate([total[0][k : k + 1], total[1][k : k + 1]], axis=0)


def block_node(parts, sides, i):
    k = parts.shape[2]
    first = lax.axis_index("c") == 0
    own, other, rows = parts[i, k - 8 : k], parts[i, k : k + 8], parts[i, k + 8 :]
    none = jnp.zeros((7, k), F32)
    maps = [sides[0, i], jnp.where(first, own, other), rows[:1], none]
    given = [sides[1, i], jnp.where(first, other, own), rows[1:2], none]
    return jnp.concatenate(maps, axis=0), jnp.concatenate(given, axis=0)


def near_kernel(parts, sides, smooth_rate, twos, fours, half_total):
    rate = smooth_rate[...]
    nodes = [block_node(parts, sides, i) for i in range(parts.shape[0])]
    hours = 16.0
    for kept in (twos, fours, None):
        fade = jnp.exp(-hours * rate)
        nodes = [joined(nodes[i], nodes[i + 1], fade) for i in range(0, len(nodes), 2)]
        if kept is not None:
            for i, node in enumerate(nodes):
                kept[0, i], kept[1, i] = node
        hours = 2.0 * hours
    half_total[...] = jnp.where(lax.axis_index("c") == 0, *nodes[0])[: half_total.shape[0]]


def applied(current, one):
    k = one.shape[1]
    return dot3(current, one[:k]) + one[k : k + 1]


def stepped(current, node):
    maps, given = node
    k = current.shape[1]
    product = dot3(current, jnp.concatenate([maps[:k], given[:k]], axis=1))
    return product[:, :k] + maps[k : k + 1], product[:1, k:] + given[k : k + 1]


def walked(nodes, current, own):
    found = current
    gives = []
    for i, node in enumerate(nodes):
        found = jnp.where(i == own, current, found)
        current, give = stepped(current, node)
        gives.append(give)
    return found, current, gives


def followed(gives, after, own, fade):
    found = following = after
    for i in reversed(range(len(gives))):
        found = jnp.where(i == own, following, found)
        following = gives[i] + fade * following
    return found


def narrowed(current, following, left, right, goes_right, fade):
    middle = applied(current, left)
    _, give = stepped(middle, right)
    before = jnp.where(goes_right, middle, current)
    return before, jnp.where(goes_right, following, give + fade * following)


def final_kernel(
    planes, fours, twos, parts, sides, leaves, pairs, quads, eighths, factor_rate, smooth_rate,
    readings, present, loadings, noise, regions, scale, smoothed, out,
):
    hours, _, k = leaves.shape
    far, near = lax.axis_index("zh"), lax.axis_index(NEAR)
    decays = jnp.exp(-factor_rate[...])
    rate = smooth_rate[...]
    retain = jnp.exp(-rate)
    plane_nodes = [(planes[0, i], planes[1, i]) for i in range(planes.shape[1])]
    start, final, plane_gives = walked(plane_nodes, jnp.zeros((8, k), F32), far)
    count = parts.shape[0]
    following = followed(
        plane_gives, decays * final[:1], far, jnp.exp(-float(count * hours) * rate)
    )
    for part, size in ((fours, 4), (twos, 2), (None, 1)):
        slot = lax.div(near, size)
        first = slot - lax.rem(slot, 2)
        if part is None:
            left, right = (block_node(parts, sides, first + i) for i in (0, 1))
        else:
            left, right = ((part[0, first + i], part[1, first + i]) for i in (0, 1))
        start, following = narrowed(
            start, following, left[0], right, first < slot, jnp.exp(-float(size * hours) * rate)
        )
    after = {-1: start}
    after[7] = applied(start, eighths[0])
    after[3] = applied(start, quads[0])
    after[11] = applied(after[7], quads[2])
    after[15] = applied(after[7], eighths[1])
    for i in range(4):
        after[4 * i + 1] = applied(after[4 * i - 1], pairs[2 * i])
    for i in range(8):
        after[2 * i] = applied(after[2 * i - 1], leaves[2 * i])
    weight = 1.0 - retain * decays
    for h in reversed(range(hours)):
        following = weight * after[h][:1] + retain * following
        smoothed[h : h + 1] = following
    fitted = across(smoothed[...].astype(BF16), loadings[...])
    standard = (readings[...].astype(F32) - fitted) * jnp.sqrt(noise[...])
    probab = 0.5 * (1.0 + lax.erf(standard * 0.7071067811865476))
    seen = present[...].astype(F32)
    rows = []
    for b in range(BINS):
        kernel = jnp.maximum(0.0, 1.0 - BINS * jnp.abs(probab - (b + 0.5) / BINS))
        rows.append(jnp.sum(seen * kernel, axis=0, keepdims=True))
    rows.append(jnp.zeros((4, probab.shape[1]), F32))
    table = jnp.concatenate(rows, axis=0)
    slot, _ = iotas(128, probab.shape[1])
    member = (lax.rem(slot, GROUPS) == regions[...]).astype(F32).astype(BF16)
    wide = across(jnp.concatenate(halves(table), axis=0), member)
    wide = wide[:24] + wide[24:]
    brow, blane = iotas(24, 128)
    kept = jnp.where(lax.div(blane, GROUPS) == lax.rem(brow, 8), wide, 0.0) * scale[0]
    out[...] = jnp.concatenate(
        [jnp.sum(kept[8 * r : 8 * r + 8], axis=0, keepdims=True) for r in range(3)], axis=0
    )


def tail_kernel(parts, out):
    total = jnp.sum(parts[...], axis=0)
    group, lane = iotas(GROUPS, 128)
    slot, column = iotas(128, 128)
    spread = jnp.concatenate(
        [jnp.where(lax.rem(lane, GROUPS) == group, total[r : r + 1], 0.0) for r in range(3)], axis=1
    )
    first = lax.div(slot, GROUPS)
    chosen = jnp.concatenate([(first + 8 * r == column).astype(F32) for r in range(3)], axis=0)
    found = bdot(jnp.concatenate(halves(spread), axis=0), chosen.astype(BF16))
    out[...] = (found[:GROUPS] + found[GROUPS:])[:, :BINS]


def sent_to_all(shard, axis):
    count = lax.axis_size(axis)
    return lax.all_to_all(
        jnp.broadcast_to(shard[None], (count, *shard.shape)), axis, 0, 0, tiled=True
    )


def shape_of(*sizes):
    return jax.ShapeDtypeStruct(sizes, F32)


def body(
    readings, present, loadings, noise_precision, update_gain, factor_rate, smooth_rate, regions
):
    hours, series = readings.shape
    k = loadings.shape[1]
    height, tall = k // 2 + 2, k + 8
    padded = -(-height // 8) * 8
    noise = noise_precision.reshape(1, series)
    gain, factor, smooth = (a.reshape(1, k) for a in (update_gain, factor_rate, smooth_rate))
    core = lax.axis_index("c")
    blocks, ny, cores = (lax.axis_size(a) for a in (TM, "y", "c"))
    share = hours // cores

    kept, sent = pl.pallas_call(
        information_kernel,
        out_shape=[shape_of(share, height, k), shape_of(share, padded, k)],
        in_specs=[HB] * 4,
        out_specs=[VM] * 2,
        scratch_shapes=[
            pltpu.VMEM((hours, series), BF16),
            pltpu.VMEM((hours, series), jnp.int32),
            pltpu.VMEM((series, k), BF16),
            pltpu.VMEM((1, series), F32),
            pltpu.VMEM((hours, series), F32),
            pltpu.VMEM((hours, k), F32),
            pltpu.SemaphoreType.DMA((4,)),
        ],
        compiler_params=PARAMS,
        name="information",
    )(*(pltpu.with_memory_space_constraint(a, pltpu.HBM) for a in (readings, present, loadings, noise)))
    arrived = lax.dynamic_index_in_dim(lax.all_gather(sent, "c"), 1 - core, 0, keepdims=False)
    packed = lax.all_to_all(kept + arrived[:, :height], "y", 0, 0, tiled=True).sum(axis=0)
    packed = jnp.pad(sent_to_all(packed, "y"), ((0, 0), (0, padded - height), (0, 0)))
    packed = lax.all_gather(packed, "c").reshape(hours, padded, k)

    nodes = [shape_of(hours // n, tall, k) for n in (1, 2, 4, 8)]
    leaves, pairs, quads, eighths, sent = pl.pallas_call(
        block_kernel,
        out_shape=nodes + [shape_of(k + 10, k)],
        in_specs=[VM] * 4,
        out_specs=[VM] * 5,
        compiler_params=PARAMS,
        name="block",
    )(packed, gain, factor, smooth)
    parts = sent_to_all(sent, NEAR)
    count = parts.shape[0]
    sides = lax.all_gather(parts[:, : k - 8], "c")

    twos, fours, half_total = pl.pallas_call(
        near_kernel,
        out_shape=[
            shape_of(2, count // 2, tall, k),
            shape_of(2, count // 4, tall, k),
            shape_of(k + 1, k),
        ],
        in_specs=[VM] * 3,
        out_specs=[VM] * 3,
        compiler_params=PARAMS,
        name="near",
    )(parts, sides, smooth)
    planes = lax.all_gather(sent_to_all(half_total, "zh"), "c")

    hours_all = hours * blocks
    series_all = series * ny * cores
    scale = jnp.full((1,), BINS * GROUPS / (hours_all * series_all), F32)
    smoothed, local = pl.pallas_call(
        final_kernel,
        out_shape=[shape_of(hours, k), shape_of(3, 128)],
        in_specs=[VM] * 16 + [SM],
        out_specs=[VM] * 2,
        compiler_params=PARAMS,
        name="final",
    )(
        planes, fours, twos, parts, sides, leaves, pairs, quads, eighths, factor, smooth,
        readings, present, loadings, noise, regions.reshape(1, series), scale,
    )

    local = sent_to_all(local, SERIES).sum(axis=0)
    histogram = pl.pallas_call(
        tail_kernel,
        out_shape=shape_of(GROUPS, BINS),
        in_specs=[VM],
        out_specs=VM,
        compiler_params=PARAMS,
        name="tail",
    )(sent_to_all(local, TM))
    return (smoothed, histogram)


def solution(mesh):
    split = Mesh(mesh.devices.reshape(4, 2, 4, 8, 2), (*TM, *SERIES))
    in_specs = (P(TM, SERIES), P(TM, SERIES), P(SERIES, None), P(SERIES), P(), P(), P(), P(SERIES))
    out_specs = (P(TM, None), P())
    return jax.shard_map(body, mesh=split, in_specs=in_specs, out_specs=out_specs, check_vma=False)
```

```python
import jax
import jax.numpy as jnp
from jax import lax
from jax.experimental import pallas as pl
from jax.experimental.pallas import tpu as pltpu
from jax.sharding import Mesh
from jax.sharding import PartitionSpec as P

BINS = 20
GROUPS = 16
SERIES = ("y", "c")
NEAR = ("zl", "x")
TM = ("zh", *NEAR)
F32 = jnp.float32
BF16 = jnp.bfloat16
VM = pl.BlockSpec(memory_space=pltpu.VMEM)
SM = pl.BlockSpec(memory_space=pltpu.SMEM)
HB = pl.BlockSpec(memory_space=pltpu.HBM)
PARAMS = pltpu.CompilerParams(vmem_limit_bytes=40 * 1024 * 1024)


def iotas(rows, lanes):
    shape = (rows, lanes)
    return lax.broadcasted_iota(jnp.int32, shape, 0), lax.broadcasted_iota(jnp.int32, shape, 1)


def halves(a):
    high = a.astype(BF16)
    return high, (a - high.astype(F32)).astype(BF16)


def bdot(a, b):
    return jnp.dot(a, b, preferred_element_type=F32)


def dot3(a, b):
    rows = a.shape[0]
    ah, al = halves(a)
    bh, bl = halves(b)
    both = bdot(jnp.concatenate([ah, al], axis=0), bh)
    return both[:rows] + (both[rows:] + bdot(ah, bl))


def across(a, b):
    return lax.dot_general(a, b, (((1,), (1,)), ((), ())), preferred_element_type=F32)


def joined(earlier, later, fade):
    k = fade.shape[1]
    wide = jnp.concatenate([later[0][:k], later[1][:k]], axis=1)
    product = dot3(earlier[0], wide)
    maps = jnp.concatenate([product[:k, :k], product[k:, :k] + later[0][k:]], axis=0)
    gives = jnp.concatenate([product[:k, k:], product[k:, k:] + later[1][k:]], axis=0)
    return maps, earlier[1] + fade * gives


def information_kernel(
    readings_hbm, present_hbm, loadings_hbm, noise_hbm, kept, sent,
    readings, present, loadings, noise, seen, scores, sems,
):
    pairs = (
        (loadings_hbm, loadings),
        (noise_hbm, noise),
        (present_hbm, present),
        (readings_hbm, readings),
    )
    copies = [pltpu.make_async_copy(a, b, sems.at[i]) for i, (a, b) in enumerate(pairs)]
    for copy in copies:
        copy.start()
    core = lax.axis_index("c")
    count, _, k = kept.shape
    half = k // 2
    copies[0].wait()
    copies[1].wait()
    load = loadings[...]
    scaled = (jnp.transpose(load.astype(F32)) * noise[...]).astype(BF16)
    copies[2].wait()
    seen[...] = present[...].astype(F32)
    copies[3].wait()
    scores[...] = across(readings[...] * seen[...].astype(BF16), scaled)
    row, lane = iotas(half, k)
    row_k, lane_k = iotas(k, k)
    for slot, out in enumerate((kept, sent)):
        first = (core if slot == 0 else 1 - core) * count
        for i in range(count):
            observed = seen[pl.ds(first + i, 1), :].astype(BF16)
            inform = bdot(scaled * observed, load)
            folded = pltpu.roll(inform[half:], half, 1)
            out[i, :half] = jnp.where(lane >= row, inform[:half], folded)
            diagonal = jnp.sum(jnp.where(row_k == lane_k, inform, 0.0), axis=0, keepdims=True)
            out[i, half : half + 2] = jnp.concatenate(
                [diagonal, scores[pl.ds(first + i, 1), :]], axis=0
            )


def block_kernel(
    packed, gain, factor_rate, smooth_rate, leaves, pairs, quads, eighths, sent,
    given1, given2, given4, given8,
):
    hours = packed.shape[0]
    k = packed.shape[2]
    half = k // 2
    gain_row = gain[...]
    decay_row = jnp.exp(-factor_rate[...])
    decay_col = jnp.transpose(jnp.broadcast_to(decay_row, (k, k)))
    rate = smooth_rate[...]
    weight = 1.0 - jnp.exp(-rate) * decay_row
    row, lane = iotas(half, k)
    row_k, lane_k = iotas(k, k)
    on_diag = row_k == lane_k
    identity = on_diag.astype(F32)
    for h in range(hours):
        page = packed[h]
        top = page[:half]
        upper = jnp.where(lane >= row, top, 0.0)
        lower = pltpu.roll(jnp.where(lane < row, top, 0.0), half, 1)
        part = jnp.concatenate([upper, lower], axis=0)
        inform = jnp.where(on_diag, page[half : half + 1], part + jnp.transpose(part))
        matrix = (identity - inform * gain_row) * decay_col
        shift = gain_row * page[half + 1 : half + 2]
        one = jnp.concatenate([matrix, shift, jnp.zeros((7, k), F32)], axis=0)
        leaves[h] = one
        given1[h] = one * weight
        if h % 2:
            pairs[h // 2], given2[h // 2] = joined(
                (leaves[h - 1], given1[h - 1]), (leaves[h], given1[h]), jnp.exp(-rate)
            )
    below, given = pairs, given2
    for span, above, gives in ((2, quads, given4), (4, eighths, given8)):
        fade = jnp.exp(-span * rate)
        for i in range(hours // (2 * span)):
            above[i], gives[i] = joined(
                (below[2 * i], given[2 * i]), (below[2 * i + 1], given[2 * i + 1]), fade
            )
        below, given = above, gives
    total = joined((below[0], given[0]), (below[1], given[1]), jnp.exp(-8.0 * rate))
    first = lax.axis_index("c") == 0
    sent[:k] = jnp.where(first, total[0][:k], total[1][:k])
    sent[k : k + 8] = jnp.where(first, total[1][k - 8 : k], total[0][k - 8 : k])
    sent[k + 8 :] = jnp.concatenate([total[0][k : k + 1], total[1][k : k + 1]], axis=0)


def block_node(parts, sides, i):
    k = parts.shape[2]
    first = lax.axis_index("c") == 0
    own, other, rows = parts[i, k - 8 : k], parts[i, k : k + 8], parts[i, k + 8 :]
    none = jnp.zeros((7, k), F32)
    maps = [sides[0, i], jnp.where(first, own, other), rows[:1], none]
    given = [sides[1, i], jnp.where(first, other, own), rows[1:2], none]
    return jnp.concatenate(maps, axis=0), jnp.concatenate(given, axis=0)


def near_kernel(parts, sides, smooth_rate, twos, fours, half_total):
    rate = smooth_rate[...]
    nodes = [block_node(parts, sides, i) for i in range(parts.shape[0])]
    hours = 16.0
    for kept in (twos, fours, None):
        fade = jnp.exp(-hours * rate)
        nodes = [joined(nodes[i], nodes[i + 1], fade) for i in range(0, len(nodes), 2)]
        if kept is not None:
            for i, node in enumerate(nodes):
                kept[0, i], kept[1, i] = node
        hours = 2.0 * hours
    half_total[...] = jnp.where(lax.axis_index("c") == 0, *nodes[0])[: half_total.shape[0]]


def applied(current, one):
    k = one.shape[1]
    return dot3(current, one[:k]) + one[k : k + 1]


def stepped(current, node):
    maps, given = node
    k = current.shape[1]
    product = dot3(current, jnp.concatenate([maps[:k], given[:k]], axis=1))
    return product[:, :k] + maps[k : k + 1], product[:1, k:] + given[k : k + 1]


def walked(nodes, current, own):
    found = current
    gives = []
    for i, node in enumerate(nodes):
        found = jnp.where(i == own, current, found)
        current, give = stepped(current, node)
        gives.append(give)
    return found, current, gives


def followed(gives, after, own, fade):
    found = following = after
    for i in reversed(range(len(gives))):
        found = jnp.where(i == own, following, found)
        following = gives[i] + fade * following
    return found


def narrowed(current, following, left, right, goes_right, fade):
    middle = applied(current, left)
    _, give = stepped(middle, right)
    before = jnp.where(goes_right, middle, current)
    return before, jnp.where(goes_right, following, give + fade * following)


def final_kernel(
    planes, fours, twos, parts, sides, leaves, pairs, quads, eighths, factor_rate, smooth_rate,
    readings, present, loadings, noise, regions, scale, smoothed, out,
):
    hours, _, k = leaves.shape
    far, near = lax.axis_index("zh"), lax.axis_index(NEAR)
    decays = jnp.exp(-factor_rate[...])
    rate = smooth_rate[...]
    retain = jnp.exp(-rate)
    plane_nodes = [(planes[0, i], planes[1, i]) for i in range(planes.shape[1])]
    start, final, plane_gives = walked(plane_nodes, jnp.zeros((8, k), F32), far)
    count = parts.shape[0]
    following = followed(
        plane_gives, decays * final[:1], far, jnp.exp(-float(count * hours) * rate)
    )
    for part, size in ((fours, 4), (twos, 2), (None, 1)):
        slot = lax.div(near, size)
        first = slot - lax.rem(slot, 2)
        if part is None:
            left, right = (block_node(parts, sides, first + i) for i in (0, 1))
        else:
            left, right = ((part[0, first + i], part[1, first + i]) for i in (0, 1))
        start, following = narrowed(
            start, following, left[0], right, first < slot, jnp.exp(-float(size * hours) * rate)
        )
    after = {-1: start}
    after[7] = applied(start, eighths[0])
    after[3] = applied(start, quads[0])
    after[11] = applied(after[7], quads[2])
    after[15] = applied(after[7], eighths[1])
    for i in range(4):
        after[4 * i + 1] = applied(after[4 * i - 1], pairs[2 * i])
    for i in range(8):
        after[2 * i] = applied(after[2 * i - 1], leaves[2 * i])
    weight = 1.0 - retain * decays
    for h in reversed(range(hours)):
        following = weight * after[h][:1] + retain * following
        smoothed[h : h + 1] = following
    fitted = across(smoothed[...].astype(BF16), loadings[...])
    standard = (readings[...].astype(F32) - fitted) * jnp.sqrt(noise[...])
    probab = 0.5 * (1.0 + lax.erf(standard * 0.7071067811865476))
    place = jnp.where(present[...] > 0, float(BINS) * probab, -8.0)
    rows = []
    for b in range(BINS):
        kernel = jnp.maximum(0.0, 1.0 - jnp.abs(place - (b + 0.5)))
        rows.append(sum(kernel[at : at + 8] for at in range(0, hours, 8)))
    table = jnp.concatenate(rows, axis=0)
    slot, _ = iotas(128, probab.shape[1])
    member = (lax.rem(slot, GROUPS) == regions[...]).astype(F32).astype(BF16)
    wide = across(jnp.concatenate(halves(table), axis=0), member)
    wide = wide[: 8 * BINS] + wide[8 * BINS :]
    brow, blane = iotas(8 * BINS, 128)
    kept = jnp.where(lax.div(blane, GROUPS) == lax.rem(lax.div(brow, 8), 8), wide, 0.0) * scale[0]
    out[...] = jnp.concatenate(
        [jnp.sum(kept[at : at + 64], axis=0, keepdims=True) for at in range(0, 8 * BINS, 64)],
        axis=0,
    )


def tail_kernel(parts, out):
    total = jnp.sum(parts[...], axis=0)
    group, lane = iotas(GROUPS, 128)
    slot, column = iotas(128, 128)
    spread = jnp.concatenate(
        [jnp.where(lax.rem(lane, GROUPS) == group, total[r : r + 1], 0.0) for r in range(3)], axis=1
    )
    first = lax.div(slot, GROUPS)
    chosen = jnp.concatenate([(first + 8 * r == column).astype(F32) for r in range(3)], axis=0)
    found = bdot(jnp.concatenate(halves(spread), axis=0), chosen.astype(BF16))
    out[...] = (found[:GROUPS] + found[GROUPS:])[:, :BINS]


def sent_to_all(shard, axis):
    count = lax.axis_size(axis)
    return lax.all_to_all(
        jnp.broadcast_to(shard[None], (count, *shard.shape)), axis, 0, 0, tiled=True
    )


def shape_of(*sizes):
    return jax.ShapeDtypeStruct(sizes, F32)


def body(
    readings, present, loadings, noise_precision, update_gain, factor_rate, smooth_rate, regions
):
    hours, series = readings.shape
    k = loadings.shape[1]
    height, tall = k // 2 + 2, k + 8
    padded = -(-height // 8) * 8
    noise = noise_precision.reshape(1, series)
    gain, factor, smooth = (a.reshape(1, k) for a in (update_gain, factor_rate, smooth_rate))
    core = lax.axis_index("c")
    blocks, ny, cores = (lax.axis_size(a) for a in (TM, "y", "c"))
    share = hours // cores

    kept, sent = pl.pallas_call(
        information_kernel,
        out_shape=[shape_of(share, height, k), shape_of(share, padded, k)],
        in_specs=[HB] * 4,
        out_specs=[VM] * 2,
        scratch_shapes=[
            pltpu.VMEM((hours, series), BF16),
            pltpu.VMEM((hours, series), jnp.int32),
            pltpu.VMEM((series, k), BF16),
            pltpu.VMEM((1, series), F32),
            pltpu.VMEM((hours, series), F32),
            pltpu.VMEM((hours, k), F32),
            pltpu.SemaphoreType.DMA((4,)),
        ],
        compiler_params=PARAMS,
        name="information",
    )(*(pltpu.with_memory_space_constraint(a, pltpu.HBM) for a in (readings, present, loadings, noise)))
    arrived = lax.dynamic_index_in_dim(lax.all_gather(sent, "c"), 1 - core, 0, keepdims=False)
    packed = lax.all_to_all(kept + arrived[:, :height], "y", 0, 0, tiled=True).sum(axis=0)
    packed = jnp.pad(sent_to_all(packed, "y"), ((0, 0), (0, padded - height), (0, 0)))
    packed = lax.all_gather(packed, "c").reshape(hours, padded, k)

    nodes = [shape_of(hours // n, tall, k) for n in (1, 2, 4, 8)]
    leaves, pairs, quads, eighths, sent = pl.pallas_call(
        block_kernel,
        out_shape=nodes + [shape_of(k + 10, k)],
        in_specs=[VM] * 4,
        out_specs=[VM] * 5,
        scratch_shapes=[pltpu.VMEM((hours // n, tall, k), F32) for n in (1, 2, 4, 8)],
        compiler_params=PARAMS,
        name="block",
    )(packed, gain, factor, smooth)
    parts = sent_to_all(sent, NEAR)
    count = parts.shape[0]
    sides = lax.all_gather(parts[:, : k - 8], "c")

    twos, fours, half_total = pl.pallas_call(
        near_kernel,
        out_shape=[
            shape_of(2, count // 2, tall, k),
            shape_of(2, count // 4, tall, k),
            shape_of(k + 1, k),
        ],
        in_specs=[VM] * 3,
        out_specs=[VM] * 3,
        compiler_params=PARAMS,
        name="near",
    )(parts, sides, smooth)
    planes = lax.all_gather(sent_to_all(half_total, "zh"), "c")

    hours_all = hours * blocks
    series_all = series * ny * cores
    scale = jnp.full((1,), BINS * GROUPS / (hours_all * series_all), F32)
    smoothed, local = pl.pallas_call(
        final_kernel,
        out_shape=[shape_of(hours, k), shape_of(3, 128)],
        in_specs=[VM] * 16 + [SM],
        out_specs=[VM] * 2,
        compiler_params=PARAMS,
        name="final",
    )(
        planes, fours, twos, parts, sides, leaves, pairs, quads, eighths, factor, smooth,
        readings, present, loadings, noise, regions.reshape(1, series), scale,
    )

    local = sent_to_all(local, SERIES).sum(axis=0)
    histogram = pl.pallas_call(
        tail_kernel,
        out_shape=shape_of(GROUPS, BINS),
        in_specs=[VM],
        out_specs=VM,
        compiler_params=PARAMS,
        name="tail",
    )(sent_to_all(local, TM))
    return (smoothed, histogram)


def solution(mesh):
    split = Mesh(mesh.devices.reshape(4, 2, 4, 8, 2), (*TM, *SERIES))
    in_specs = (P(TM, SERIES), P(TM, SERIES), P(SERIES, None), P(SERIES), P(), P(), P(), P(SERIES))
    out_specs = (P(TM, None), P())
    return jax.shard_map(body, mesh=split, in_specs=in_specs, out_specs=out_specs, check_vma=False)
```

```python
import jax
import jax.numpy as jnp
from jax import lax
from jax.experimental import pallas as pl
from jax.experimental.pallas import tpu as pltpu
from jax.sharding import Mesh
from jax.sharding import PartitionSpec as P

BINS = 20
GROUPS = 16
SERIES = ("y", "c")
NEAR = ("zl", "x")
TM = ("zh", *NEAR)
F32 = jnp.float32
BF16 = jnp.bfloat16
VM = pl.BlockSpec(memory_space=pltpu.VMEM)
SM = pl.BlockSpec(memory_space=pltpu.SMEM)
HB = pl.BlockSpec(memory_space=pltpu.HBM)
PARAMS = pltpu.CompilerParams(vmem_limit_bytes=40 * 1024 * 1024)


def iotas(rows, lanes):
    shape = (rows, lanes)
    return lax.broadcasted_iota(jnp.int32, shape, 0), lax.broadcasted_iota(jnp.int32, shape, 1)


def halves(a):
    high = a.astype(BF16)
    return high, (a - high.astype(F32)).astype(BF16)


def bdot(a, b):
    return jnp.dot(a, b, preferred_element_type=F32)


def dot3(a, b):
    rows = a.shape[0]
    ah, al = halves(a)
    bh, bl = halves(b)
    both = bdot(jnp.concatenate([ah, al], axis=0), bh)
    return both[:rows] + (both[rows:] + bdot(ah, bl))


def across(a, b):
    return lax.dot_general(a, b, (((1,), (1,)), ((), ())), preferred_element_type=F32)


def joined(earlier, later, fade):
    k = fade.shape[1]
    wide = jnp.concatenate([later[0][:k], later[1][:k]], axis=1)
    product = dot3(earlier[0], wide)
    maps = jnp.concatenate([product[:k, :k], product[k:, :k] + later[0][k:]], axis=0)
    gives = jnp.concatenate([product[:k, k:], product[k:, k:] + later[1][k:]], axis=0)
    return maps, earlier[1] + fade * gives


def information_kernel(
    readings_hbm, present_hbm, loadings_hbm, noise_hbm, kept, sent,
    readings, present, loadings, noise, seen, scores, sems,
):
    quarter = loadings.shape[0] // 4
    spans = [pl.ds(i * quarter, quarter) for i in range(4)]
    pairs = (
        *((loadings_hbm.at[span], loadings.at[span]) for span in spans),
        (noise_hbm, noise),
        (present_hbm, present),
        (readings_hbm, readings),
    )
    copies = [pltpu.make_async_copy(a, b, sems.at[i]) for i, (a, b) in enumerate(pairs)]
    for copy in copies:
        copy.start()
    core = lax.axis_index("c")
    count, _, k = kept.shape
    half = k // 2
    for copy in copies[:5]:
        copy.wait()
    load = loadings[...]
    scaled = (jnp.transpose(load).astype(F32) * noise[...]).astype(BF16)
    copies[5].wait()
    seen[...] = present[...].astype(F32)
    copies[6].wait()
    scores[...] = across(readings[...] * seen[...].astype(BF16), scaled)
    row, lane = iotas(half, k)
    row_k, lane_k = iotas(k, k)
    for slot, out in enumerate((kept, sent)):
        first = (core if slot == 0 else 1 - core) * count
        for i in range(count):
            observed = seen[pl.ds(first + i, 1), :].astype(BF16)
            inform = bdot(scaled * observed, load)
            folded = pltpu.roll(inform[half:], half, 1)
            out[i, :half] = jnp.where(lane >= row, inform[:half], folded)
            diagonal = jnp.sum(jnp.where(row_k == lane_k, inform, 0.0), axis=0, keepdims=True)
            out[i, half : half + 2] = jnp.concatenate(
                [diagonal, scores[pl.ds(first + i, 1), :]], axis=0
            )


def block_kernel(
    packed, gain, factor_rate, smooth_rate, leaves, pairs, quads, eighths, sent,
    given1, given2, given4, given8,
):
    hours = packed.shape[0]
    k = packed.shape[2]
    half = k // 2
    gain_row = gain[...]
    decay_row = jnp.exp(-factor_rate[...])
    decay_col = jnp.transpose(jnp.broadcast_to(decay_row, (k, k)))
    rate = smooth_rate[...]
    weight = 1.0 - jnp.exp(-rate) * decay_row
    row, lane = iotas(half, k)
    row_k, lane_k = iotas(k, k)
    on_diag = row_k == lane_k
    identity = on_diag.astype(F32)
    for h in range(hours):
        page = packed[h]
        top = page[:half]
        upper = jnp.where(lane >= row, top, 0.0)
        lower = pltpu.roll(jnp.where(lane < row, top, 0.0), half, 1)
        part = jnp.concatenate([upper, lower], axis=0)
        inform = jnp.where(on_diag, page[half : half + 1], part + jnp.transpose(part))
        matrix = (identity - inform * gain_row) * decay_col
        shift = gain_row * page[half + 1 : half + 2]
        one = jnp.concatenate([matrix, shift, jnp.zeros((7, k), F32)], axis=0)
        leaves[h] = one
        given1[h] = one * weight
        if h % 2:
            pairs[h // 2], given2[h // 2] = joined(
                (leaves[h - 1], given1[h - 1]), (leaves[h], given1[h]), jnp.exp(-rate)
            )
    below, given = pairs, given2
    for span, above, gives in ((2, quads, given4), (4, eighths, given8)):
        fade = jnp.exp(-span * rate)
        for i in range(hours // (2 * span)):
            above[i], gives[i] = joined(
                (below[2 * i], given[2 * i]), (below[2 * i + 1], given[2 * i + 1]), fade
            )
        below, given = above, gives
    total = joined((below[0], given[0]), (below[1], given[1]), jnp.exp(-8.0 * rate))
    first = lax.axis_index("c") == 0
    sent[:k] = jnp.where(first, total[0][:k], total[1][:k])
    sent[k : k + 8] = jnp.where(first, total[1][k - 8 : k], total[0][k - 8 : k])
    sent[k + 8 :] = jnp.concatenate([total[0][k : k + 1], total[1][k : k + 1]], axis=0)


def block_node(parts, sides, i):
    k = parts.shape[2]
    first = lax.axis_index("c") == 0
    own, other, rows = parts[i, k - 8 : k], parts[i, k : k + 8], parts[i, k + 8 :]
    none = jnp.zeros((7, k), F32)
    maps = [sides[0, i], jnp.where(first, own, other), rows[:1], none]
    given = [sides[1, i], jnp.where(first, other, own), rows[1:2], none]
    return jnp.concatenate(maps, axis=0), jnp.concatenate(given, axis=0)


def near_kernel(parts, sides, smooth_rate, twos, fours, half_total):
    rate = smooth_rate[...]
    nodes = [block_node(parts, sides, i) for i in range(parts.shape[0])]
    hours = 16.0
    for kept in (twos, fours, None):
        fade = jnp.exp(-hours * rate)
        nodes = [joined(nodes[i], nodes[i + 1], fade) for i in range(0, len(nodes), 2)]
        if kept is not None:
            for i, node in enumerate(nodes):
                kept[0, i], kept[1, i] = node
        hours = 2.0 * hours
    half_total[...] = jnp.where(lax.axis_index("c") == 0, *nodes[0])[: half_total.shape[0]]


def applied(current, one):
    k = one.shape[1]
    return dot3(current, one[:k]) + one[k : k + 1]


def stepped(current, node):
    maps, given = node
    k = current.shape[1]
    product = dot3(current, jnp.concatenate([maps[:k], given[:k]], axis=1))
    return product[:, :k] + maps[k : k + 1], product[:1, k:] + given[k : k + 1]


def walked(nodes, current, own):
    found = current
    gives = []
    for i, node in enumerate(nodes):
        found = jnp.where(i == own, current, found)
        current, give = stepped(current, node)
        gives.append(give)
    return found, current, gives


def followed(gives, after, own, fade):
    found = following = after
    for i in reversed(range(len(gives))):
        found = jnp.where(i == own, following, found)
        following = gives[i] + fade * following
    return found


def narrowed(current, following, left, right, goes_right, fade):
    middle = applied(current, left)
    _, give = stepped(middle, right)
    before = jnp.where(goes_right, middle, current)
    return before, jnp.where(goes_right, following, give + fade * following)


def final_kernel(
    planes, fours, twos, parts, sides, leaves, pairs, quads, eighths, factor_rate, smooth_rate,
    readings, present, loadings, noise, regions, scale, smoothed, out,
):
    hours, _, k = leaves.shape
    far, near = lax.axis_index("zh"), lax.axis_index(NEAR)
    decays = jnp.exp(-factor_rate[...])
    rate = smooth_rate[...]
    retain = jnp.exp(-rate)
    plane_nodes = [(planes[0, i], planes[1, i]) for i in range(planes.shape[1])]
    start, final, plane_gives = walked(plane_nodes, jnp.zeros((8, k), F32), far)
    count = parts.shape[0]
    following = followed(
        plane_gives, decays * final[:1], far, jnp.exp(-float(count * hours) * rate)
    )
    for part, size in ((fours, 4), (twos, 2), (None, 1)):
        slot = lax.div(near, size)
        first = slot - lax.rem(slot, 2)
        if part is None:
            left, right = (block_node(parts, sides, first + i) for i in (0, 1))
        else:
            left, right = ((part[0, first + i], part[1, first + i]) for i in (0, 1))
        start, following = narrowed(
            start, following, left[0], right, first < slot, jnp.exp(-float(size * hours) * rate)
        )
    after = {-1: start}
    after[7] = applied(start, eighths[0])
    after[3] = applied(start, quads[0])
    after[11] = applied(after[7], quads[2])
    after[15] = applied(after[7], eighths[1])
    for i in range(4):
        after[4 * i + 1] = applied(after[4 * i - 1], pairs[2 * i])
    for i in range(8):
        after[2 * i] = applied(after[2 * i - 1], leaves[2 * i])
    weight = 1.0 - retain * decays
    for h in reversed(range(hours)):
        following = weight * after[h][:1] + retain * following
        smoothed[h : h + 1] = following
    fitted = across(smoothed[...].astype(BF16), loadings[...])
    standard = (readings[...].astype(F32) - fitted) * jnp.sqrt(noise[...])
    probab = 0.5 * (1.0 + lax.erf(standard * 0.7071067811865476))
    place = jnp.where(present[...] > 0, float(BINS) * probab, -8.0)
    rows = []
    for b in range(BINS):
        kernel = jnp.maximum(0.0, 1.0 - jnp.abs(place - (b + 0.5)))
        rows.append(sum(kernel[at : at + 8] for at in range(0, hours, 8)))
    table = jnp.concatenate(rows, axis=0)
    slot, _ = iotas(128, probab.shape[1])
    member = (lax.rem(slot, GROUPS) == regions[...]).astype(F32).astype(BF16)
    wide = across(jnp.concatenate(halves(table), axis=0), member)
    wide = wide[: 8 * BINS] + wide[8 * BINS :]
    brow, blane = iotas(8 * BINS, 128)
    kept = jnp.where(lax.div(blane, GROUPS) == lax.rem(lax.div(brow, 8), 8), wide, 0.0) * scale[0]
    out[...] = jnp.concatenate(
        [jnp.sum(kept[at : at + 64], axis=0, keepdims=True) for at in range(0, 8 * BINS, 64)],
        axis=0,
    )


def tail_kernel(parts, out):
    total = jnp.sum(parts[...], axis=0)
    group, lane = iotas(GROUPS, 128)
    slot, column = iotas(128, 128)
    spread = jnp.concatenate(
        [jnp.where(lax.rem(lane, GROUPS) == group, total[r : r + 1], 0.0) for r in range(3)], axis=1
    )
    first = lax.div(slot, GROUPS)
    chosen = jnp.concatenate([(first + 8 * r == column).astype(F32) for r in range(3)], axis=0)
    found = bdot(jnp.concatenate(halves(spread), axis=0), chosen.astype(BF16))
    out[...] = (found[:GROUPS] + found[GROUPS:])[:, :BINS]


def sent_to_all(shard, axis):
    count = lax.axis_size(axis)
    return lax.all_to_all(
        jnp.broadcast_to(shard[None], (count, *shard.shape)), axis, 0, 0, tiled=True
    )


def shape_of(*sizes):
    return jax.ShapeDtypeStruct(sizes, F32)


def body(
    readings, present, loadings, noise_precision, update_gain, factor_rate, smooth_rate, regions
):
    hours, series = readings.shape
    k = loadings.shape[1]
    height, tall = k // 2 + 2, k + 8
    padded = -(-height // 8) * 8
    noise = noise_precision.reshape(1, series)
    gain, factor, smooth = (a.reshape(1, k) for a in (update_gain, factor_rate, smooth_rate))
    core = lax.axis_index("c")
    blocks, ny, cores = (lax.axis_size(a) for a in (TM, "y", "c"))
    share = hours // cores

    kept, sent = pl.pallas_call(
        information_kernel,
        out_shape=[shape_of(share, height, k), shape_of(share, padded, k)],
        in_specs=[HB] * 4,
        out_specs=[VM] * 2,
        scratch_shapes=[
            pltpu.VMEM((hours, series), BF16),
            pltpu.VMEM((hours, series), jnp.int32),
            pltpu.VMEM((series, k), BF16),
            pltpu.VMEM((1, series), F32),
            pltpu.VMEM((hours, series), F32),
            pltpu.VMEM((hours, k), F32),
            pltpu.SemaphoreType.DMA((7,)),
        ],
        compiler_params=PARAMS,
        name="information",
    )(*(pltpu.with_memory_space_constraint(a, pltpu.HBM) for a in (readings, present, loadings, noise)))
    arrived = lax.dynamic_index_in_dim(lax.all_gather(sent, "c"), 1 - core, 0, keepdims=False)
    packed = lax.all_to_all(kept + arrived[:, :height], "y", 0, 0, tiled=True).sum(axis=0)
    packed = jnp.pad(sent_to_all(packed, "y"), ((0, 0), (0, padded - height), (0, 0)))
    packed = lax.all_gather(packed, "c").reshape(hours, padded, k)

    nodes = [shape_of(hours // n, tall, k) for n in (1, 2, 4, 8)]
    leaves, pairs, quads, eighths, sent = pl.pallas_call(
        block_kernel,
        out_shape=nodes + [shape_of(k + 10, k)],
        in_specs=[VM] * 4,
        out_specs=[VM] * 5,
        scratch_shapes=[pltpu.VMEM((hours // n, tall, k), F32) for n in (1, 2, 4, 8)],
        compiler_params=PARAMS,
        name="block",
    )(packed, gain, factor, smooth)
    parts = sent_to_all(sent, NEAR)
    count = parts.shape[0]
    sides = lax.all_gather(parts[:, : k - 8], "c")

    twos, fours, half_total = pl.pallas_call(
        near_kernel,
        out_shape=[
            shape_of(2, count // 2, tall, k),
            shape_of(2, count // 4, tall, k),
            shape_of(k + 1, k),
        ],
        in_specs=[VM] * 3,
        out_specs=[VM] * 3,
        compiler_params=PARAMS,
        name="near",
    )(parts, sides, smooth)
    planes = lax.all_gather(sent_to_all(half_total, "zh"), "c")

    hours_all = hours * blocks
    series_all = series * ny * cores
    scale = jnp.full((1,), BINS * GROUPS / (hours_all * series_all), F32)
    smoothed, local = pl.pallas_call(
        final_kernel,
        out_shape=[shape_of(hours, k), shape_of(3, 128)],
        in_specs=[VM] * 16 + [SM],
        out_specs=[VM] * 2,
        compiler_params=PARAMS,
        name="final",
    )(
        planes, fours, twos, parts, sides, leaves, pairs, quads, eighths, factor, smooth,
        readings, present, loadings, noise, regions.reshape(1, series), scale,
    )

    local = sent_to_all(local, SERIES).sum(axis=0)
    histogram = pl.pallas_call(
        tail_kernel,
        out_shape=shape_of(GROUPS, BINS),
        in_specs=[VM],
        out_specs=VM,
        compiler_params=PARAMS,
        name="tail",
    )(sent_to_all(local, TM))
    return (smoothed, histogram)


def solution(mesh):
    split = Mesh(mesh.devices.reshape(4, 2, 4, 8, 2), (*TM, *SERIES))
    in_specs = (P(TM, SERIES), P(TM, SERIES), P(SERIES, None), P(SERIES), P(), P(), P(), P(SERIES))
    out_specs = (P(TM, None), P())
    return jax.shard_map(body, mesh=split, in_specs=in_specs, out_specs=out_specs, check_vma=False)
```

```python
import jax
import jax.numpy as jnp
from jax import lax
from jax.experimental import pallas as pl
from jax.experimental.pallas import tpu as pltpu
from jax.sharding import Mesh
from jax.sharding import PartitionSpec as P

BINS = 20
GROUPS = 16
SERIES = ("y", "c")
NEAR = ("zl", "x")
TM = ("zh", *NEAR)
F32 = jnp.float32
BF16 = jnp.bfloat16
VM = pl.BlockSpec(memory_space=pltpu.VMEM)
SM = pl.BlockSpec(memory_space=pltpu.SMEM)
HB = pl.BlockSpec(memory_space=pltpu.HBM)
PARAMS = pltpu.CompilerParams(vmem_limit_bytes=40 * 1024 * 1024)


def iotas(rows, lanes):
    shape = (rows, lanes)
    return lax.broadcasted_iota(jnp.int32, shape, 0), lax.broadcasted_iota(jnp.int32, shape, 1)


def halves(a):
    high = a.astype(BF16)
    return high, (a - high.astype(F32)).astype(BF16)


def bdot(a, b):
    return jnp.dot(a, b, preferred_element_type=F32)


def dot3(a, b):
    rows = a.shape[0]
    ah, al = halves(a)
    bh, bl = halves(b)
    both = bdot(jnp.concatenate([ah, al], axis=0), bh)
    return both[:rows] + (both[rows:] + bdot(ah, bl))


def across(a, b):
    return lax.dot_general(a, b, (((1,), (1,)), ((), ())), preferred_element_type=F32)


def joined(earlier, later, fade):
    k = fade.shape[1]
    wide = jnp.concatenate([later[0][:k], later[1][:k]], axis=1)
    product = dot3(earlier[0], wide)
    maps = jnp.concatenate([product[:k, :k], product[k:, :k] + later[0][k:]], axis=0)
    gives = jnp.concatenate([product[:k, k:], product[k:, k:] + later[1][k:]], axis=0)
    return maps, earlier[1] + fade * gives


def information_kernel(
    readings_hbm, present_hbm, loadings_hbm, noise_hbm, kept, sent,
    readings, present, loadings, noise, seen, scores, sems,
):
    pairs = (
        (loadings_hbm, loadings),
        (noise_hbm, noise),
        (present_hbm, present),
        (readings_hbm, readings),
    )
    copies = [pltpu.make_async_copy(a, b, sems.at[i]) for i, (a, b) in enumerate(pairs)]
    for copy in copies:
        copy.start()
    core = lax.axis_index("c")
    count, _, k = kept.shape
    half = k // 2
    copies[0].wait()
    copies[1].wait()
    load = loadings[...]
    scaled = (jnp.transpose(load.astype(F32)) * noise[...]).astype(BF16)
    copies[2].wait()
    seen[...] = present[...].astype(F32)
    copies[3].wait()
    scores[...] = across(readings[...] * seen[...].astype(BF16), scaled)
    row, lane = iotas(half, k)
    row_k, lane_k = iotas(k, k)
    for slot, out in enumerate((kept, sent)):
        first = (core if slot == 0 else 1 - core) * count
        for i in range(count):
            observed = seen[pl.ds(first + i, 1), :].astype(BF16)
            inform = bdot(scaled * observed, load)
            folded = pltpu.roll(inform[half:], half, 1)
            out[i, :half] = jnp.where(lane >= row, inform[:half], folded)
            diagonal = jnp.sum(jnp.where(row_k == lane_k, inform, 0.0), axis=0, keepdims=True)
            out[i, half : half + 2] = jnp.concatenate(
                [diagonal, scores[pl.ds(first + i, 1), :]], axis=0
            )


def block_kernel(
    packed, gain, factor_rate, smooth_rate, leaves, pairs, quads, eighths, sent,
    given1, given2, given4, given8,
):
    hours = packed.shape[0]
    k = packed.shape[2]
    half = k // 2
    gain_row = gain[...]
    decay_row = jnp.exp(-factor_rate[...])
    decay_col = jnp.transpose(jnp.broadcast_to(decay_row, (k, k)))
    rate = smooth_rate[...]
    weight = 1.0 - jnp.exp(-rate) * decay_row
    row, lane = iotas(half, k)
    row_k, lane_k = iotas(k, k)
    on_diag = row_k == lane_k
    identity = on_diag.astype(F32)
    for h in range(hours):
        page = packed[h]
        top = page[:half]
        upper = jnp.where(lane >= row, top, 0.0)
        lower = pltpu.roll(jnp.where(lane < row, top, 0.0), half, 1)
        part = jnp.concatenate([upper, lower], axis=0)
        inform = jnp.where(on_diag, page[half : half + 1], part + jnp.transpose(part))
        matrix = (identity - inform * gain_row) * decay_col
        shift = gain_row * page[half + 1 : half + 2]
        one = jnp.concatenate([matrix, shift, jnp.zeros((7, k), F32)], axis=0)
        leaves[h] = one
        given1[h] = one * weight
        if h % 2:
            pairs[h // 2], given2[h // 2] = joined(
                (leaves[h - 1], given1[h - 1]), (leaves[h], given1[h]), jnp.exp(-rate)
            )
    below, given = pairs, given2
    for span, above, gives in ((2, quads, given4), (4, eighths, given8)):
        fade = jnp.exp(-span * rate)
        for i in range(hours // (2 * span)):
            above[i], gives[i] = joined(
                (below[2 * i], given[2 * i]), (below[2 * i + 1], given[2 * i + 1]), fade
            )
        below, given = above, gives
    total = joined((below[0], given[0]), (below[1], given[1]), jnp.exp(-8.0 * rate))
    first = lax.axis_index("c") == 0
    sent[:k] = jnp.where(first, total[0][:k], total[1][:k])
    sent[k : k + 8] = jnp.where(first, total[1][k - 8 : k], total[0][k - 8 : k])
    sent[k + 8 :] = jnp.concatenate([total[0][k : k + 1], total[1][k : k + 1]], axis=0)


def block_node(parts, sides, i):
    k = parts.shape[2]
    first = lax.axis_index("c") == 0
    own, other, rows = parts[i, k - 8 : k], parts[i, k : k + 8], parts[i, k + 8 :]
    none = jnp.zeros((7, k), F32)
    maps = [sides[0, i], jnp.where(first, own, other), rows[:1], none]
    given = [sides[1, i], jnp.where(first, other, own), rows[1:2], none]
    return jnp.concatenate(maps, axis=0), jnp.concatenate(given, axis=0)


def near_kernel(parts, sides, smooth_rate, twos, fours, half_total):
    rate = smooth_rate[...]
    nodes = [block_node(parts, sides, i) for i in range(parts.shape[0])]
    hours = 16.0
    for kept in (twos, fours, None):
        fade = jnp.exp(-hours * rate)
        nodes = [joined(nodes[i], nodes[i + 1], fade) for i in range(0, len(nodes), 2)]
        if kept is not None:
            for i, node in enumerate(nodes):
                kept[0, i], kept[1, i] = node
        hours = 2.0 * hours
    half_total[...] = jnp.where(lax.axis_index("c") == 0, *nodes[0])[: half_total.shape[0]]


def applied(current, one):
    k = one.shape[1]
    return dot3(current, one[:k]) + one[k : k + 1]


def stepped(current, node):
    maps, given = node
    k = current.shape[1]
    product = dot3(current, jnp.concatenate([maps[:k], given[:k]], axis=1))
    return product[:, :k] + maps[k : k + 1], product[:1, k:] + given[k : k + 1]


def walked(nodes, current, own):
    found = current
    gives = []
    for i, node in enumerate(nodes):
        found = jnp.where(i == own, current, found)
        current, give = stepped(current, node)
        gives.append(give)
    return found, current, gives


def followed(gives, after, own, fade):
    found = following = after
    for i in reversed(range(len(gives))):
        found = jnp.where(i == own, following, found)
        following = gives[i] + fade * following
    return found


def narrowed(current, following, left, right, goes_right, fade):
    middle = applied(current, left)
    _, give = stepped(middle, right)
    before = jnp.where(goes_right, middle, current)
    return before, jnp.where(goes_right, following, give + fade * following)


def final_kernel(
    planes, fours, twos, parts, sides, leaves, pairs, quads, eighths, factor_rate, smooth_rate,
    readings, present, loadings, noise, regions, scale, smoothed, out,
):
    hours, _, k = leaves.shape
    far, near = lax.axis_index("zh"), lax.axis_index(NEAR)
    decays = jnp.exp(-factor_rate[...])
    rate = smooth_rate[...]
    retain = jnp.exp(-rate)
    plane_nodes = [(planes[0, i], planes[1, i]) for i in range(planes.shape[1])]
    start, final, plane_gives = walked(plane_nodes, jnp.zeros((8, k), F32), far)
    count = parts.shape[0]
    following = followed(
        plane_gives, decays * final[:1], far, jnp.exp(-float(count * hours) * rate)
    )
    for part, size in ((fours, 4), (twos, 2), (None, 1)):
        slot = lax.div(near, size)
        first = slot - lax.rem(slot, 2)
        if part is None:
            left, right = (block_node(parts, sides, first + i) for i in (0, 1))
        else:
            left, right = ((part[0, first + i], part[1, first + i]) for i in (0, 1))
        start, following = narrowed(
            start, following, left[0], right, first < slot, jnp.exp(-float(size * hours) * rate)
        )
    after = {-1: start}
    after[7] = applied(start, eighths[0])
    after[3] = applied(start, quads[0])
    after[11] = applied(after[7], quads[2])
    after[15] = applied(after[7], eighths[1])
    for i in range(4):
        after[4 * i + 1] = applied(after[4 * i - 1], pairs[2 * i])
    for i in range(8):
        after[2 * i] = applied(after[2 * i - 1], leaves[2 * i])
    weight = 1.0 - retain * decays
    for h in reversed(range(hours)):
        following = weight * after[h][:1] + retain * following
        smoothed[h : h + 1] = following
    fitted = across(smoothed[...].astype(BF16), loadings[...])
    standard = (readings[...].astype(F32) - fitted) * jnp.sqrt(noise[...])
    probab = 0.5 * (1.0 + lax.erf(standard * 0.7071067811865476))
    place = jnp.where(present[...] > 0, float(BINS) * probab, -8.0)
    rows = []
    for b in range(BINS):
        kernel = jnp.maximum(0.0, 1.0 - jnp.abs(place - (b + 0.5)))
        rows.append(sum(kernel[at : at + 8] for at in range(0, hours, 8)))
    table = jnp.concatenate(rows, axis=0)
    slot, _ = iotas(128, probab.shape[1])
    member = (lax.rem(slot, GROUPS) == regions[...]).astype(F32).astype(BF16)
    wide = across(jnp.concatenate(halves(table), axis=0), member)
    wide = wide[: 8 * BINS] + wide[8 * BINS :]
    brow, blane = iotas(8 * BINS, 128)
    kept = jnp.where(lax.div(blane, GROUPS) == lax.rem(lax.div(brow, 8), 8), wide, 0.0) * scale[0]
    out[...] = jnp.concatenate(
        [jnp.sum(kept[at : at + 64], axis=0, keepdims=True) for at in range(0, 8 * BINS, 64)],
        axis=0,
    )


def tail_kernel(parts, out):
    total = jnp.sum(parts[...], axis=0)
    group, lane = iotas(GROUPS, 128)
    slot, column = iotas(128, 128)
    spread = jnp.concatenate(
        [jnp.where(lax.rem(lane, GROUPS) == group, total[r : r + 1], 0.0) for r in range(3)], axis=1
    )
    first = lax.div(slot, GROUPS)
    chosen = jnp.concatenate([(first + 8 * r == column).astype(F32) for r in range(3)], axis=0)
    found = bdot(jnp.concatenate(halves(spread), axis=0), chosen.astype(BF16))
    out[...] = (found[:GROUPS] + found[GROUPS:])[:, :BINS]


def sent_to_all(shard, axis):
    count = lax.axis_size(axis)
    return lax.all_to_all(
        jnp.broadcast_to(shard[None], (count, *shard.shape)), axis, 0, 0, tiled=True
    )


def shape_of(*sizes):
    return jax.ShapeDtypeStruct(sizes, F32)


def body(
    readings, present, loadings, noise_precision, update_gain, factor_rate, smooth_rate, regions
):
    hours, series = readings.shape
    k = loadings.shape[1]
    height, tall = k // 2 + 2, k + 8
    padded = -(-height // 8) * 8
    noise = noise_precision.reshape(1, series)
    gain, factor, smooth = (a.reshape(1, k) for a in (update_gain, factor_rate, smooth_rate))
    core = lax.axis_index("c")
    blocks, ny, cores = (lax.axis_size(a) for a in (TM, "y", "c"))
    share = hours // cores

    kept, sent = pl.pallas_call(
        information_kernel,
        out_shape=[shape_of(share, height, k), shape_of(share, padded, k)],
        in_specs=[HB] * 4,
        out_specs=[VM] * 2,
        scratch_shapes=[
            pltpu.VMEM((hours, series), BF16),
            pltpu.VMEM((hours, series), jnp.int32),
            pltpu.VMEM((series, k), BF16),
            pltpu.VMEM((1, series), F32),
            pltpu.VMEM((hours, series), F32),
            pltpu.VMEM((hours, k), F32),
            pltpu.SemaphoreType.DMA((4,)),
        ],
        compiler_params=PARAMS,
        name="information",
    )(*(pltpu.with_memory_space_constraint(a, pltpu.HBM) for a in (readings, present, loadings, noise)))
    arrived = lax.dynamic_index_in_dim(lax.all_gather(sent, "c"), 1 - core, 0, keepdims=False)
    packed = lax.all_to_all(kept + arrived[:, :height], "y", 0, 0, tiled=True).sum(axis=0)
    packed = jnp.pad(sent_to_all(packed, "y"), ((0, 0), (0, padded - height), (0, 0)))
    packed = lax.all_gather(packed, "c").reshape(hours, padded, k)

    nodes = [shape_of(hours // n, tall, k) for n in (1, 2, 4, 8)]
    leaves, pairs, quads, eighths, sent = pl.pallas_call(
        block_kernel,
        out_shape=nodes + [shape_of(k + 10, k)],
        in_specs=[VM] * 4,
        out_specs=[VM] * 5,
        scratch_shapes=[pltpu.VMEM((hours // n, tall, k), F32) for n in (1, 2, 4, 8)],
        compiler_params=PARAMS,
        name="block",
    )(packed, gain, factor, smooth)
    parts = sent_to_all(sent, NEAR)
    count = parts.shape[0]
    sides = lax.all_gather(parts[:, : k - 8], "c")

    twos, fours, half_total = pl.pallas_call(
        near_kernel,
        out_shape=[
            shape_of(2, count // 2, tall, k),
            shape_of(2, count // 4, tall, k),
            shape_of(k + 1, k),
        ],
        in_specs=[VM] * 3,
        out_specs=[VM] * 3,
        compiler_params=PARAMS,
        name="near",
    )(parts, sides, smooth)
    planes = lax.all_gather(sent_to_all(half_total, "zh"), "c")

    hours_all = hours * blocks
    series_all = series * ny * cores
    scale = jnp.full((1,), BINS * GROUPS / (hours_all * series_all), F32)
    smoothed, local = pl.pallas_call(
        final_kernel,
        out_shape=[shape_of(hours, k), shape_of(3, 128)],
        in_specs=[VM] * 16 + [SM],
        out_specs=[VM] * 2,
        compiler_params=PARAMS,
        name="final",
    )(
        planes, fours, twos, parts, sides, leaves, pairs, quads, eighths, factor, smooth,
        readings, present, loadings, noise, regions.reshape(1, series), scale,
    )

    local = sent_to_all(local, ("zl", *SERIES)).sum(axis=0)
    histogram = pl.pallas_call(
        tail_kernel,
        out_shape=shape_of(GROUPS, BINS),
        in_specs=[VM],
        out_specs=VM,
        compiler_params=PARAMS,
        name="tail",
    )(sent_to_all(local, ("zh", "x")))
    return (smoothed, histogram)


def solution(mesh):
    split = Mesh(mesh.devices.reshape(4, 2, 4, 8, 2), (*TM, *SERIES))
    in_specs = (P(TM, SERIES), P(TM, SERIES), P(SERIES, None), P(SERIES), P(), P(), P(), P(SERIES))
    out_specs = (P(TM, None), P())
    return jax.shard_map(body, mesh=split, in_specs=in_specs, out_specs=out_specs, check_vma=False)
```

```python
import jax
import jax.numpy as jnp
from jax import lax
from jax.experimental import pallas as pl
from jax.experimental.pallas import tpu as pltpu
from jax.sharding import Mesh
from jax.sharding import PartitionSpec as P

BINS = 20
GROUPS = 16
SERIES = ("y", "c")
NEAR = ("zl", "x")
TM = ("zh", *NEAR)
F32 = jnp.float32
BF16 = jnp.bfloat16
VM = pl.BlockSpec(memory_space=pltpu.VMEM)
SM = pl.BlockSpec(memory_space=pltpu.SMEM)
HB = pl.BlockSpec(memory_space=pltpu.HBM)
PARAMS = pltpu.CompilerParams(vmem_limit_bytes=40 * 1024 * 1024)


def iotas(rows, lanes):
    shape = (rows, lanes)
    return lax.broadcasted_iota(jnp.int32, shape, 0), lax.broadcasted_iota(jnp.int32, shape, 1)


def halves(a):
    high = a.astype(BF16)
    return high, (a - high.astype(F32)).astype(BF16)


def bdot(a, b):
    return jnp.dot(a, b, preferred_element_type=F32)


def dot3(a, b):
    rows = a.shape[0]
    ah, al = halves(a)
    bh, bl = halves(b)
    both = bdot(jnp.concatenate([ah, al], axis=0), bh)
    return both[:rows] + (both[rows:] + bdot(ah, bl))


def across(a, b):
    return lax.dot_general(a, b, (((1,), (1,)), ((), ())), preferred_element_type=F32)


def joined(earlier, later, fade):
    k = fade.shape[1]
    wide = jnp.concatenate([later[0][:k], later[1][:k]], axis=1)
    product = dot3(earlier[0], wide)
    maps = jnp.concatenate([product[:k, :k], product[k:, :k] + later[0][k:]], axis=0)
    gives = jnp.concatenate([product[:k, k:], product[k:, k:] + later[1][k:]], axis=0)
    return maps, earlier[1] + fade * gives


def information_kernel(
    readings_hbm, present_hbm, loadings_hbm, noise_hbm, kept, sent,
    readings, present, loadings, noise, seen, scores, sems,
):
    pairs = (
        (loadings_hbm, loadings),
        (noise_hbm, noise),
        (present_hbm, present),
        (readings_hbm, readings),
    )
    copies = [pltpu.make_async_copy(a, b, sems.at[i]) for i, (a, b) in enumerate(pairs)]
    for copy in copies:
        copy.start()
    core = lax.axis_index("c")
    count, _, k = kept.shape
    half = k // 2
    copies[0].wait()
    copies[1].wait()
    load = loadings[...]
    scaled = (jnp.transpose(load.astype(F32)) * noise[...]).astype(BF16)
    copies[2].wait()
    seen[...] = present[...].astype(F32)
    copies[3].wait()
    scores[...] = across(readings[...] * seen[...].astype(BF16), scaled)
    row, lane = iotas(half, k)
    row_k, lane_k = iotas(k, k)
    for slot, out in enumerate((kept, sent)):
        first = (core if slot == 0 else 1 - core) * count
        for i in range(count):
            observed = seen[pl.ds(first + i, 1), :].astype(BF16)
            inform = bdot(scaled * observed, load)
            folded = pltpu.roll(inform[half:], half, 1)
            out[i, :half] = jnp.where(lane >= row, inform[:half], folded)
            diagonal = jnp.sum(jnp.where(row_k == lane_k, inform, 0.0), axis=0, keepdims=True)
            out[i, half : half + 2] = jnp.concatenate(
                [diagonal, scores[pl.ds(first + i, 1), :]], axis=0
            )


def block_kernel(
    packed, gain, factor_rate, smooth_rate, leaves, pairs, quads, eighths, sent,
    given1, given2, given4, given8,
):
    hours = packed.shape[0]
    k = packed.shape[2]
    half = k // 2
    gain_row = gain[...]
    decay_row = jnp.exp(-factor_rate[...])
    decay_col = jnp.transpose(jnp.broadcast_to(decay_row, (k, k)))
    rate = smooth_rate[...]
    weight = 1.0 - jnp.exp(-rate) * decay_row
    row, lane = iotas(half, k)
    row_k, lane_k = iotas(k, k)
    on_diag = row_k == lane_k
    identity = on_diag.astype(F32)
    for h in range(hours):
        page = packed[h]
        top = page[:half]
        upper = jnp.where(lane >= row, top, 0.0)
        lower = pltpu.roll(jnp.where(lane < row, top, 0.0), half, 1)
        part = jnp.concatenate([upper, lower], axis=0)
        inform = jnp.where(on_diag, page[half : half + 1], part + jnp.transpose(part))
        matrix = (identity - inform * gain_row) * decay_col
        shift = gain_row * page[half + 1 : half + 2]
        one = jnp.concatenate([matrix, shift, jnp.zeros((7, k), F32)], axis=0)
        leaves[h] = one
        given1[h] = one * weight
        if h % 2:
            pairs[h // 2], given2[h // 2] = joined(
                (leaves[h - 1], given1[h - 1]), (leaves[h], given1[h]), jnp.exp(-rate)
            )
    below, given = pairs, given2
    for span, above, gives in ((2, quads, given4), (4, eighths, given8)):
        fade = jnp.exp(-span * rate)
        for i in range(hours // (2 * span)):
            above[i], gives[i] = joined(
                (below[2 * i], given[2 * i]), (below[2 * i + 1], given[2 * i + 1]), fade
            )
        below, given = above, gives
    total = joined((below[0], given[0]), (below[1], given[1]), jnp.exp(-8.0 * rate))
    first = lax.axis_index("c") == 0
    sent[:k] = jnp.where(first, total[0][:k], total[1][:k])
    sent[k : k + 8] = jnp.where(first, total[1][k - 8 : k], total[0][k - 8 : k])
    sent[k + 8 :] = jnp.concatenate([total[0][k : k + 1], total[1][k : k + 1]], axis=0)


def block_node(parts, sides, i):
    k = parts.shape[2]
    first = lax.axis_index("c") == 0
    own, other, rows = parts[i, k - 8 : k], parts[i, k : k + 8], parts[i, k + 8 :]
    none = jnp.zeros((7, k), F32)
    maps = [sides[0, i], jnp.where(first, own, other), rows[:1], none]
    given = [sides[1, i], jnp.where(first, other, own), rows[1:2], none]
    return jnp.concatenate(maps, axis=0), jnp.concatenate(given, axis=0)


def near_kernel(parts, sides, smooth_rate, twos, fours, half_total):
    rate = smooth_rate[...]
    nodes = [block_node(parts, sides, i) for i in range(parts.shape[0])]
    hours = 16.0
    for kept in (twos, fours, None):
        fade = jnp.exp(-hours * rate)
        nodes = [joined(nodes[i], nodes[i + 1], fade) for i in range(0, len(nodes), 2)]
        if kept is not None:
            for i, node in enumerate(nodes):
                kept[0, i], kept[1, i] = node
        hours = 2.0 * hours
    half_total[...] = jnp.where(lax.axis_index("c") == 0, *nodes[0])[: half_total.shape[0]]


def applied(current, one):
    k = one.shape[1]
    return dot3(current, one[:k]) + one[k : k + 1]


def stepped(current, node):
    maps, given = node
    k = current.shape[1]
    product = dot3(current, jnp.concatenate([maps[:k], given[:k]], axis=1))
    return product[:, :k] + maps[k : k + 1], product[:1, k:] + given[k : k + 1]


def walked(nodes, current, own):
    found = current
    gives = []
    for i, node in enumerate(nodes):
        found = jnp.where(i == own, current, found)
        current, give = stepped(current, node)
        gives.append(give)
    return found, current, gives


def followed(gives, after, own, fade):
    found = following = after
    for i in reversed(range(len(gives))):
        found = jnp.where(i == own, following, found)
        following = gives[i] + fade * following
    return found


def narrowed(current, following, left, right, goes_right, fade):
    middle = applied(current, left)
    _, give = stepped(middle, right)
    before = jnp.where(goes_right, middle, current)
    return before, jnp.where(goes_right, following, give + fade * following)


def final_kernel(
    planes, fours, twos, parts, sides, leaves, pairs, quads, eighths, factor_rate, smooth_rate,
    readings, present, loadings, noise, regions, scale, smoothed, out,
):
    hours, _, k = leaves.shape
    far, near = lax.axis_index("zh"), lax.axis_index(NEAR)
    decays = jnp.exp(-factor_rate[...])
    rate = smooth_rate[...]
    retain = jnp.exp(-rate)
    plane_nodes = [(planes[0, i], planes[1, i]) for i in range(planes.shape[1])]
    start, final, plane_gives = walked(plane_nodes, jnp.zeros((8, k), F32), far)
    count = parts.shape[0]
    following = followed(
        plane_gives, decays * final[:1], far, jnp.exp(-float(count * hours) * rate)
    )
    for part, size in ((fours, 4), (twos, 2), (None, 1)):
        slot = lax.div(near, size)
        first = slot - lax.rem(slot, 2)
        if part is None:
            left, right = (block_node(parts, sides, first + i) for i in (0, 1))
        else:
            left, right = ((part[0, first + i], part[1, first + i]) for i in (0, 1))
        start, following = narrowed(
            start, following, left[0], right, first < slot, jnp.exp(-float(size * hours) * rate)
        )
    after = {-1: start}
    after[7] = applied(start, eighths[0])
    after[3] = applied(start, quads[0])
    after[11] = applied(after[7], quads[2])
    after[15] = applied(after[7], eighths[1])
    for i in range(4):
        after[4 * i + 1] = applied(after[4 * i - 1], pairs[2 * i])
    for i in range(8):
        after[2 * i] = applied(after[2 * i - 1], leaves[2 * i])
    weight = 1.0 - retain * decays
    for h in reversed(range(hours)):
        following = weight * after[h][:1] + retain * following
        smoothed[h : h + 1] = following
    fitted = across(smoothed[...].astype(BF16), loadings[...])
    standard = (readings[...].astype(F32) - fitted) * jnp.sqrt(noise[...])
    probab = 0.5 * (1.0 + lax.erf(standard * 0.7071067811865476))
    place = jnp.where(present[...] > 0, float(BINS) * probab, -8.0)
    rows = []
    for b in range(BINS):
        kernel = jnp.maximum(0.0, 1.0 - jnp.abs(place - (b + 0.5)))
        rows.append(sum(kernel[at : at + 8] for at in range(0, hours, 8)))
    table = jnp.concatenate(rows, axis=0)
    slot, _ = iotas(128, probab.shape[1])
    member = (lax.rem(slot, GROUPS) == regions[...]).astype(F32).astype(BF16)
    wide = across(jnp.concatenate(halves(table), axis=0), member)
    wide = wide[: 8 * BINS] + wide[8 * BINS :]
    brow, blane = iotas(8 * BINS, 128)
    kept = jnp.where(lax.div(blane, GROUPS) == lax.rem(lax.div(brow, 8), 8), wide, 0.0) * scale[0]
    out[...] = jnp.concatenate(
        [jnp.sum(kept[at : at + 64], axis=0, keepdims=True) for at in range(0, 8 * BINS, 64)],
        axis=0,
    )


def tail_kernel(parts, out):
    total = jnp.sum(parts[...], axis=0)
    group, lane = iotas(GROUPS, 128)
    slot, column = iotas(128, 128)
    spread = jnp.concatenate(
        [jnp.where(lax.rem(lane, GROUPS) == group, total[r : r + 1], 0.0) for r in range(3)], axis=1
    )
    first = lax.div(slot, GROUPS)
    chosen = jnp.concatenate([(first + 8 * r == column).astype(F32) for r in range(3)], axis=0)
    found = bdot(jnp.concatenate(halves(spread), axis=0), chosen.astype(BF16))
    out[...] = (found[:GROUPS] + found[GROUPS:])[:, :BINS]


def sent_to_all(shard, axis):
    count = lax.axis_size(axis)
    return lax.all_to_all(
        jnp.broadcast_to(shard[None], (count, *shard.shape)), axis, 0, 0, tiled=True
    )


def shape_of(*sizes):
    return jax.ShapeDtypeStruct(sizes, F32)


def body(
    readings, present, loadings, noise_precision, update_gain, factor_rate, smooth_rate, regions
):
    hours, series = readings.shape
    k = loadings.shape[1]
    height, tall = k // 2 + 2, k + 8
    padded = -(-height // 8) * 8
    noise = noise_precision.reshape(1, series)
    gain, factor, smooth = (a.reshape(1, k) for a in (update_gain, factor_rate, smooth_rate))
    core = lax.axis_index("c")
    blocks, ny, cores = (lax.axis_size(a) for a in (TM, "y", "c"))
    share = hours // cores

    kept, sent = pl.pallas_call(
        information_kernel,
        out_shape=[shape_of(share, height, k), shape_of(share, padded, k)],
        in_specs=[HB] * 4,
        out_specs=[VM] * 2,
        scratch_shapes=[
            pltpu.VMEM((hours, series), BF16),
            pltpu.VMEM((hours, series), jnp.int32),
            pltpu.VMEM((series, k), BF16),
            pltpu.VMEM((1, series), F32),
            pltpu.VMEM((hours, series), F32),
            pltpu.VMEM((hours, k), F32),
            pltpu.SemaphoreType.DMA((4,)),
        ],
        compiler_params=PARAMS,
        name="information",
    )(*(pltpu.with_memory_space_constraint(a, pltpu.HBM) for a in (readings, present, loadings, noise)))
    arrived = lax.dynamic_index_in_dim(lax.all_gather(sent, "c"), 1 - core, 0, keepdims=False)
    packed = lax.all_to_all(kept + arrived[:, :height], "y", 0, 0, tiled=True).sum(axis=0)
    packed = jnp.pad(sent_to_all(packed, "y"), ((0, 0), (0, padded - height), (0, 0)))
    packed = lax.all_gather(packed, "c").reshape(hours, padded, k)

    nodes = [shape_of(hours // n, tall, k) for n in (1, 2, 4, 8)]
    leaves, pairs, quads, eighths, sent = pl.pallas_call(
        block_kernel,
        out_shape=nodes + [shape_of(k + 10, k)],
        in_specs=[VM] * 4,
        out_specs=[VM] * 5,
        scratch_shapes=[pltpu.VMEM((hours // n, tall, k), F32) for n in (1, 2, 4, 8)],
        compiler_params=PARAMS,
        name="block",
    )(packed, gain, factor, smooth)
    parts = sent_to_all(sent, NEAR)
    count = parts.shape[0]
    sides = lax.all_gather(parts[:, : k - 8], "c")

    twos, fours, half_total = pl.pallas_call(
        near_kernel,
        out_shape=[
            shape_of(2, count // 2, tall, k),
            shape_of(2, count // 4, tall, k),
            shape_of(k + 1, k),
        ],
        in_specs=[VM] * 3,
        out_specs=[VM] * 3,
        compiler_params=PARAMS,
        name="near",
    )(parts, sides, smooth)
    planes = lax.all_gather(sent_to_all(half_total, "zh"), "c")

    hours_all = hours * blocks
    series_all = series * ny * cores
    scale = jnp.full((1,), BINS * GROUPS / (hours_all * series_all), F32)
    smoothed, local = pl.pallas_call(
        final_kernel,
        out_shape=[shape_of(hours, k), shape_of(3, 128)],
        in_specs=[VM] * 16 + [SM],
        out_specs=[VM] * 2,
        compiler_params=PARAMS,
        name="final",
    )(
        planes, fours, twos, parts, sides, leaves, pairs, quads, eighths, factor, smooth,
        readings, present, loadings, noise, regions.reshape(1, series), scale,
    )

    local = sent_to_all(local, TM).sum(axis=0)
    histogram = pl.pallas_call(
        tail_kernel,
        out_shape=shape_of(GROUPS, BINS),
        in_specs=[VM],
        out_specs=VM,
        compiler_params=PARAMS,
        name="tail",
    )(sent_to_all(local, SERIES))
    return (smoothed, histogram)


def solution(mesh):
    split = Mesh(mesh.devices.reshape(4, 2, 4, 8, 2), (*TM, *SERIES))
    in_specs = (P(TM, SERIES), P(TM, SERIES), P(SERIES, None), P(SERIES), P(), P(), P(), P(SERIES))
    out_specs = (P(TM, None), P())
    return jax.shard_map(body, mesh=split, in_specs=in_specs, out_specs=out_specs, check_vma=False)
```
